32 devices in a mesh: dp: 4 (over z), row: 4 (over x, core), col: 2 (over y).
Axes of the slice: x: 2, y: 2, z: 4, core: 2. Of those that a mesh axis runs over, the one named last changes fastest.
Arguments:
- residual_in: bfloat16 [4096, 2048], P(('dp', 'col'), 'row'), may hold values from -6 to 6
- attention_gain: bfloat16 [2048], P('row'), may hold values from 0.099609375 to 1.8984375
- query_weight: bfloat16 [2048, 2048], P('row', 'col'), may hold values from -0.125 to 0.125
- key_weight: bfloat16 [2048, 2048], P('row', 'col'), may hold values from -0.125 to 0.125
- value_weight: bfloat16 [2048, 2048], P('row', 'col'), may hold values from -0.125 to 0.125
- query_gain: bfloat16 [2048], P('col'), may hold values from 0.099609375 to 1.8984375
- key_gain: bfloat16 [2048], P('col'), may hold values from 0.099609375 to 1.8984375
- output_weight: bfloat16 [2048, 2048], P('col', 'row'), may hold values from -0.5 to 0.5
- expert_gain: bfloat16 [2048], P('row'), may hold values from 0.099609375 to 1.8984375
- router_weight: bfloat16 [2048, 32], P('row'), may hold values from -0.0625 to 0.0625
- gate_weight: bfloat16 [32, 2048, 1024], P(None, 'row', 'col'), may hold values from -0.125 to 0.125
- up_weight: bfloat16 [32, 2048, 1024], P(None, 'row', 'col'), may hold values from -0.125 to 0.125
- down_weight: bfloat16 [32, 1024, 2048], P(None, 'col', 'row'), may hold values from -2.5 to 2.5
- segments: int32 [4096], P('dp'), may hold values from 0 to 2, as said below
- routes: int32 [4096, 8], P('dp'), may hold values from 0 to 31, all different within a row; in each aligned block of 1024 rows (0 to 1023, 1024 to 2047, ...) at most 384 rows name the same one
- cotangent: bfloat16 [4096, 2048], P(('dp', 'col'), 'row'), may hold values from -6 to 6
Outputs:
- residual_out: bfloat16 [4096, 2048], P(('dp', 'col'), 'row')
- input_gradient: float32 [4096, 2048], P(('dp', 'col'), 'row')
- attention_gain_gradient: float32 [2048], P('row')
- query_weight_gradient: float32 [2048, 2048], P('row', 'col')
- key_weight_gradient: float32 [2048, 2048], P('row', 'col')
- value_weight_gradient: float32 [2048, 2048], P('row', 'col')
- query_gain_gradient: float32 [2048], P('col')
- key_gain_gradient: float32 [2048], P('col')
- output_weight_gradient: float32 [2048, 2048], P('col', 'row')
- expert_gain_gradient: float32 [2048], P('row')
- router_weight_gradient: float32 [2048, 32], P('row')
- gate_weight_gradient: float32 [32, 2048, 1024], P(None, 'row', 'col')
- up_weight_gradient: float32 [32, 2048, 1024], P(None, 'row', 'col')
- down_weight_gradient: float32 [32, 1024, 2048], P(None, 'col', 'row')
The draws below stay inside these ranges and needn't reach their ends.
Inputs may be any that keep to these rules, and one draw needn't show every extreme that they name: `segments`: within each sequence the numbers never fall and start at 1; each sequence holds exactly 2 documents of 60 to 800 tokens, followed by a tail of 1 to 59 padding tokens that carry 0. In each data group's 1024 tokens (aligned blocks of rows) no expert is named by more than 384 routes, and in every draw some expert is named by exactly 384 of them.
All inputs are finite; a program needn't handle non-finite values.
Results may differ from the reference program's by a relative error of at most 0.018.
Values may be sent and summed in bfloat16 or wider, within the bound.
No kernel may reach another device: no remote copies, remote signals or barrier semaphores. Data moves between devices by JAX's collectives and lax.ppermute only.
A program may use at most 640 MiB of HBM per device.

```python
import math
import jax
import jax.numpy as jnp
import numpy as np
from jax import lax

D = 2048
HEADS = 16
HEAD_DIM = 128
FF = 1024
TOPK = 8
EXPERTS = 32
DOC_MIN = 60
GROUP_TOK = 1024
TOKENS = 4096
SEQ_LEN = 1024
DOCS = 2
CAP = 384
N_DP = 4


def draw_segments(key, part):
    key = jax.random.fold_in(key, 11)
    sequence_total = TOKENS // SEQ_LEN
    share_key, padding_key = jax.random.split(key)
    padding = jax.random.randint(padding_key, (sequence_total, 1), 1, DOC_MIN)
    content = SEQ_LEN - padding
    spare = content - DOCS * DOC_MIN
    shares_raw = jax.random.randint(share_key, (sequence_total, DOCS), 8, 17)
    shares = spare * shares_raw // jnp.sum(shares_raw, axis=1, keepdims=True)
    leftover = spare - jnp.sum(shares, axis=1, keepdims=True)
    last_mark = (jnp.arange(DOCS, dtype=jnp.int32) == DOCS - 1).astype(jnp.int32)[None, :]
    document_lengths = DOC_MIN + shares + leftover * last_mark
    document_ends = jnp.cumsum(document_lengths, axis=1)
    places = jnp.arange(SEQ_LEN, dtype=jnp.int32)
    numbers = 1 + jnp.sum((document_ends[:, None, :] <= places[None, :, None]).astype(jnp.int32), axis=2)
    numbers = jnp.where(places[None, :] >= content, 0, numbers)
    return numbers.reshape(-1).astype(jnp.int32)


def steps_of(rng, dims, cuts, low, largest):
    def one(dim, blocks):
        draws = jax.random.uniform(jax.random.fold_in(jax.random.fold_in(rng, 6), dim), (blocks,), jnp.float32, low / len(cuts), largest / len(cuts))
        return jnp.repeat(jnp.exp(draws), dims[dim] // blocks).reshape((-1,) + (1,) * (len(dims) - dim - 1))

    loudness = one(*cuts[0])
    for cut in cuts[1:]:
        loudness = loudness * one(*cut)
    return loudness


def routed_block(key, own, number, rows, number_of, top, most, skew):
    order = jax.random.permutation(key, number_of)
    packed, usual = portions_of(number_of, rows * top, most, skew, True), portions_of(number_of, rows * top, most, skew, False)
    places = jnp.arange(number_of)

    def named(tallies, turn):
        used = int((tallies > 0).sum())
        fixed = max(1, used // 4)
        passed = fixed + (places - fixed + turn * (used - fixed)) % max(1, number_of - fixed)
        return jnp.zeros((number_of,), jnp.int32).at[order[jnp.where(places < fixed, places, passed)]].set(jnp.asarray(tallies, jnp.int32))

    tallies = jnp.where(number % 4 == 0, named(packed, number // 4), named(usual, number - number // 4 - 1))
    mixed = jax.random.permutation(jax.random.fold_in(own, 3), number_of)
    source_of, sink = mixed[0:number_of // 2 * 2:2], mixed[1:number_of // 2 * 2:2]
    room = jnp.minimum(tallies[source_of] - 1, most - tallies[sink]) // 2
    room = jnp.where((source_of == order[0]) | (sink == order[0]) | (tallies[sink] == 0), 0, jnp.maximum(room, 0))
    passed = jax.random.randint(jax.random.fold_in(own, 4), (number_of // 2,), 0, 1 << 20) % (room + 1)
    tallies = tallies.at[source_of].add(-passed).at[sink].add(passed)
    labels = jnp.searchsorted(jnp.cumsum(tallies), jnp.arange(rows * top), side="right").astype(jnp.int32)
    listing = labels.reshape(top, rows).T
    listing = listing[jax.random.permutation(jax.random.fold_in(own, 1), rows)]
    turn = jax.random.randint(jax.random.fold_in(own, 2), (rows, 1), 0, top)
    return jnp.take_along_axis(listing, (jnp.arange(top)[None, :] + turn) % top, axis=1)


def portions_of(count, total, bound, slope, full):
    weights = [(1 << 20) // math.isqrt(standing ** slope) + 1 for standing in range(1, count + 1)]
    largest = bound if full else min(bound, max(-(-total // count), total * weights[0] // sum(weights)))
    least = 1 if total - largest >= count - 1 else 0
    given, spare = [largest] + [least] * (count - 1), total - largest - least * (count - 1)
    while spare > 0:
        candidates = [i for i in range(1, count) if given[i] < largest] or [i for i in range(1, count) if given[i] < bound]
        mass, left = sum([weights[i] for i in candidates]), spare
        for i in candidates:
            extra = min(bound - given[i], max(1, left * weights[i] // mass), spare)
            given[i] = given[i] + extra
            spare = spare - extra
    return np.array(given)


def normal_values(own_key, shape, deviation, most, shards=(), kind=jnp.bfloat16):
    array = jax.random.normal(own_key, shape, jnp.float32) * deviation
    if len(shards) > 0:
        array = steps_of(own_key, shape, shards, -0.22, 0.18) * array
    return jnp.clip(array, min=-most, max=most).astype(kind)


def setup_inputs(seed: int = 0) -> dict:
    splits = jax.random.split(jax.random.key(seed), 17)
    residual_in = normal_values(splits[0], (TOKENS, D), 1.0, 6.0, ((0, 8), (1, 4)))
    attention_gain = jnp.clip(1.0 + 0.18 * jax.random.normal(splits[1], (D,), jnp.float32), 0.099609375, 1.8984375).astype(jnp.bfloat16)
    query_weight = normal_values(splits[2], (D, D), D ** -0.5, 0.125, ((0, 4), (1, 2)))
    key_weight = normal_values(splits[3], (D, D), D ** -0.5, 0.125, ((0, 4), (1, 2)))
    value_weight = normal_values(splits[4], (D, D), D ** -0.5, 0.125, ((0, 4), (1, 2)))
    query_gain = jnp.clip(1.0 + 0.18 * jax.random.normal(splits[5], (D,), jnp.float32), 0.099609375, 1.8984375).astype(jnp.bfloat16)
    key_gain = jnp.clip(1.0 + 0.18 * jax.random.normal(splits[6], (D,), jnp.float32), 0.099609375, 1.8984375).astype(jnp.bfloat16)
    output_weight = normal_values(splits[7], (D, D), (D // 16) ** -0.5, 0.5, ((0, 2), (1, 4)))
    expert_gain = jnp.clip(1.0 + 0.18 * jax.random.normal(splits[8], (D,), jnp.float32), 0.099609375, 1.8984375).astype(jnp.bfloat16)
    router_weight = normal_values(splits[9], (D, EXPERTS), (4 * D) ** -0.5, 0.0625, ((0, 4),))
    gate_weight = normal_values(splits[10], (EXPERTS, D, FF), D ** -0.5, 0.125, ((1, 4), (2, 2)))
    up_weight = normal_values(splits[11], (EXPERTS, D, FF), D ** -0.5, 0.125, ((1, 4), (2, 2)))
    down_weight = normal_values(splits[12], (EXPERTS, FF, D), (max(FF // 200, 1)) ** -0.5, 2.5, ((1, 2), (2, 4)))
    segments = draw_segments(jax.random.fold_in(splits[16], 71), 0)
    routes_keys = jax.random.split(jax.random.fold_in(splits[14], 1), TOKENS // GROUP_TOK)
    routes_turns = jax.random.permutation(jax.random.fold_in(splits[14], 3), TOKENS // GROUP_TOK)
    routes = jax.vmap(lambda own, number: routed_block(jax.random.fold_in(splits[14], 2), own, number, GROUP_TOK, EXPERTS, TOPK, CAP, 1))(routes_keys, routes_turns).reshape((TOKENS, TOPK))
    cotangent = normal_values(splits[15], (TOKENS, D), 1.0, 6.0, ((0, 8), (1, 4)))
    return {"residual_in": residual_in, "attention_gain": attention_gain, "query_weight": query_weight, "key_weight": key_weight, "value_weight": value_weight, "query_gain": query_gain, "key_gain": key_gain, "output_weight": output_weight, "expert_gain": expert_gain, "router_weight": router_weight, "gate_weight": gate_weight, "up_weight": up_weight, "down_weight": down_weight, "segments": segments, "routes": routes, "cotangent": cotangent}


EPSILON = 1e-05
NEGATIVE = -1e+30
HIGHEST = lax.Precision.HIGHEST

@jax.custom_vjp
def low(v):
    return lax.optimization_barrier(v.astype(jnp.bfloat16)).astype(jnp.float32)

@jax.custom_vjp
def low_back(v):
    return v

def low_keep(v):
    return (low(v), None)

def low_pass(kept, grad):
    return (grad,)

def back_keep(v):
    return (v, None)

def back_low(kept, grad):
    return (low(grad),)
low.defvjp(low_keep, low_pass)
low_back.defvjp(back_keep, back_low)

def matmul(left, right):
    return jnp.dot(left, right, precision=HIGHEST)

def rms_scale(values, gain):
    return values * lax.rsqrt(lax.optimization_barrier(jnp.mean(values * values, axis=-1, keepdims=True)) + EPSILON) * gain

def softmax_rows(values):
    raised = jnp.exp(values - lax.optimization_barrier(jnp.max(values, axis=-1, keepdims=True)))
    return raised / lax.optimization_barrier(jnp.sum(raised, axis=-1, keepdims=True))

def expert_slots(routes, experts, capacity):
    flat_routes = routes.reshape(-1)
    route_count = flat_routes.shape[0]
    member = (flat_routes[:, None] == jnp.arange(experts, dtype=jnp.int32)[None, :]).astype(jnp.int32)
    before = jnp.cumsum(member, axis=0) - member
    slot_index = lax.optimization_barrier(jnp.sum(before * member, axis=1)).astype(jnp.int32)
    slot_table = jnp.full((experts, capacity), route_count, jnp.int32)
    slot_table = slot_table.at[flat_routes, slot_index].set(jnp.arange(route_count, dtype=jnp.int32))
    filled = slot_table < route_count
    source = jnp.where(filled, slot_table, 0).astype(jnp.int32)
    position = (flat_routes * capacity + slot_index).astype(jnp.int32)
    return (source, filled, position)

def to_routes(expert_rows, position):
    flat_rows = expert_rows.reshape(expert_rows.shape[0] * expert_rows.shape[1], expert_rows.shape[2])
    return jnp.take(flat_rows, position, axis=0)

def attend_sequence(pieces):
    query_block, key_block, value_block, segment_block = pieces
    places = jnp.arange(SEQ_LEN, dtype=jnp.int32)
    scores = low_back(jnp.einsum('qhd,khd->hqk', query_block, key_block, precision=HIGHEST) * HEAD_DIM ** (-0.5))
    allowed = (segment_block[:, None] == segment_block[None, :]) & (places[None, :] <= places[:, None])
    weights = low(softmax_rows(jnp.where(allowed[None], scores, NEGATIVE)))
    return low_back(low(jnp.einsum('hqk,khd->qhd', weights, value_block, precision=HIGHEST)))

def heads_view(values):
    return values.reshape(TOKENS // SEQ_LEN, SEQ_LEN, HEADS, HEAD_DIM)

def reference(residual_in, attention_gain, query_weight, key_weight, value_weight, query_gain, key_gain, output_weight, expert_gain, router_weight, gate_weight, up_weight, down_weight, segments, routes, cotangent):

    def forward(residual, first_gain, query_matrix, key_matrix, value_matrix, query_scale, key_scale, output_matrix, second_gain, router_matrix, gate_matrix, up_matrix, down_matrix):
        normed = low(rms_scale(residual, first_gain))
        query_raw = low_back(matmul(normed, query_matrix))
        key_raw = low_back(matmul(normed, key_matrix))
        value_raw = low_back(matmul(normed, value_matrix))
        query_round = low(rms_scale(query_raw, query_scale))
        key_round = low(rms_scale(key_raw, key_scale))
        value_round = low(value_raw)
        mixed = lax.map(jax.checkpoint(attend_sequence), (heads_view(query_round), heads_view(key_round), heads_view(value_round), segments.reshape(TOKENS // SEQ_LEN, SEQ_LEN)))
        middle = residual + low_back(matmul(mixed.reshape(TOKENS, D), output_matrix))
        second = low(rms_scale(middle, second_gain))
        logits = low_back(matmul(second, router_matrix))
        router_probs = softmax_rows(logits)
        picked = jnp.take_along_axis(router_probs, routes, axis=1)

        def expert_block(pieces):
            normed_block, route_block, picked_block = pieces
            source, filled, position = expert_slots(route_block, EXPERTS, CAP)
            normed_buffer = jnp.take(normed_block, source // TOPK, axis=0)
            gate_buffer = jnp.einsum('ecd,edf->ecf', normed_buffer, gate_matrix, precision=HIGHEST)
            up_buffer = jnp.einsum('ecd,edf->ecf', normed_buffer, up_matrix, precision=HIGHEST)
            gate_routes = low_back(to_routes(gate_buffer, position)).reshape(GROUP_TOK, TOPK, FF)
            up_routes = low_back(to_routes(up_buffer, position)).reshape(GROUP_TOK, TOPK, FF)
            hidden = low(picked_block[..., None] * (gate_routes * jax.nn.sigmoid(gate_routes)) * up_routes)
            hidden_buffer = jnp.take(hidden.reshape(GROUP_TOK * TOPK, FF), source, axis=0)
            down_buffer = jnp.einsum('ecf,efd->ecd', hidden_buffer, down_matrix, precision=HIGHEST)
            return lax.optimization_barrier(jnp.sum(to_routes(down_buffer, position).reshape(GROUP_TOK, TOPK, D), axis=1))
        expert_out = lax.map(jax.checkpoint(expert_block), (second.reshape(N_DP, GROUP_TOK, D), routes.reshape(N_DP, GROUP_TOK, TOPK), picked.reshape(N_DP, GROUP_TOK, TOPK)))
        return middle + expert_out.reshape(TOKENS, D)
    floats = tuple((argument.astype(jnp.float32) for argument in (residual_in, attention_gain, query_weight, key_weight, value_weight, query_gain, key_gain, output_weight, expert_gain, router_weight, gate_weight, up_weight, down_weight)))
    result, pullback = jax.vjp(forward, *floats)
    deltas = pullback(cotangent.astype(jnp.float32))
    return (result.astype(jnp.bfloat16), deltas[0], deltas[1], deltas[2], deltas[3], deltas[4], deltas[5], deltas[6], deltas[7], deltas[8], deltas[9], deltas[10], deltas[11], deltas[12])
```

```python
import functools

import jax
import jax.numpy as jnp
from jax import lax
from jax.experimental import pallas as pl
from jax.experimental.pallas import tpu as pltpu
from jax.sharding import PartitionSpec as P

HEAD_DIM = 128
MAX_LEN = 2048
EPSILON = 1e-05
NEGATIVE = -1e30

TILE = 128
WIDE = 512
SUB = 1024
RING = 8
MEGA = 1 << 20
BF = jnp.bfloat16
F32 = jnp.float32


def dot(left, right):
    return jnp.dot(left, right, preferred_element_type=F32)


def dot_nt(left, right):
    return lax.dot_general(left, right, (((1,), (1,)), ((), ())), preferred_element_type=F32)


def dot_tn(left, right):
    return lax.dot_general(left, right, (((0,), (0,)), ((), ())), preferred_element_type=F32)


def iota(shape, axis):
    return lax.broadcasted_iota(jnp.int32, shape, axis)


def params(mebibytes):
    return pltpu.CompilerParams(vmem_limit_bytes=mebibytes * MEGA)


def cost(flops, nbytes):
    return pl.CostEstimate(flops=int(flops), bytes_accessed=int(nbytes), transcendentals=0)


def once(shape, index):
    return pl.BlockSpec(shape, index, pipeline_mode=pl.Buffered(buffer_count=1))


def project_kernel(x_ref, q_ref, k_ref, v_ref, o_ref):
    width = q_ref.shape[1]
    x = x_ref[...]
    o_ref[0, :, :width] = dot(x, q_ref[...]).astype(BF)
    o_ref[0, :, width : 2 * width] = dot(x, k_ref[...]).astype(BF)
    o_ref[0, :, 2 * width :] = dot(x, v_ref[...]).astype(BF)


def project(x, query, key, value, spans, slots):
    tokens, depth = x.shape
    width, span = query.shape[1] // slots, tokens // spans
    weight = pl.BlockSpec((depth, width), lambda s, h: (0, h))
    return pl.pallas_call(
        project_kernel,
        grid=(spans, slots),
        in_specs=[pl.BlockSpec((span, depth), lambda s, h: (s, 0)), weight, weight, weight],
        out_specs=pl.BlockSpec((1, span, 3 * width), lambda s, h: (s * slots + h, 0, 0)),
        out_shape=jax.ShapeDtypeStruct((spans * slots, span, 3 * width), BF),
        compiler_params=params(48),
        cost_estimate=cost(6 * tokens * depth * width * slots, 6 * tokens * width * slots),
        name="project",
    )(x, query, key, value)


def project_back_kernel(d_ref, q_ref, k_ref, v_ref, o_ref, acc):
    slot = pl.program_id(1)
    width = q_ref.shape[1]

    @pl.when(slot == 0)
    def _():
        acc[...] = jnp.zeros_like(acc)

    acc[...] += (
        dot_nt(d_ref[0, :, :width], q_ref[...])
        + dot_nt(d_ref[0, :, width : 2 * width], k_ref[...])
        + dot_nt(d_ref[0, :, 2 * width :], v_ref[...])
    )

    @pl.when(slot == pl.num_programs(1) - 1)
    def _():
        o_ref[...] = acc[...].astype(BF)


def project_back(delta, query, key, value, spans, slots):
    _, span, joint = delta.shape
    depth, width = query.shape[0], joint // 3
    weight = pl.BlockSpec((depth, width), lambda s, h: (0, h))
    return pl.pallas_call(
        project_back_kernel,
        grid=(spans, slots),
        in_specs=[
            pl.BlockSpec((1, span, joint), lambda s, h: (s * slots + h, 0, 0)),
            weight,
            weight,
            weight,
        ],
        out_specs=pl.BlockSpec((span, depth), lambda s, h: (s, 0)),
        out_shape=jax.ShapeDtypeStruct((spans * span, depth), BF),
        scratch_shapes=[pltpu.VMEM((span, depth), F32)],
        compiler_params=params(48),
        cost_estimate=cost(2 * spans * span * depth * joint * slots, 2 * spans * span * joint * slots),
        name="project_back",
    )(delta, query, key, value)


def project_gradient_kernel(x_ref, d_ref, q_ref, k_ref, v_ref, acc):
    span = pl.program_id(1)
    made = dot(x_ref[...], d_ref[0])

    @pl.when(span == 0)
    def _():
        acc[...] = made

    @pl.when(span > 0)
    def _():
        acc[...] += made

    @pl.when(span == pl.num_programs(1) - 1)
    def _():
        width = q_ref.shape[1]
        q_ref[...] = acc[:, :width].astype(BF)
        k_ref[...] = acc[:, width : 2 * width].astype(BF)
        v_ref[...] = acc[:, 2 * width :].astype(BF)


def project_gradient(turned, delta, spans, slots):
    depth, tokens = turned.shape
    _, span, joint = delta.shape
    width = joint // 3
    out = pl.BlockSpec((depth, width), lambda h, s: (0, h))
    return pl.pallas_call(
        project_gradient_kernel,
        grid=(slots, spans),
        in_specs=[
            pl.BlockSpec((depth, span), lambda h, s: (0, s)),
            pl.BlockSpec((1, span, joint), lambda h, s: (s * slots + h, 0, 0)),
        ],
        out_specs=[out, out, out],
        out_shape=[jax.ShapeDtypeStruct((depth, width * slots), BF)] * 3,
        scratch_shapes=[pltpu.VMEM((depth, joint), F32)],
        compiler_params=params(48),
        cost_estimate=cost(2 * tokens * depth * joint * slots, 2 * tokens * joint * slots),
        name="project_gradient",
    )(turned, delta)


def output_kernel(m_ref, w_ref, o_ref, acc):
    slot = pl.program_id(1)

    @pl.when(slot == 0)
    def _():
        acc[...] = jnp.zeros_like(acc)

    acc[...] += dot(m_ref[0], w_ref[...])

    @pl.when(slot == pl.num_programs(1) - 1)
    def _():
        o_ref[...] = acc[...].astype(BF)


def output_project(mixed, weight, spans, slots):
    _, span, width = mixed.shape
    depth = weight.shape[1]
    return pl.pallas_call(
        output_kernel,
        grid=(spans, slots),
        in_specs=[
            pl.BlockSpec((1, span, width), lambda s, h: (s * slots + h, 0, 0)),
            pl.BlockSpec((width, depth), lambda s, h: (h, 0)),
        ],
        out_specs=pl.BlockSpec((span, depth), lambda s, h: (s, 0)),
        out_shape=jax.ShapeDtypeStruct((spans * span, depth), BF),
        scratch_shapes=[pltpu.VMEM((span, depth), F32)],
        compiler_params=params(48),
        cost_estimate=cost(2 * spans * span * depth * width * slots, 2 * spans * span * width * slots),
        name="output_project",
    )(mixed, weight)


def output_back_kernel(d_ref, w_ref, o_ref):
    o_ref[0] = dot_nt(d_ref[...], w_ref[...]).astype(BF)


def output_back(delta, weight, spans, slots):
    tokens, depth = delta.shape
    width, span = weight.shape[0] // slots, tokens // spans
    return pl.pallas_call(
        output_back_kernel,
        grid=(spans, slots),
        in_specs=[
            pl.BlockSpec((span, depth), lambda s, h: (s, 0)),
            pl.BlockSpec((width, depth), lambda s, h: (h, 0)),
        ],
        out_specs=pl.BlockSpec((1, span, width), lambda s, h: (s * slots + h, 0, 0)),
        out_shape=jax.ShapeDtypeStruct((spans * slots, span, width), BF),
        compiler_params=params(48),
        cost_estimate=cost(2 * tokens * depth * width * slots, 2 * tokens * width * slots),
        name="output_back",
    )(delta, weight)


def allowed_pairs(column_ref, row_ref, start, block, reach):
    marks = column_ref[start : start + block, :] == row_ref[0, :, :reach]
    places = iota((block, reach), 1) <= iota((block, reach), 0) + start
    return marks & places


def attend_kernel(q_ref, k_ref, v_ref, column_ref, row_ref, o_ref, log_ref):
    length = q_ref.shape[0]
    block = min(256, length)
    for start in range(0, length, block):
        reach = start + block
        scores = dot_nt(q_ref[start:reach, :], k_ref[:reach, :]) * HEAD_DIM**-0.5
        scores = jnp.where(
            allowed_pairs(column_ref, row_ref, start, block, reach), scores, NEGATIVE
        )
        largest = jnp.max(scores, axis=1, keepdims=True)
        raised = jnp.exp(scores - largest)
        summed = jnp.sum(raised, axis=1, keepdims=True)
        weights = (raised * (1.0 / summed)).astype(BF)
        o_ref[start:reach, :] = dot(weights, v_ref[:reach, :]).astype(BF)
        log_ref[0, start:reach, :] = largest + jnp.log(summed)


def attend(query, key, value, marks, length):
    tokens, width = query.shape
    heads, count = width // HEAD_DIM, tokens // length
    rows = pl.BlockSpec((length, HEAD_DIM), lambda b, h: (b, h))
    return pl.pallas_call(
        attend_kernel,
        grid=(count, heads),
        in_specs=[
            rows,
            rows,
            rows,
            pl.BlockSpec((length, 1), lambda b, h: (b, 0)),
            pl.BlockSpec((1, 1, length), lambda b, h: (b, 0, 0)),
        ],
        out_specs=[rows, pl.BlockSpec((1, length, 1), lambda b, h: (h, b, 0))],
        out_shape=[
            jax.ShapeDtypeStruct((tokens, width), BF),
            jax.ShapeDtypeStruct((heads, tokens, 1), F32),
        ],
        compiler_params=params(48),
        cost_estimate=cost(4 * tokens * length * width, 8 * tokens * width),
        name="attend",
    )(query, key, value, marks.reshape(tokens, 1), marks.reshape(count, 1, length))


def attend_back_kernel(
    q_ref, k_ref, v_ref, d_ref, log_ref, column_ref, row_ref, dq_ref, dk_ref, dv_ref
):
    length = q_ref.shape[0]
    block = min(256, length)
    scale = HEAD_DIM**-0.5
    for start in reversed(range(0, length, block)):
        reach = start + block
        query, delta = q_ref[start:reach, :], d_ref[start:reach, :]
        key, value = k_ref[:reach, :], v_ref[:reach, :]
        scores = dot_nt(query, key) * scale
        allowed = allowed_pairs(column_ref, row_ref, start, block, reach)
        probs = jnp.where(allowed, jnp.exp(scores - log_ref[0, start:reach, :]), 0.0)
        weights_delta = dot_nt(delta, value)
        centre = jnp.sum(probs * weights_delta, axis=1, keepdims=True)
        score_delta = (probs * (weights_delta - centre)).astype(BF)
        dq_ref[start:reach, :] = dot(score_delta, key) * scale
        key_delta = dot_tn(score_delta, query) * scale
        value_delta = dot_tn(probs.astype(BF), delta)
        if reach == length:
            dk_ref[...] = key_delta
            dv_ref[...] = value_delta
        else:
            dk_ref[:reach, :] += key_delta
            dv_ref[:reach, :] += value_delta


def attend_back(query, key, value, delta, logs, marks, length):
    tokens, width = query.shape
    heads, count = width // HEAD_DIM, tokens // length
    rows = pl.BlockSpec((length, HEAD_DIM), lambda b, h: (b, h))
    return pl.pallas_call(
        attend_back_kernel,
        grid=(count, heads),
        in_specs=[
            rows,
            rows,
            rows,
            rows,
            pl.BlockSpec((1, length, 1), lambda b, h: (h, b, 0)),
            pl.BlockSpec((length, 1), lambda b, h: (b, 0)),
            pl.BlockSpec((1, 1, length), lambda b, h: (b, 0, 0)),
        ],
        out_specs=[rows, rows, rows],
        out_shape=[jax.ShapeDtypeStruct((tokens, width), F32)] * 3,
        compiler_params=params(48),
        cost_estimate=cost(10 * tokens * length * width, 20 * tokens * width),
        name="attend_back",
    )(query, key, value, delta, logs, marks.reshape(tokens, 1), marks.reshape(count, 1, length))


def dispatch_kernel(token_ref, source_ref, o_ref):
    tokens = source_ref.shape[1]
    bands = []
    for i in range(WIDE // TILE):
        ids = jnp.broadcast_to(token_ref[0, 0, i : i + 1, :], (TILE, TILE)).T
        bands.append(
            jnp.concatenate(
                [
                    jnp.where(ids == iota((TILE, TILE), 1) + j, 1.0, 0.0).astype(BF)
                    for j in range(0, tokens, TILE)
                ],
                axis=1,
            )
        )
    o_ref[0] = dot(jnp.concatenate(bands, axis=0), source_ref[0]).astype(BF)


def dispatch(tokens_of, source):
    groups, rows = tokens_of.shape
    _, tokens, depth = source.shape
    return pl.pallas_call(
        dispatch_kernel,
        grid=(groups, rows // WIDE),
        in_specs=[
            pl.BlockSpec((1, 1, WIDE // TILE, TILE), lambda g, i: (g, i, 0, 0)),
            pl.BlockSpec((1, tokens, depth), lambda g, i: (g, 0, 0)),
        ],
        out_specs=pl.BlockSpec((1, WIDE, depth), lambda g, i: (g, i, 0)),
        out_shape=jax.ShapeDtypeStruct((groups, rows, depth), BF),
        compiler_params=params(48),
        cost_estimate=cost(2 * groups * rows * tokens * depth, 2 * groups * rows * depth),
        name="dispatch",
    )(tokens_of.reshape(groups, rows // WIDE, WIDE // TILE, TILE), source)


def dispatch_turned_kernel(token_ref, scale_ref, first_ref, second_ref, a_ref, b_ref):
    tokens = first_ref.shape[2]
    chosen = jnp.where(iota((tokens, WIDE), 0) == token_ref[0, 0], 1.0, 0.0).astype(BF)
    scale = scale_ref[0, 0]
    for source, out in ((first_ref, a_ref), (second_ref, b_ref)):
        rows = (dot(source[0], chosen) * scale).astype(BF)
        for i in range(WIDE // TILE):
            out[0, i] = rows[:, i * TILE : (i + 1) * TILE]


def dispatch_turned(tokens_of, scale, first, second):
    groups, rows = tokens_of.shape
    _, depth, tokens = first.shape
    line = pl.BlockSpec((1, 1, 1, WIDE), lambda g, i: (g, i, 0, 0))
    source = pl.BlockSpec((1, depth, tokens), lambda g, i: (g, 0, 0))
    out = pl.BlockSpec((1, WIDE // TILE, depth, TILE), lambda g, i: (g, i, 0, 0))
    return pl.pallas_call(
        dispatch_turned_kernel,
        grid=(groups, rows // WIDE),
        in_specs=[line, line, source, source],
        out_specs=[out, out],
        out_shape=[jax.ShapeDtypeStruct((groups, rows // TILE, depth, TILE), BF)] * 2,
        compiler_params=params(48),
        cost_estimate=cost(4 * groups * rows * tokens * depth, 4 * groups * rows * depth),
        name="dispatch_turned",
    )(
        tokens_of.reshape(groups, rows // WIDE, 1, WIDE),
        scale.reshape(groups, rows // WIDE, 1, WIDE),
        first,
        second,
    )


def pick_kernel(token_ref, expert_ref, probs_ref, o_ref):
    experts, tokens = probs_ref.shape[1], probs_ref.shape[2]
    left, parts = probs_ref[0], []
    for _ in range(3):
        part = left.astype(BF)
        parts.append(part)
        left = left - part.astype(F32)
    chosen = jnp.where(iota((tokens, WIDE), 0) == token_ref[0, 0], 1.0, 0.0).astype(BF)
    found = dot(parts[0], chosen) + dot(parts[1], chosen) + dot(parts[2], chosen)
    match = iota((experts, WIDE), 0) == expert_ref[0, 0]
    o_ref[0, 0] = jnp.sum(jnp.where(match, found, 0.0), axis=0, keepdims=True)


def pick(tokens_of, experts_of, probs):
    groups, rows = tokens_of.shape
    _, experts, tokens = probs.shape
    line = pl.BlockSpec((1, 1, 1, WIDE), lambda g, i: (g, i, 0, 0))
    shape = (groups, rows // WIDE, 1, WIDE)
    return pl.pallas_call(
        pick_kernel,
        grid=(groups, rows // WIDE),
        in_specs=[line, line, pl.BlockSpec((1, experts, tokens), lambda g, i: (g, 0, 0))],
        out_specs=line,
        out_shape=jax.ShapeDtypeStruct(shape, F32),
        compiler_params=params(48),
        cost_estimate=cost(6 * groups * rows * tokens * experts, 8 * groups * rows),
        name="pick",
    )(tokens_of.reshape(shape), experts_of.reshape(shape), probs).reshape(groups, rows)


def each_tile(low, high, run):
    first = low // TILE
    count = jnp.where(high > low, (high + TILE - 1) // TILE - first, 0)
    full = count // 4

    def step(i, carry):
        run(pl.multiple_of((first + 4 * i) * TILE, TILE), 4)
        return carry

    lax.fori_loop(0, full, step, 0)
    left = count - 4 * full
    for some in (1, 2, 3):

        @pl.when(left == some)
        def _():
            run(pl.multiple_of((first + 4 * full) * TILE, TILE), some)


def kept(base, rows, low, high):
    places = base + iota((rows, 1), 0)
    return (places >= low) & (places < high)


def gate_up_kernel(offset_ref, x_ref, gate_ref, up_ref, o_ref):
    group, expert = pl.program_id(0), pl.program_id(1)
    low, high = offset_ref[group, expert], offset_ref[group, expert + 1]
    half = gate_ref.shape[2]

    def run(base, tiles):
        rows = pl.ds(base, tiles * TILE)
        keep = kept(base, tiles * TILE, low, high)
        x = x_ref[0, rows, :]
        for start, weight in ((0, gate_ref), (half, up_ref)):
            columns = slice(start, start + half)
            made = dot(x, weight[0]).astype(BF)
            o_ref[0, rows, columns] = jnp.where(keep, made, o_ref[0, rows, columns])

    each_tile(low, high, run)


def gate_up(offsets, x, gate, up, part, half):
    groups, rows, depth = x.shape
    experts = gate.shape[0]
    weight = pl.BlockSpec((1, depth, half), lambda g, e, o: (e, 0, part))
    return pl.pallas_call(
        gate_up_kernel,
        grid_spec=pltpu.PrefetchScalarGridSpec(
            num_scalar_prefetch=1,
            grid=(groups, experts),
            in_specs=[once((1, rows, depth), lambda g, e, o: (g, 0, 0)), weight, weight],
            out_specs=once((1, rows, 2 * half), lambda g, e, o: (g, 0, 0)),
        ),
        out_shape=jax.ShapeDtypeStruct((groups, rows, 2 * half), BF),
        compiler_params=params(56),
        cost_estimate=cost(6 * groups * rows * depth * half, 2 * groups * rows * depth),
        name="gate_up",
    )(offsets, x, gate, up)


def hidden_back_kernel(offset_ref, x_ref, down_ref, o_ref):
    group, expert = pl.program_id(0), pl.program_id(1)
    low, high = offset_ref[group, expert], offset_ref[group, expert + 1]

    def run(base, tiles):
        rows = pl.ds(base, tiles * TILE)
        keep = kept(base, tiles * TILE, low, high)
        made = dot_nt(x_ref[0, rows, :], down_ref[0]).astype(BF)
        o_ref[0, rows, :] = jnp.where(keep, made, o_ref[0, rows, :])

    each_tile(low, high, run)


def hidden_back(offsets, x, down):
    groups, rows, depth = x.shape
    experts, units, _ = down.shape
    return pl.pallas_call(
        hidden_back_kernel,
        grid_spec=pltpu.PrefetchScalarGridSpec(
            num_scalar_prefetch=1,
            grid=(groups, experts),
            in_specs=[
                once((1, rows, depth), lambda g, e, o: (g, 0, 0)),
                pl.BlockSpec((1, units, depth), lambda g, e, o: (e, 0, 0)),
            ],
            out_specs=once((1, rows, units), lambda g, e, o: (g, 0, 0)),
        ),
        out_shape=jax.ShapeDtypeStruct((groups, rows, units), BF),
        compiler_params=params(56),
        cost_estimate=cost(3 * groups * rows * depth * units, 2 * groups * rows * depth),
        name="hidden_back",
    )(offsets, x, down)


def activations(gate, up, delta):
    gate, up, delta = gate.astype(F32), up.astype(F32), delta.astype(F32)
    sigmoid = 0.5 * jnp.tanh(0.5 * gate) + 0.5
    silu = gate * sigmoid
    through = delta * up
    return silu * up, through * (sigmoid + silu - silu * sigmoid), delta * silu, through * silu


def combine(token_ref, scale_ref, rows_ref, o_ref):
    tokens = o_ref.shape[1]
    o_ref[0] = jnp.zeros(o_ref.shape[1:], F32)

    def step(i, carry):
        chosen = iota((tokens, WIDE), 0) == token_ref[0, i]
        chosen = jnp.where(chosen, scale_ref[0, i], 0.0).astype(BF)
        o_ref[0] += dot(chosen, rows_ref[pl.ds(pl.multiple_of(i * WIDE, WIDE), WIDE), :])
        return carry

    lax.fori_loop(0, rows_ref.shape[0] // WIDE, step, 0)


def expert_back_kernel(
    part, offset_ref, gu_ref, hd_ref, gate_ref, up_ref, token_ref, scale_ref, o_ref, made_ref
):
    group, expert = pl.program_id(0), pl.program_id(1)
    experts = pl.num_programs(1)
    low, high = offset_ref[group, expert], offset_ref[group, expert + 1]
    depth, half = gate_ref.shape[1], gate_ref.shape[2]

    def run(base, tiles):
        count = tiles * TILE
        rows = pl.ds(base, count)
        keep = kept(base, count, low, high)
        _, gate_delta, up_delta, picked = activations(
            gu_ref[0, rows, :half],
            gu_ref[0, rows, half:],
            hd_ref[0, rows, part * half : (part + 1) * half],
        )
        made = dot_nt(gate_delta.astype(BF), gate_ref[0]) + dot_nt(up_delta.astype(BF), up_ref[0])
        made_ref[rows, :depth] = jnp.where(keep, made.astype(BF), made_ref[rows, :depth])
        picked = jnp.sum(picked, axis=1, keepdims=True)
        upper = picked.astype(BF).astype(F32)
        lane = iota((count, TILE), 1)
        spread = jnp.where(
            lane == expert, upper, jnp.where(lane == expert + experts, picked - upper, 0.0)
        )
        made_ref[rows, depth:] = jnp.where(keep, spread.astype(BF), made_ref[rows, depth:])

    each_tile(low, high, run)

    @pl.when(expert == experts - 1)
    def _():
        combine(token_ref, scale_ref, made_ref, o_ref)


def expert_back(offsets, gu, hd, gate, up, tokens_of, scale, part, half, tokens):
    groups, rows, units = hd.shape
    experts, depth = gate.shape[:2]
    weight = pl.BlockSpec((1, depth, half), lambda g, e, o: (e, 0, part))
    line = once((1, rows // WIDE, 1, WIDE), lambda g, e, o: (g, 0, 0, 0))
    shape = (groups, rows // WIDE, 1, WIDE)
    return pl.pallas_call(
        functools.partial(expert_back_kernel, part),
        grid_spec=pltpu.PrefetchScalarGridSpec(
            num_scalar_prefetch=1,
            grid=(groups, experts),
            in_specs=[
                once((1, rows, 2 * half), lambda g, e, o: (g, 0, 0)),
                once((1, rows, units), lambda g, e, o: (g, 0, 0)),
                weight,
                weight,
                line,
                line,
            ],
            out_specs=once((1, tokens, depth + TILE), lambda g, e, o: (g, 0, 0)),
            scratch_shapes=[pltpu.VMEM((rows, depth + TILE), BF)],
        ),
        out_shape=jax.ShapeDtypeStruct((groups, tokens, depth + TILE), F32),
        compiler_params=params(56),
        cost_estimate=cost(
            groups * rows * depth * (6 * half + 2 * tokens), 2 * groups * rows * (2 * half + units)
        ),
        name="expert_back",
    )(offsets, gu, hd, gate, up, tokens_of.reshape(shape), scale.reshape(shape))


def down_kernel(offset_ref, down_ref, token_ref, scale_ref, *rest):
    sources, (o_ref, made_ref) = rest[:-2], rest[-2:]
    group, expert = pl.program_id(0), pl.program_id(1)
    low, high = offset_ref[group, expert], offset_ref[group, expert + 1]
    half = sources[0].shape[2] // 2

    def run(base, tiles):
        count = tiles * TILE
        rows = pl.ds(base, count)
        keep = kept(base, count, low, high)
        made = 0.0
        for i, source in enumerate(sources):
            gate = source[0, rows, :half].astype(F32)
            up = source[0, rows, half:].astype(F32)
            hidden = (gate * (0.5 * jnp.tanh(0.5 * gate) + 0.5) * up).astype(BF)
            made += dot(hidden, down_ref[0, i * half : (i + 1) * half, :])
        made_ref[rows, :] = jnp.where(keep, made.astype(BF), made_ref[rows, :])

    each_tile(low, high, run)

    @pl.when(expert == pl.num_programs(1) - 1)
    def _():
        combine(token_ref, scale_ref, made_ref, o_ref)


def expert_down(offsets, sources, down, tokens_of, scale, tokens):
    groups, rows, pair = sources[0].shape
    experts, units, depth = down.shape
    line = once((1, rows // WIDE, 1, WIDE), lambda g, e, o: (g, 0, 0, 0))
    shape = (groups, rows // WIDE, 1, WIDE)
    source = once((1, rows, pair), lambda g, e, o: (g, 0, 0))
    return pl.pallas_call(
        down_kernel,
        grid_spec=pltpu.PrefetchScalarGridSpec(
            num_scalar_prefetch=1,
            grid=(groups, experts),
            in_specs=[
                pl.BlockSpec((1, units, depth), lambda g, e, o: (e, 0, 0)),
                line,
                line,
                *[source] * len(sources),
            ],
            out_specs=once((1, tokens, depth), lambda g, e, o: (g, 0, 0)),
            scratch_shapes=[pltpu.VMEM((rows, depth), BF)],
        ),
        out_shape=jax.ShapeDtypeStruct((groups, tokens, depth), F32),
        compiler_params=params(56),
        cost_estimate=cost(
            groups * rows * depth * (3 * units + 2 * tokens), 4 * groups * rows * units
        ),
        name="expert_down",
    )(offsets, down, tokens_of.reshape(shape), scale.reshape(shape), *sources)


def gradient_kernel(part, aliased, offset_ref, gu_ref, hd_ref, xs_ref, xc_ref, *rest):
    rest = rest[3 * aliased :]
    gate_out, up_out, down_out = rest[:3]
    gu_ring, hd_ring, xs_ring, xc_ring, wide, narrow, issued, waited, sems = rest[3:]
    segments, tiles = gu_ref.shape[:2]
    half = gate_out.shape[2]
    expert = pl.program_id(0)

    def copies(segment, tile):
        slot = lax.rem(tile, RING)
        units = pl.ds(part * half, half)
        return [
            pltpu.make_async_copy(
                gu_ref.at[segment, tile], gu_ring.at[segment, slot], sems.at[0, segment, slot]
            ),
            pltpu.make_async_copy(
                hd_ref.at[segment, tile, :, units],
                hd_ring.at[segment, slot],
                sems.at[1, segment, slot],
            ),
            pltpu.make_async_copy(
                xs_ref.at[segment, tile], xs_ring.at[segment, slot], sems.at[2, segment, slot]
            ),
            pltpu.make_async_copy(
                xc_ref.at[segment, tile], xc_ring.at[segment, slot], sems.at[3, segment, slot]
            ),
        ]

    def start_until(segment, limit):
        def step(tile, carry):
            for copy in copies(segment, tile):
                copy.start()
            return carry

        lax.fori_loop(issued[segment], limit, step, 0)
        issued[segment] = jnp.maximum(issued[segment], limit)

    def wait_until(segment, limit):
        def step(tile, carry):
            for copy in copies(segment, tile):
                copy.wait()
            return carry

        lax.fori_loop(waited[segment], limit, step, 0)
        waited[segment] = jnp.maximum(waited[segment], limit)

    @pl.when(expert == 0)
    def _():
        for segment in range(segments):
            issued[segment] = 0
            waited[segment] = 0
            start_until(segment, min(RING, tiles))

    wide[...] = jnp.zeros_like(wide)
    narrow[...] = jnp.zeros_like(narrow)

    def of_segment(segment, carry):
        low, high = offset_ref[segment, expert], offset_ref[segment, expert + 1]
        first = low // TILE
        last = jnp.where(high > low, (high + TILE - 1) // TILE, first)

        def step(i, carry):
            tile = first + 4 * i
            start_until(segment, jnp.minimum(tiles, tile + RING))
            end = jnp.minimum(last, tile + 4)
            wait_until(segment, end)

            def multiply(count):
                pair, hidden, xs, xc = [], [], [], []
                for j in range(count):
                    slot = lax.rem(tile + j, RING)
                    keep = kept((tile + j) * TILE, TILE, low, high)
                    some, gate_delta, up_delta, _ = activations(
                        gu_ring[segment, slot, :, :half],
                        gu_ring[segment, slot, :, half:],
                        hd_ring[segment, slot],
                    )
                    pair.append(
                        jnp.concatenate(
                            [
                                jnp.where(keep, gate_delta, 0.0).astype(BF),
                                jnp.where(keep, up_delta, 0.0).astype(BF),
                            ],
                            axis=1,
                        )
                    )
                    hidden.append(jnp.where(keep, some, 0.0).astype(BF))
                    xs.append(xs_ring[segment, slot])
                    xc.append(xc_ring[segment, slot])
                wide[...] += dot(jnp.concatenate(xs, axis=1), jnp.concatenate(pair, axis=0))
                narrow[...] += dot(jnp.concatenate(xc, axis=1), jnp.concatenate(hidden, axis=0))

            for count in (1, 2, 3, 4):
                pl.when(end - tile == count)(functools.partial(multiply, count))
            return carry

        lax.fori_loop(0, (last - first + 3) // 4, step, 0)
        return carry

    lax.fori_loop(0, segments, of_segment, 0)
    gate_out[0] = wide[:, :half]
    up_out[0] = wide[:, half:]
    down_out[0] = narrow[...].T


def expert_gradients(offsets, gu, hd, xs, xc, part, before):
    segments, rows, pair = gu.shape
    half, tiles = pair // 2, rows // TILE
    units = hd.shape[2]
    depth = xs.shape[2]
    experts = offsets.shape[1] - 1
    anywhere = pl.BlockSpec(memory_space=pl.ANY)
    columns = pl.BlockSpec((1, depth, half), lambda e, o: (e, 0, part))
    before = list(before)
    return pl.pallas_call(
        functools.partial(gradient_kernel, part, int(bool(before))),
        grid_spec=pltpu.PrefetchScalarGridSpec(
            num_scalar_prefetch=1,
            grid=(experts,),
            in_specs=[anywhere] * (4 + len(before)),
            out_specs=[
                columns,
                columns,
                pl.BlockSpec((1, half, depth), lambda e, o: (e, part, 0)),
            ],
            scratch_shapes=[
                pltpu.VMEM((segments, RING, TILE, pair), BF),
                pltpu.VMEM((segments, RING, TILE, half), BF),
                pltpu.VMEM((segments, RING, depth, TILE), BF),
                pltpu.VMEM((segments, RING, depth, TILE), BF),
                pltpu.VMEM((depth, pair), F32),
                pltpu.VMEM((depth, half), F32),
                pltpu.SMEM((segments,), jnp.int32),
                pltpu.SMEM((segments,), jnp.int32),
                pltpu.SemaphoreType.DMA((4, segments, RING)),
            ],
        ),
        out_shape=[
            jax.ShapeDtypeStruct((experts, depth, units), F32),
            jax.ShapeDtypeStruct((experts, depth, units), F32),
            jax.ShapeDtypeStruct((experts, units, depth), F32),
        ],
        input_output_aliases={5 + i: i for i in range(len(before))},
        compiler_params=params(56),
        cost_estimate=cost(
            9 * segments * rows * depth * half, 2 * segments * rows * (3 * half + 2 * depth)
        ),
        name="expert_gradients",
    )(
        offsets,
        gu.reshape(segments, tiles, TILE, pair),
        hd.reshape(segments, tiles, TILE, units),
        xs,
        xc,
        *before,
    )


def total_rows(value):
    return lax.psum(value, "row")


def gather_columns(value):
    if lax.axis_size("col") != 2:
        return lax.all_gather(value, "col", axis=0, tiled=True)
    other = lax.ppermute(value, "col", [(0, 1), (1, 0)])
    first = lax.axis_index("col") == 0
    return jnp.concatenate(
        [jnp.where(first, value, other), jnp.where(first, other, value)], axis=0
    )


def add_columns(value):
    if lax.axis_size("col") != 2:
        return lax.psum(value, "col").astype(F32)
    other = lax.ppermute(value, "col", [(0, 1), (1, 0)])
    return value.astype(F32) + other.astype(F32)


def share_columns(value):
    count = lax.axis_size("col")
    if count != 2:
        return lax.psum_scatter(value, "col", scatter_dimension=0, tiled=True).astype(F32)
    index = lax.axis_index("col")
    halves = value.reshape(2, value.shape[0] // 2, value.shape[1])
    other = lax.ppermute(
        lax.dynamic_index_in_dim(halves, 1 - index, 0, False), "col", [(0, 1), (1, 0)]
    )
    return lax.dynamic_index_in_dim(halves, index, 0, False).astype(F32) + other.astype(F32)


def on_device(
    residual_in,
    attention_gain,
    query_weight,
    key_weight,
    value_weight,
    query_gain,
    key_gain,
    output_weight,
    expert_gain,
    router_weight,
    gate_weight,
    up_weight,
    down_weight,
    segments,
    routes,
    cotangent,
):
    row_count = lax.axis_size("row")
    row_index = lax.axis_index("row")
    column_count = lax.axis_size("col")
    column_index = lax.axis_index("col")
    local_tokens, width_part = residual_in.shape
    model_width = width_part * row_count
    tokens = local_tokens * column_count
    head_part = query_weight.shape[1]
    heads_here = head_part // HEAD_DIM
    slots = min(row_count, heads_here)
    spans = row_count // slots
    own_part = head_part // slots
    experts, _, units = gate_weight.shape
    parts = 2 if units % 256 == 0 else 1
    half = units // parts
    top_count = routes.shape[1]
    length = min(MAX_LEN, tokens)
    sub = min(SUB, tokens)
    groups = tokens // sub
    rows = sub * top_count

    keys = routes * sub + (jnp.arange(tokens, dtype=jnp.int32) % sub)[:, None]
    keys = lax.sort(keys.reshape(groups, rows), dimension=1)

    def places(keys):
        bounds = jnp.arange(experts + 1, dtype=jnp.int32) * sub
        below = keys[:, None, :] < bounds[None, :, None]
        return keys % sub, keys // sub, jnp.sum(below.astype(jnp.int32), axis=2)

    tokens_of, experts_of, offsets = places(keys)

    delta_group = gather_columns(cotangent)
    delta_rows = dispatch(tokens_of, delta_group.reshape(groups, sub, width_part))
    hidden_delta = hidden_back(offsets, delta_rows, down_weight)
    hidden_delta = lax.psum_scatter(
        hidden_delta.reshape(groups * rows, units), "row", scatter_dimension=0, tiled=True
    )

    residual = gather_columns(residual_in).astype(F32)
    first_scale = attention_gain.astype(F32)
    first_inverse = lax.rsqrt(
        total_rows(jnp.sum(residual * residual, axis=1)) / model_width + EPSILON
    )
    normed = (residual * first_inverse[:, None] * first_scale).astype(BF)
    joint = lax.psum_scatter(
        project(normed, query_weight, key_weight, value_weight, spans, slots),
        "row",
        scatter_dimension=0,
        tiled=False,
    )
    query_raw = joint[:, :own_part].astype(F32)
    key_raw = joint[:, own_part : 2 * own_part].astype(F32)
    value_round = joint[:, 2 * own_part :]
    span = tokens // spans
    span_start = row_index // slots * span

    def total_heads(first, second):
        sums = jnp.stack([jnp.sum(first, axis=1), jnp.sum(second, axis=1)])
        if spans > 1:
            sums = lax.dynamic_update_slice(
                jnp.zeros((2, tokens), F32), sums, (jnp.zeros((), jnp.int32), span_start)
            )
        sums = lax.psum(sums, ("row", "col"))
        return lax.dynamic_slice_in_dim(sums, span_start, span, 1) if spans > 1 else sums

    own_segments = lax.dynamic_slice_in_dim(segments, span_start, span, 0)
    square_sums = total_heads(query_raw * query_raw, key_raw * key_raw)
    query_inverse = lax.rsqrt(square_sums[0] / model_width + EPSILON)
    key_inverse = lax.rsqrt(square_sums[1] / model_width + EPSILON)
    own_start = (row_index % slots * own_part,)
    query_scale = lax.dynamic_slice(query_gain, own_start, (own_part,)).astype(F32)
    key_scale = lax.dynamic_slice(key_gain, own_start, (own_part,)).astype(F32)
    query_round = (query_raw * query_inverse[:, None] * query_scale).astype(BF)
    key_round = (key_raw * key_inverse[:, None] * key_scale).astype(BF)
    mixed, logs = attend(query_round, key_round, value_round, own_segments, length)
    mixed_group = lax.all_gather(mixed, "row", axis=0, tiled=False)
    middle = residual + add_columns(output_project(mixed_group, output_weight, spans, slots))

    second_scale = expert_gain.astype(F32)
    second_inverse = lax.rsqrt(total_rows(jnp.sum(middle * middle, axis=1)) / model_width + EPSILON)
    second = (middle * second_inverse[:, None] * second_scale).astype(BF)
    logits = total_rows(dot(second, router_weight))
    router_probs = jax.nn.softmax(logits, axis=1)
    second_rows = dispatch(tokens_of, second.reshape(groups, sub, width_part))
    scale = pick(
        tokens_of, experts_of, jnp.swapaxes(router_probs.reshape(groups, sub, experts), 1, 2)
    )
    shares, pairs = [], []
    for part in range(parts):
        made = gate_up(offsets, second_rows, gate_weight, up_weight, part, half)
        shares.append(
            lax.psum_scatter(
                made.reshape(groups * rows, 2 * half), "row", scatter_dimension=0, tiled=True
            )
        )
    for part in range(parts):
        pairs.append(
            lax.all_gather(shares[part], "row", axis=0, tiled=True).reshape(groups, rows, 2 * half)
        )

    gathered = tokens <= 2 * SUB
    if gathered:
        every = ("dp", "row")
        all_keys = lax.all_gather(keys, "dp", axis=0, tiled=True)
        all_scales = lax.all_gather(scale, "dp", axis=0, tiled=True)
        all_second = lax.all_gather(second, "dp", axis=0, tiled=True)
        all_delta = lax.all_gather(delta_group, "dp", axis=0, tiled=True)
        all_hidden = lax.all_gather(hidden_delta, every, axis=0, tiled=True)
        all_pairs = [lax.all_gather(share, every, axis=0, tiled=True) for share in shares]
        all_tokens_of, _, all_offsets = places(all_keys)
        own = lax.axis_index("dp") * (groups * rows)
        hidden_rows = lax.dynamic_slice_in_dim(all_hidden, own, groups * rows, 0)
    else:
        all_tokens_of, all_offsets, all_scales = tokens_of, offsets, scale
        all_second, all_delta, all_pairs = second, delta_group, pairs
        hidden_rows = lax.all_gather(hidden_delta, "row", axis=0, tiled=True)
        all_hidden = hidden_rows
    hidden_rows = hidden_rows.reshape(groups, rows, units)

    back = sum(
        expert_back(
            offsets, pairs[part], hidden_rows, gate_weight, up_weight, tokens_of, scale, part, half, sub
        )
        for part in range(parts)
    ).reshape(tokens, width_part + TILE)
    picked_delta = (
        back[:, width_part : width_part + experts]
        + back[:, width_part + experts : width_part + 2 * experts]
    )
    logits_delta = (
        picked_delta - router_probs * jnp.sum(picked_delta, axis=1, keepdims=True)
    ).astype(BF)
    second_delta = add_columns(
        (back[:, :width_part] + dot_nt(logits_delta, router_weight)).astype(BF)
    )
    router_gradient = lax.psum(dot_tn(second, logits_delta), ("dp", "col"))

    out_delta = delta_group.astype(F32)
    second_inner = total_rows(jnp.sum(second_delta * second_scale * middle, axis=1))
    middle_delta = (
        out_delta
        + second_inverse[:, None] * second_scale * second_delta
        - middle * (second_inverse**3 * second_inner / model_width)[:, None]
    )
    second_gain_part = jnp.sum(second_delta * middle * second_inverse[:, None], axis=0)
    attention_round = middle_delta.astype(BF)

    mixed_delta = lax.psum_scatter(
        output_back(attention_round, output_weight, spans, slots),
        "row",
        scatter_dimension=0,
        tiled=False,
    )
    query_delta, key_delta, value_delta = attend_back(
        query_round, key_round, value_round, mixed_delta, logs, own_segments, length
    )
    inner_sums = total_heads(
        query_delta * query_scale * query_raw, key_delta * key_scale * key_raw
    )
    query_raw_delta = (
        query_inverse[:, None] * query_scale * query_delta
        - query_raw * (query_inverse**3 * inner_sums[0] / model_width)[:, None]
    )
    key_raw_delta = (
        key_inverse[:, None] * key_scale * key_delta
        - key_raw * (key_inverse**3 * inner_sums[1] / model_width)[:, None]
    )
    query_gain_part = jnp.sum(query_delta * query_raw * query_inverse[:, None], axis=0)
    key_gain_part = jnp.sum(key_delta * key_raw * key_inverse[:, None], axis=0)
    joint_delta = jnp.concatenate([query_raw_delta, key_raw_delta, value_delta], axis=1).astype(BF)
    joint_group = lax.all_gather(joint_delta, "row", axis=0, tiled=False)
    first_delta = share_columns(
        project_back(joint_group, query_weight, key_weight, value_weight, spans, slots)
    )
    joint_gradients = project_gradient(normed.T, joint_group, spans, slots)

    own_tokens = column_index * local_tokens
    own_residual = residual_in.astype(F32)
    own_inverse = lax.dynamic_slice_in_dim(first_inverse, own_tokens, local_tokens, 0)
    first_inner = total_rows(jnp.sum(first_delta * first_scale * own_residual, axis=1))
    input_gradient = (
        lax.dynamic_slice_in_dim(middle_delta, own_tokens, local_tokens, 0)
        + own_inverse[:, None] * first_scale * first_delta
        - own_residual * (own_inverse**3 * first_inner / model_width)[:, None]
    )
    first_gain_part = jnp.sum(first_delta * own_residual * own_inverse[:, None], axis=0)

    expert_out = expert_down(offsets, pairs, down_weight, tokens_of, scale, sub)
    expert_out = share_columns(expert_out.reshape(tokens, width_part).astype(BF))
    residual_out = (
        lax.dynamic_slice_in_dim(middle, own_tokens, local_tokens, 0) + expert_out
    ).astype(BF)

    output_gradient = jnp.einsum(
        "srth,std->rhd",
        mixed_group.reshape(spans, slots, span, own_part),
        attention_round.reshape(spans, span, width_part),
        preferred_element_type=F32,
    ).reshape(head_part, width_part)
    query_gradient, key_gradient, value_gradient, output_gradient = [
        lax.psum(value.astype(BF), "dp").astype(F32)
        for value in (*joint_gradients, output_gradient)
    ]
    segment_count = all_offsets.shape[0]

    def turned(value):
        return jnp.swapaxes(value.reshape(segment_count, sub, width_part), 1, 2)

    second_turned, delta_turned = dispatch_turned(
        all_tokens_of, all_scales, turned(all_second), turned(all_delta)
    )
    gradients = ()
    for part in range(parts):
        gradients = expert_gradients(
            all_offsets,
            all_pairs[part].reshape(segment_count, rows, 2 * half),
            all_hidden.reshape(segment_count, rows, units),
            second_turned,
            delta_turned,
            part,
            gradients,
        )
    if not gathered:
        gradients = [lax.psum(value.astype(BF), "dp").astype(F32) for value in gradients]
    gate_gradient, up_gradient, down_gradient = gradients

    first_gain_gradient = lax.psum(first_gain_part, ("dp", "col"))
    second_gain_gradient = lax.psum(second_gain_part, "dp")
    head_gains = lax.psum(jnp.stack([query_gain_part, key_gain_part]), "dp")
    head_gains = lax.all_gather(head_gains, "row", axis=1, tiled=True)
    head_gains = jnp.sum(head_gains.reshape(2, spans, head_part), axis=1)
    return (
        residual_out,
        input_gradient,
        first_gain_gradient,
        query_gradient,
        key_gradient,
        value_gradient,
        head_gains[0],
        head_gains[1],
        output_gradient,
        second_gain_gradient,
        router_gradient,
        gate_gradient,
        up_gradient,
        down_gradient,
    )


def solution(mesh):
    tokens, routed = P(("dp", "col"), "row"), P(None, "row", "col")
    heads, gain = P("row", "col"), P("row")
    down, back = P(None, "col", "row"), P("col", "row")
    return jax.shard_map(
        on_device,
        mesh=mesh,
        in_specs=(
            tokens,
            gain,
            heads,
            heads,
            heads,
            P("col"),
            P("col"),
            back,
            gain,
            P("row", None),
            routed,
            routed,
            down,
            P("dp"),
            P("dp", None),
            tokens,
        ),
        out_specs=(
            tokens,
            tokens,
            gain,
            heads,
            heads,
            heads,
            P("col"),
            P("col"),
            back,
            gain,
            P("row", None),
            routed,
            routed,
            down,
        ),
        check_vma=False,
    )
```

```python
import functools

import jax
import jax.numpy as jnp
from jax import lax
from jax.experimental import pallas as pl
from jax.experimental.pallas import tpu as pltpu
from jax.sharding import PartitionSpec as P

HEAD_DIM = 128
MAX_LEN = 2048
EPSILON = 1e-05
NEGATIVE = -1e30

TILE = 128
WIDE = 512
SUB = 1024
PACK = 4
BAND = 4
RING = 8
MEGA = 1 << 20
BF = jnp.bfloat16
F32 = jnp.float32


def dot(left, right):
    return jnp.dot(left, right, preferred_element_type=F32)


def dot_nt(left, right):
    return lax.dot_general(left, right, (((1,), (1,)), ((), ())), preferred_element_type=F32)


def dot_tn(left, right):
    return lax.dot_general(left, right, (((0,), (0,)), ((), ())), preferred_element_type=F32)


def iota(shape, axis):
    return lax.broadcasted_iota(jnp.int32, shape, axis)


def params(mebibytes):
    return pltpu.CompilerParams(vmem_limit_bytes=mebibytes * MEGA)


def cost(flops, nbytes):
    return pl.CostEstimate(
        flops=int(flops) // 64, bytes_accessed=int(nbytes) // 64, transcendentals=0
    )


def once(shape, index):
    return pl.BlockSpec(shape, index, pipeline_mode=pl.Buffered(buffer_count=1))


def project_kernel(x_ref, q_ref, k_ref, v_ref, o_ref):
    width = q_ref.shape[1]
    x = x_ref[...]
    o_ref[0, :, :width] = dot(x, q_ref[...]).astype(BF)
    o_ref[0, :, width : 2 * width] = dot(x, k_ref[...]).astype(BF)
    o_ref[0, :, 2 * width :] = dot(x, v_ref[...]).astype(BF)


def project(x, query, key, value, spans, slots):
    tokens, depth = x.shape
    width, span = query.shape[1] // slots, tokens // spans
    weight = pl.BlockSpec((depth, width), lambda s, h: (0, h))
    return pl.pallas_call(
        project_kernel,
        grid=(spans, slots),
        in_specs=[pl.BlockSpec((span, depth), lambda s, h: (s, 0)), weight, weight, weight],
        out_specs=pl.BlockSpec((1, span, 3 * width), lambda s, h: (s * slots + h, 0, 0)),
        out_shape=jax.ShapeDtypeStruct((spans * slots, span, 3 * width), BF),
        compiler_params=params(48),
        cost_estimate=cost(6 * tokens * depth * width * slots, 6 * tokens * width * slots),
        name="project",
    )(x, query, key, value)


def project_back_kernel(d_ref, q_ref, k_ref, v_ref, o_ref, acc):
    slot = pl.program_id(1)
    width = q_ref.shape[1]

    @pl.when(slot == 0)
    def _():
        acc[...] = jnp.zeros_like(acc)

    acc[...] += (
        dot_nt(d_ref[0, :, :width], q_ref[...])
        + dot_nt(d_ref[0, :, width : 2 * width], k_ref[...])
        + dot_nt(d_ref[0, :, 2 * width :], v_ref[...])
    )

    @pl.when(slot == pl.num_programs(1) - 1)
    def _():
        o_ref[...] = acc[...].astype(BF)


def project_back(delta, query, key, value, spans, slots):
    _, span, joint = delta.shape
    depth, width = query.shape[0], joint // 3
    weight = pl.BlockSpec((depth, width), lambda s, h: (0, h))
    return pl.pallas_call(
        project_back_kernel,
        grid=(spans, slots),
        in_specs=[
            pl.BlockSpec((1, span, joint), lambda s, h: (s * slots + h, 0, 0)),
            weight,
            weight,
            weight,
        ],
        out_specs=pl.BlockSpec((span, depth), lambda s, h: (s, 0)),
        out_shape=jax.ShapeDtypeStruct((spans * span, depth), BF),
        scratch_shapes=[pltpu.VMEM((span, depth), F32)],
        compiler_params=params(48),
        cost_estimate=cost(2 * spans * span * depth * joint * slots, 2 * spans * span * joint * slots),
        name="project_back",
    )(delta, query, key, value)


def project_gradient_kernel(x_ref, d_ref, q_ref, k_ref, v_ref, acc):
    span = pl.program_id(1)
    made = dot(x_ref[...], d_ref[0])

    @pl.when(span == 0)
    def _():
        acc[...] = made

    @pl.when(span > 0)
    def _():
        acc[...] += made

    @pl.when(span == pl.num_programs(1) - 1)
    def _():
        width = q_ref.shape[1]
        q_ref[...] = acc[:, :width].astype(BF)
        k_ref[...] = acc[:, width : 2 * width].astype(BF)
        v_ref[...] = acc[:, 2 * width :].astype(BF)


def project_gradient(turned, delta, spans, slots):
    depth, tokens = turned.shape
    _, span, joint = delta.shape
    width = joint // 3
    out = pl.BlockSpec((depth, width), lambda h, s: (0, h))
    return pl.pallas_call(
        project_gradient_kernel,
        grid=(slots, spans),
        in_specs=[
            pl.BlockSpec((depth, span), lambda h, s: (0, s)),
            pl.BlockSpec((1, span, joint), lambda h, s: (s * slots + h, 0, 0)),
        ],
        out_specs=[out, out, out],
        out_shape=[jax.ShapeDtypeStruct((depth, width * slots), BF)] * 3,
        scratch_shapes=[pltpu.VMEM((depth, joint), F32)],
        compiler_params=params(48),
        cost_estimate=cost(2 * tokens * depth * joint * slots, 2 * tokens * joint * slots),
        name="project_gradient",
    )(turned, delta)


def output_kernel(m_ref, w_ref, o_ref, acc):
    slot = pl.program_id(1)

    @pl.when(slot == 0)
    def _():
        acc[...] = jnp.zeros_like(acc)

    acc[...] += dot(m_ref[0], w_ref[...])

    @pl.when(slot == pl.num_programs(1) - 1)
    def _():
        o_ref[...] = acc[...].astype(BF)


def output_project(mixed, weight, spans, slots):
    _, span, width = mixed.shape
    depth = weight.shape[1]
    return pl.pallas_call(
        output_kernel,
        grid=(spans, slots),
        in_specs=[
            pl.BlockSpec((1, span, width), lambda s, h: (s * slots + h, 0, 0)),
            pl.BlockSpec((width, depth), lambda s, h: (h, 0)),
        ],
        out_specs=pl.BlockSpec((span, depth), lambda s, h: (s, 0)),
        out_shape=jax.ShapeDtypeStruct((spans * span, depth), BF),
        scratch_shapes=[pltpu.VMEM((span, depth), F32)],
        compiler_params=params(48),
        cost_estimate=cost(2 * spans * span * depth * width * slots, 2 * spans * span * width * slots),
        name="output_project",
    )(mixed, weight)


def output_back_kernel(d_ref, w_ref, o_ref):
    o_ref[0] = dot_nt(d_ref[...], w_ref[...]).astype(BF)


def output_back(delta, weight, spans, slots):
    tokens, depth = delta.shape
    width, span = weight.shape[0] // slots, tokens // spans
    return pl.pallas_call(
        output_back_kernel,
        grid=(spans, slots),
        in_specs=[
            pl.BlockSpec((span, depth), lambda s, h: (s, 0)),
            pl.BlockSpec((width, depth), lambda s, h: (h, 0)),
        ],
        out_specs=pl.BlockSpec((1, span, width), lambda s, h: (s * slots + h, 0, 0)),
        out_shape=jax.ShapeDtypeStruct((spans * slots, span, width), BF),
        compiler_params=params(48),
        cost_estimate=cost(2 * tokens * depth * width * slots, 2 * tokens * width * slots),
        name="output_back",
    )(delta, weight)


def allowed_pairs(column_ref, row_ref, start, block, reach):
    marks = column_ref[start : start + block, :] == row_ref[0, :, :reach]
    places = iota((block, reach), 1) <= iota((block, reach), 0) + start
    return marks & places


def attend_kernel(q_ref, k_ref, v_ref, column_ref, row_ref, o_ref, log_ref):
    length = q_ref.shape[0]
    block = min(256, length)
    for start in range(0, length, block):
        reach = start + block
        scores = dot_nt(q_ref[start:reach, :], k_ref[:reach, :]) * HEAD_DIM**-0.5
        scores = jnp.where(
            allowed_pairs(column_ref, row_ref, start, block, reach), scores, NEGATIVE
        )
        largest = jnp.max(scores, axis=1, keepdims=True)
        raised = jnp.exp(scores - largest)
        summed = jnp.sum(raised, axis=1, keepdims=True)
        weights = (raised * (1.0 / summed)).astype(BF)
        o_ref[start:reach, :] = dot(weights, v_ref[:reach, :]).astype(BF)
        log_ref[0, start:reach, :] = largest + jnp.log(summed)


def attend(query, key, value, marks, length):
    tokens, width = query.shape
    heads, count = width // HEAD_DIM, tokens // length
    rows = pl.BlockSpec((length, HEAD_DIM), lambda b, h: (b, h))
    return pl.pallas_call(
        attend_kernel,
        grid=(count, heads),
        in_specs=[
            rows,
            rows,
            rows,
            pl.BlockSpec((length, 1), lambda b, h: (b, 0)),
            pl.BlockSpec((1, 1, length), lambda b, h: (b, 0, 0)),
        ],
        out_specs=[rows, pl.BlockSpec((1, length, 1), lambda b, h: (h, b, 0))],
        out_shape=[
            jax.ShapeDtypeStruct((tokens, width), BF),
            jax.ShapeDtypeStruct((heads, tokens, 1), F32),
        ],
        compiler_params=params(48),
        cost_estimate=cost(4 * tokens * length * width, 8 * tokens * width),
        name="attend",
    )(query, key, value, marks.reshape(tokens, 1), marks.reshape(count, 1, length))


def attend_back_kernel(
    q_ref, k_ref, v_ref, d_ref, log_ref, column_ref, row_ref, dq_ref, dk_ref, dv_ref
):
    length = q_ref.shape[0]
    block = min(256, length)
    scale = HEAD_DIM**-0.5
    for start in reversed(range(0, length, block)):
        reach = start + block
        query, delta = q_ref[start:reach, :], d_ref[start:reach, :]
        key, value = k_ref[:reach, :], v_ref[:reach, :]
        scores = dot_nt(query, key) * scale
        allowed = allowed_pairs(column_ref, row_ref, start, block, reach)
        probs = jnp.where(allowed, jnp.exp(scores - log_ref[0, start:reach, :]), 0.0)
        weights_delta = dot_nt(delta, value)
        centre = jnp.sum(probs * weights_delta, axis=1, keepdims=True)
        score_delta = (probs * (weights_delta - centre)).astype(BF)
        dq_ref[start:reach, :] = dot(score_delta, key) * scale
        key_delta = dot_tn(score_delta, query) * scale
        value_delta = dot_tn(probs.astype(BF), delta)
        if reach == length:
            dk_ref[...] = key_delta
            dv_ref[...] = value_delta
        else:
            dk_ref[:reach, :] += key_delta
            dv_ref[:reach, :] += value_delta


def attend_back(query, key, value, delta, logs, marks, length):
    tokens, width = query.shape
    heads, count = width // HEAD_DIM, tokens // length
    rows = pl.BlockSpec((length, HEAD_DIM), lambda b, h: (b, h))
    return pl.pallas_call(
        attend_back_kernel,
        grid=(count, heads),
        in_specs=[
            rows,
            rows,
            rows,
            rows,
            pl.BlockSpec((1, length, 1), lambda b, h: (h, b, 0)),
            pl.BlockSpec((length, 1), lambda b, h: (b, 0)),
            pl.BlockSpec((1, 1, length), lambda b, h: (b, 0, 0)),
        ],
        out_specs=[rows, rows, rows],
        out_shape=[jax.ShapeDtypeStruct((tokens, width), F32)] * 3,
        compiler_params=params(48),
        cost_estimate=cost(10 * tokens * length * width, 20 * tokens * width),
        name="attend_back",
    )(query, key, value, delta, logs, marks.reshape(tokens, 1), marks.reshape(count, 1, length))


def dispatch_kernel(token_ref, source_ref, o_ref):
    tokens = source_ref.shape[1]
    bands = []
    for i in range(WIDE // TILE):
        ids = jnp.broadcast_to(token_ref[0, 0, i : i + 1, :], (TILE, TILE)).T
        bands.append(
            jnp.concatenate(
                [
                    jnp.where(ids == iota((TILE, TILE), 1) + j, 1.0, 0.0).astype(BF)
                    for j in range(0, tokens, TILE)
                ],
                axis=1,
            )
        )
    o_ref[0] = dot(jnp.concatenate(bands, axis=0), source_ref[0]).astype(BF)


def dispatch(tokens_of, source):
    groups, rows = tokens_of.shape
    _, tokens, depth = source.shape
    return pl.pallas_call(
        dispatch_kernel,
        grid=(groups, rows // WIDE),
        in_specs=[
            pl.BlockSpec((1, 1, WIDE // TILE, TILE), lambda g, i: (g, i, 0, 0)),
            pl.BlockSpec((1, tokens, depth), lambda g, i: (g, 0, 0)),
        ],
        out_specs=pl.BlockSpec((1, WIDE, depth), lambda g, i: (g, i, 0)),
        out_shape=jax.ShapeDtypeStruct((groups, rows, depth), BF),
        compiler_params=params(48),
        cost_estimate=cost(2 * groups * rows * tokens * depth, 2 * groups * rows * depth),
        name="dispatch",
    )(tokens_of.reshape(groups, rows // WIDE, WIDE // TILE, TILE), source)


def dispatch_turned_kernel(token_ref, scale_ref, first_ref, second_ref, a_ref, b_ref):
    tokens = first_ref.shape[2]
    chosen = jnp.where(iota((tokens, WIDE), 0) == token_ref[0, 0], 1.0, 0.0).astype(BF)
    scale = scale_ref[0, 0]
    for source, out in ((first_ref, a_ref), (second_ref, b_ref)):
        rows = (dot(source[0], chosen) * scale).astype(BF)
        for i in range(WIDE // TILE):
            out[0, i] = rows[:, i * TILE : (i + 1) * TILE]


def dispatch_turned(tokens_of, scale, first, second):
    groups, rows = tokens_of.shape
    _, depth, tokens = first.shape
    line = pl.BlockSpec((1, 1, 1, WIDE), lambda g, i: (g, i, 0, 0))
    source = pl.BlockSpec((1, depth, tokens), lambda g, i: (g, 0, 0))
    out = pl.BlockSpec((1, WIDE // TILE, depth, TILE), lambda g, i: (g, i, 0, 0))
    return pl.pallas_call(
        dispatch_turned_kernel,
        grid=(groups, rows // WIDE),
        in_specs=[line, line, source, source],
        out_specs=[out, out],
        out_shape=[jax.ShapeDtypeStruct((groups, rows // TILE, depth, TILE), BF)] * 2,
        compiler_params=params(48),
        cost_estimate=cost(4 * groups * rows * tokens * depth, 4 * groups * rows * depth),
        name="dispatch_turned",
    )(
        tokens_of.reshape(groups, rows // WIDE, 1, WIDE),
        scale.reshape(groups, rows // WIDE, 1, WIDE),
        first,
        second,
    )


def pick_kernel(token_ref, expert_ref, probs_ref, o_ref):
    experts, tokens = probs_ref.shape[1], probs_ref.shape[2]
    left, parts = probs_ref[0], []
    for _ in range(3):
        part = left.astype(BF)
        parts.append(part)
        left = left - part.astype(F32)
    chosen = jnp.where(iota((tokens, WIDE), 0) == token_ref[0, 0], 1.0, 0.0).astype(BF)
    found = dot(parts[0], chosen) + dot(parts[1], chosen) + dot(parts[2], chosen)
    match = iota((experts, WIDE), 0) == expert_ref[0, 0]
    o_ref[0, 0] = jnp.sum(jnp.where(match, found, 0.0), axis=0, keepdims=True)


def pick(tokens_of, experts_of, probs):
    groups, rows = tokens_of.shape
    _, experts, tokens = probs.shape
    line = pl.BlockSpec((1, 1, 1, WIDE), lambda g, i: (g, i, 0, 0))
    shape = (groups, rows // WIDE, 1, WIDE)
    return pl.pallas_call(
        pick_kernel,
        grid=(groups, rows // WIDE),
        in_specs=[line, line, pl.BlockSpec((1, experts, tokens), lambda g, i: (g, 0, 0))],
        out_specs=line,
        out_shape=jax.ShapeDtypeStruct(shape, F32),
        compiler_params=params(48),
        cost_estimate=cost(6 * groups * rows * tokens * experts, 8 * groups * rows),
        name="pick",
    )(tokens_of.reshape(shape), experts_of.reshape(shape), probs).reshape(groups, rows)


def each_expert(offset_ref, total, run):
    group, step = pl.program_id(0), pl.program_id(1)
    spans = []
    for i in range(PACK):
        expert = step * PACK + i
        low, high = offset_ref[group, expert], offset_ref[group, expert + 1]
        spans.append((expert, low, high, low // TILE * TILE))
    rounds = 0
    for _, low, high, first in spans:
        rounds = jnp.maximum(rounds, jnp.where(high > low, (high - first + WIDE - 1) // WIDE, 0))

    def turn(j, carry):
        for i, (expert, low, high, first) in enumerate(spans):
            base = pl.multiple_of(jnp.minimum(first + j * WIDE, total - WIDE), TILE)
            run(i, expert, base, low, high)
        return carry

    lax.fori_loop(0, rounds, turn, 0)


def kept(base, rows, low, high):
    places = base + iota((rows, 1), 0)
    return (places >= low) & (places < high)


def gate_up_kernel(offset_ref, x_ref, gate_ref, up_ref, o_ref):
    half = gate_ref.shape[2]

    def run(i, expert, base, low, high):
        rows = pl.ds(base, WIDE)
        keep = kept(base, WIDE, low, high)
        x = x_ref[0, rows, :]
        for start, weight in ((0, gate_ref), (half, up_ref)):
            columns = slice(start, start + half)
            made = dot(x, weight[i]).astype(BF)
            o_ref[0, rows, columns] = jnp.where(keep, made, o_ref[0, rows, columns])

    each_expert(offset_ref, x_ref.shape[1], run)


def gate_up(offsets, x, gate, up, part, half):
    groups, rows, depth = x.shape
    experts = gate.shape[0]
    weight = pl.BlockSpec((PACK, depth, half), lambda g, e, o: (e, 0, part))
    return pl.pallas_call(
        gate_up_kernel,
        grid_spec=pltpu.PrefetchScalarGridSpec(
            num_scalar_prefetch=1,
            grid=(groups, experts // PACK),
            in_specs=[once((1, rows, depth), lambda g, e, o: (g, 0, 0)), weight, weight],
            out_specs=once((1, rows, 2 * half), lambda g, e, o: (g, 0, 0)),
        ),
        out_shape=jax.ShapeDtypeStruct((groups, rows, 2 * half), BF),
        compiler_params=params(56),
        cost_estimate=cost(6 * groups * rows * depth * half, 2 * groups * rows * depth),
        name="gate_up",
    )(offsets, x, gate, up)


def hidden_back_kernel(offset_ref, x_ref, down_ref, o_ref):
    def run(i, expert, base, low, high):
        rows = pl.ds(base, WIDE)
        made = dot_nt(x_ref[0, rows, :], down_ref[i]).astype(BF)
        keep = kept(base, WIDE, low, high)
        o_ref[0, rows, :] = jnp.where(keep, made, o_ref[0, rows, :])

    each_expert(offset_ref, x_ref.shape[1], run)


def hidden_back(offsets, x, down):
    groups, rows, depth = x.shape
    experts, units, _ = down.shape
    return pl.pallas_call(
        hidden_back_kernel,
        grid_spec=pltpu.PrefetchScalarGridSpec(
            num_scalar_prefetch=1,
            grid=(groups, experts // PACK),
            in_specs=[
                once((1, rows, depth), lambda g, e, o: (g, 0, 0)),
                pl.BlockSpec((PACK, units, depth), lambda g, e, o: (e, 0, 0)),
            ],
            out_specs=once((1, rows, units), lambda g, e, o: (g, 0, 0)),
        ),
        out_shape=jax.ShapeDtypeStruct((groups, rows, units), BF),
        compiler_params=params(56),
        cost_estimate=cost(3 * groups * rows * depth * units, 2 * groups * rows * depth),
        name="hidden_back",
    )(offsets, x, down)


def slopes(gate):
    gate = 0.5 * gate.astype(F32)
    turned = jnp.tanh(gate)
    product = gate * turned
    return gate + product, (0.5 + 0.5 * turned) * ((1.0 + gate) - product)


def combine(token_ref, scale_ref, rows_ref, o_ref):
    tokens = o_ref.shape[1]
    o_ref[0] = jnp.zeros(o_ref.shape[1:], F32)

    def step(i, carry):
        chosen = iota((tokens, WIDE), 0) == token_ref[0, i]
        chosen = jnp.where(chosen, scale_ref[0, i], 0.0).astype(BF)
        o_ref[0] += dot(chosen, rows_ref[pl.ds(pl.multiple_of(i * WIDE, WIDE), WIDE), :])
        return carry

    lax.fori_loop(0, rows_ref.shape[0] // WIDE, step, 0)


def expert_back_kernel(
    part, offset_ref, _, g_ref, u_ref, hd_ref, gate_ref, up_ref, token_ref, scale_ref, o_ref, made_ref
):
    experts = PACK * pl.num_programs(1)
    depth, half = gate_ref.shape[1], gate_ref.shape[2]

    def run(i, expert, base, low, high):
        rows = pl.ds(base, WIDE)
        keep = kept(base, WIDE, low, high)
        silu, slope = slopes(g_ref[0, rows, :])
        delta = hd_ref[0, rows, part * half : (part + 1) * half]
        through = delta * u_ref[0, rows, :]
        picked = through.astype(F32) * silu
        made = dot_nt(through * slope.astype(BF), gate_ref[i])
        made += dot_nt(delta * silu.astype(BF), up_ref[i])
        made_ref[rows, :depth] = jnp.where(keep, made.astype(BF), made_ref[rows, :depth])
        picked = jnp.sum(picked, axis=1, keepdims=True)
        upper = picked.astype(BF).astype(F32)
        lane = iota((WIDE, TILE), 1)
        spread = jnp.where(
            lane == expert, upper, jnp.where(lane == expert + experts, picked - upper, 0.0)
        )
        made_ref[rows, depth:] = jnp.where(keep, spread.astype(BF), made_ref[rows, depth:])

    each_expert(offset_ref, made_ref.shape[0], run)

    @pl.when(pl.program_id(1) == pl.num_programs(1) - 1)
    def _():
        combine(token_ref, scale_ref, made_ref, o_ref)


def expert_back(offsets, base, pair, hd, gate, up, tokens_of, scale, part, half, tokens):
    groups, rows = tokens_of.shape
    units = hd.shape[2]
    experts, depth = gate.shape[:2]
    weight = pl.BlockSpec((PACK, depth, half), lambda g, e, o, b: (e, 0, part))
    line = once((1, rows // WIDE, 1, WIDE), lambda g, e, o, b: (g, 0, 0, 0))
    shape = (groups, rows // WIDE, 1, WIDE)
    return pl.pallas_call(
        functools.partial(expert_back_kernel, part),
        grid_spec=pltpu.PrefetchScalarGridSpec(
            num_scalar_prefetch=2,
            grid=(groups, experts // PACK),
            in_specs=[
                *[
                    once((1, rows, half), lambda g, e, o, b, c=column: (b[0] + g, 0, c))
                    for _, column in pair
                ],
                once((1, rows, units), lambda g, e, o, b: (b[1] + g, 0, 0)),
                weight,
                weight,
                line,
                line,
            ],
            out_specs=once((1, tokens, depth + TILE), lambda g, e, o, b: (g, 0, 0)),
            scratch_shapes=[pltpu.VMEM((rows, depth + TILE), BF)],
        ),
        out_shape=jax.ShapeDtypeStruct((groups, tokens, depth + TILE), F32),
        compiler_params=params(56),
        cost_estimate=cost(
            groups * rows * depth * (6 * half + 2 * tokens), 2 * groups * rows * (2 * half + units)
        ),
        name="expert_back",
    )(offsets, base, pair[0][0], pair[1][0], hd, gate, up, tokens_of.reshape(shape), scale.reshape(shape))


def down_kernel(offset_ref, base_ref, down_ref, token_ref, scale_ref, *rest):
    sources, (o_ref, made_ref) = rest[:-2], rest[-2:]
    half = sources[0].shape[2]

    def run(i, expert, base, low, high):
        rows = pl.ds(base, WIDE)
        keep = kept(base, WIDE, low, high)
        hidden = []
        for gate_ref, up_ref in zip(sources[::2], sources[1::2]):
            gate = 0.5 * gate_ref[0, rows, :].astype(F32)
            silu = gate + gate * jnp.tanh(gate)
            hidden.append((silu * up_ref[0, rows, :].astype(F32)).astype(BF))
        made = dot(jnp.concatenate(hidden, axis=1), down_ref[i])
        made_ref[rows, :] = jnp.where(keep, made.astype(BF), made_ref[rows, :])

    each_expert(offset_ref, made_ref.shape[0], run)

    @pl.when(pl.program_id(1) == pl.num_programs(1) - 1)
    def _():
        combine(token_ref, scale_ref, made_ref, o_ref)


def expert_down(offsets, bases, pairs, half, down, tokens_of, scale, tokens):
    groups, rows = tokens_of.shape
    experts, units, depth = down.shape
    line = once((1, rows // WIDE, 1, WIDE), lambda g, e, o, b: (g, 0, 0, 0))
    shape = (groups, rows // WIDE, 1, WIDE)

    def source(i, column):
        return once((1, rows, half), lambda g, e, o, b: (b[i] + g, 0, column))

    specs = [source(i, column) for i, pair in enumerate(pairs) for _, column in pair]
    sources = [value for pair in pairs for value, _ in pair]
    return pl.pallas_call(
        down_kernel,
        grid_spec=pltpu.PrefetchScalarGridSpec(
            num_scalar_prefetch=2,
            grid=(groups, experts // PACK),
            in_specs=[
                pl.BlockSpec((PACK, units, depth), lambda g, e, o, b: (e, 0, 0)),
                line,
                line,
                *specs,
            ],
            out_specs=once((1, tokens, depth), lambda g, e, o, b: (g, 0, 0)),
            scratch_shapes=[pltpu.VMEM((rows, depth), BF)],
        ),
        out_shape=jax.ShapeDtypeStruct((groups, tokens, depth), F32),
        compiler_params=params(56),
        cost_estimate=cost(
            groups * rows * depth * (3 * units + 2 * tokens), 4 * groups * rows * units
        ),
        name="expert_down",
    )(offsets, bases, down, tokens_of.reshape(shape), scale.reshape(shape), *sources)


def gradient_kernel(part, start, pieces, aliased, offset_ref, *rest):
    piece_refs, rest = rest[:pieces], rest[pieces:]
    hd_ref, xs_ref, xc_ref = rest[:3]
    rest = rest[3 + 3 * aliased :]
    gate_out, up_out, down_out = rest[:3]
    gu_ring, hd_ring, xs_ring, xc_ring, wide, narrow, issued, waited, sems = rest[3:]
    segments, tiles = xs_ref.shape[:2]
    shares, run_tiles = piece_refs[0].shape[1:3]
    share_tiles = pieces * run_tiles
    half = gate_out.shape[2]
    expert = start + pl.program_id(0)
    stop = start + pl.num_programs(0)

    def copies(segment, tile):
        slot = lax.rem(tile, RING)
        units = pl.ds(part * half, half)
        return [
            pltpu.make_async_copy(
                hd_ref.at[segment, tile, :, units],
                hd_ring.at[segment, slot],
                sems.at[1, segment, slot],
            ),
            pltpu.make_async_copy(
                xs_ref.at[segment, tile], xs_ring.at[segment, slot], sems.at[2, segment, slot]
            ),
            pltpu.make_async_copy(
                xc_ref.at[segment, tile], xc_ring.at[segment, slot], sems.at[3, segment, slot]
            ),
        ]

    def piece_copy(piece, segment, tile):
        slot = lax.rem(tile, RING)
        share, place = tile // share_tiles, lax.rem(tile, run_tiles)
        return pltpu.make_async_copy(
            piece_refs[piece].at[segment, share, place],
            gu_ring.at[segment, slot],
            sems.at[0, segment, slot],
        )

    def start_until(segment, limit):
        def step(tile, carry):
            for copy in copies(segment, tile):
                copy.start()
            if pieces == 1:
                piece_copy(0, segment, tile).start()
            else:
                held = lax.rem(tile, share_tiles) // run_tiles
                for piece in range(pieces):
                    pl.when(held == piece)(
                        lambda piece=piece: piece_copy(piece, segment, tile).start()
                    )
            return carry

        lax.fori_loop(issued[segment], limit, step, 0)
        issued[segment] = jnp.maximum(issued[segment], limit)

    def wait_until(segment, limit):
        def step(tile, carry):
            for copy in copies(segment, tile):
                copy.wait()
            piece_copy(0, segment, tile).wait()
            return carry

        lax.fori_loop(waited[segment], limit, step, 0)
        waited[segment] = jnp.maximum(waited[segment], limit)

    bounds = [
        (offset_ref[i, start] // TILE, (offset_ref[i, stop] + TILE - 1) // TILE)
        for i in range(segments)
    ]

    @pl.when(expert == start)
    def _():
        for segment, (head, tail) in enumerate(bounds):
            issued[segment] = head
            waited[segment] = head
            start_until(segment, jnp.minimum(head + RING - 1, tail))
            wait_until(segment, jnp.minimum(head + 1, tail))

            @pl.when(tail <= head)
            def _():
                slot = lax.rem(head, RING)
                for ring in (gu_ring, hd_ring, xs_ring, xc_ring):
                    ring[segment, slot] = jnp.zeros(ring.shape[2:], BF)

    wide[...] = jnp.zeros_like(wide)
    narrow[...] = jnp.zeros_like(narrow)
    spans, rounds = [], 0
    for segment in range(segments):
        low, high = offset_ref[segment, expert], offset_ref[segment, expert + 1]
        first = low // TILE
        last = jnp.where(high > low, (high + TILE - 1) // TILE, first)
        spans.append((low, high, first, last))
        rounds = jnp.maximum(rounds, (last - first + BAND - 1) // BAND)

    def turn(i, carry):
        for segment, (low, high, first, last) in enumerate(spans):
            tile = jnp.minimum(first + BAND * i, last)
            start_until(segment, jnp.minimum(bounds[segment][1], tile + RING - 1))
            wait_until(segment, jnp.minimum(last, tile + BAND))
        for segment, (low, high, first, last) in enumerate(spans):
            if segment % 2 == 0:
                pair, hidden, xs, xc = [], [], [], []
            for j in range(BAND):
                tile = first + BAND * i + j
                slot = lax.rem(jnp.maximum(jnp.minimum(tile, last - 1), bounds[segment][0]), RING)
                keep = kept(tile * TILE, TILE, low, high)
                silu, slope = slopes(gu_ring[segment, slot, :, :half])
                silu = jnp.where(keep, silu, 0.0).astype(BF)
                slope = jnp.where(keep, slope, 0.0).astype(BF)
                up, delta = gu_ring[segment, slot, :, half:], hd_ring[segment, slot]
                pair.append(jnp.concatenate([delta * up * slope, delta * silu], axis=1))
                hidden.append(silu * up)
                xs.append(xs_ring[segment, slot])
                xc.append(xc_ring[segment, slot])
            if segment % 2 == 0 and segment + 1 < segments:
                continue
            wide[...] += dot(jnp.concatenate(xs, axis=1), jnp.concatenate(pair, axis=0))
            narrow[...] += dot(jnp.concatenate(xc, axis=1), jnp.concatenate(hidden, axis=0))
        return carry

    lax.fori_loop(0, rounds, turn, 0)

    @pl.when(expert == stop - 1)
    def _():
        for segment in range(segments):
            wait_until(segment, issued[segment])

    gate_out[0] = wide[:, :half]
    up_out[0] = wide[:, half:]
    down_out[0] = narrow[...].T


def expert_gradients(offsets, pieces, hd, xs, xc, part, start, count, before):
    segments, shares, run, pair = pieces[0].shape
    half, rows = pair // 2, hd.shape[1]
    tiles = rows // TILE
    units = hd.shape[2]
    depth = xs.shape[2]
    experts = offsets.shape[1] - 1
    anywhere = pl.BlockSpec(memory_space=pl.ANY)
    columns = pl.BlockSpec((1, depth, half), lambda e, o: (start + e, 0, part))
    before = list(before)
    return pl.pallas_call(
        functools.partial(gradient_kernel, part, start, len(pieces), int(bool(before))),
        grid_spec=pltpu.PrefetchScalarGridSpec(
            num_scalar_prefetch=1,
            grid=(count,),
            in_specs=[anywhere] * (len(pieces) + 3 + len(before)),
            out_specs=[
                columns,
                columns,
                pl.BlockSpec((1, half, depth), lambda e, o: (start + e, part, 0)),
            ],
            scratch_shapes=[
                pltpu.VMEM((segments, RING, TILE, pair), BF),
                pltpu.VMEM((segments, RING, TILE, half), BF),
                pltpu.VMEM((segments, RING, depth, TILE), BF),
                pltpu.VMEM((segments, RING, depth, TILE), BF),
                pltpu.VMEM((depth, pair), F32),
                pltpu.VMEM((depth, half), F32),
                pltpu.SMEM((segments,), jnp.int32),
                pltpu.SMEM((segments,), jnp.int32),
                pltpu.SemaphoreType.DMA((4, segments, RING)),
            ],
        ),
        out_shape=[
            jax.ShapeDtypeStruct((experts, depth, units), F32),
            jax.ShapeDtypeStruct((experts, depth, units), F32),
            jax.ShapeDtypeStruct((experts, units, depth), F32),
        ],
        input_output_aliases={len(pieces) + 4 + i: i for i in range(len(before))},
        compiler_params=params(56),
        cost_estimate=cost(
            9 * segments * rows * depth * half, 2 * segments * rows * (3 * half + 2 * depth)
        ),
        name="expert_gradients",
    )(
        offsets,
        *[piece.reshape(segments, shares, run // TILE, TILE, pair) for piece in pieces],
        hd.reshape(segments, tiles, TILE, units),
        xs,
        xc,
        *before,
    )


def in_order(*values):
    return lax.optimization_barrier(values)


def total_rows(value):
    return lax.psum(value, "row")


def exchange(value, axis):
    count, apart = lax.axis_size(axis), 1
    while apart < count:
        value = value + lax.ppermute(value, axis, [(i, i ^ apart) for i in range(count)])
        apart *= 2
    return value


def scatter_rows(value):
    count = lax.axis_size("row")
    if count != 4:
        return lax.psum_scatter(value, "row", scatter_dimension=0, tiled=False)
    index = lax.axis_index("row")

    def halve(value, axis, mine, apart):
        sent = lax.dynamic_index_in_dim(value, 1 - mine, axis, False)
        kept = lax.dynamic_index_in_dim(value, mine, axis, False)
        other = lax.ppermute(sent, "row", [(i, i ^ apart) for i in range(count)])
        return (kept.astype(F32) + other.astype(F32)).astype(BF)

    value = halve(value.reshape(2, 2, *value.shape[1:]), 1, index % 2, 1)
    return halve(value, 0, index // 2, 2)


def gather_planes(value):
    count = lax.axis_size("dp")
    pieces = [value] + [
        lax.ppermute(value, "dp", [(i, (i - apart) % count) for i in range(count)])
        for apart in range(1, count)
    ]
    first = (count - lax.axis_index("dp")) % count * value.shape[0]
    return lax.dynamic_slice_in_dim(
        jnp.concatenate(pieces + pieces[:-1], axis=0), first, count * value.shape[0], 0
    )


def exchange_columns(value):
    if lax.axis_size("col") != 2:
        return lax.psum(value, "col")
    return value + lax.ppermute(value, "col", [(0, 1), (1, 0)])


def gather_columns(value):
    if lax.axis_size("col") != 2:
        return lax.all_gather(value, "col", axis=0, tiled=True)
    other = lax.ppermute(value, "col", [(0, 1), (1, 0)])
    first = lax.axis_index("col") == 0
    return jnp.concatenate(
        [jnp.where(first, value, other), jnp.where(first, other, value)], axis=0
    )


def add_columns(value):
    if lax.axis_size("col") != 2:
        return lax.psum(value, "col").astype(F32)
    other = lax.ppermute(value, "col", [(0, 1), (1, 0)])
    return value.astype(F32) + other.astype(F32)


def share_columns(value):
    count = lax.axis_size("col")
    if count != 2:
        return lax.psum_scatter(value, "col", scatter_dimension=0, tiled=True).astype(F32)
    index = lax.axis_index("col")
    halves = value.reshape(2, value.shape[0] // 2, value.shape[1])
    other = lax.ppermute(
        lax.dynamic_index_in_dim(halves, 1 - index, 0, False), "col", [(0, 1), (1, 0)]
    )
    return lax.dynamic_index_in_dim(halves, index, 0, False).astype(F32) + other.astype(F32)


def on_device(
    residual_in,
    attention_gain,
    query_weight,
    key_weight,
    value_weight,
    query_gain,
    key_gain,
    output_weight,
    expert_gain,
    router_weight,
    gate_weight,
    up_weight,
    down_weight,
    segments,
    routes,
    cotangent,
):
    row_count = lax.axis_size("row")
    row_index = lax.axis_index("row")
    column_count = lax.axis_size("col")
    column_index = lax.axis_index("col")
    local_tokens, width_part = residual_in.shape
    model_width = width_part * row_count
    tokens = local_tokens * column_count
    head_part = query_weight.shape[1]
    heads_here = head_part // HEAD_DIM
    slots = min(row_count, heads_here)
    spans = row_count // slots
    own_part = head_part // slots
    experts, _, units = gate_weight.shape
    parts = 2 if units % 256 == 0 else 1
    half = units // parts
    top_count = routes.shape[1]
    length = min(MAX_LEN, tokens)
    sub = min(SUB, tokens)
    groups = tokens // sub
    rows = sub * top_count

    keys = routes * sub + (jnp.arange(tokens, dtype=jnp.int32) % sub)[:, None]
    keys = lax.sort(keys.reshape(groups, rows), dimension=1)

    def places(keys):
        bounds = jnp.arange(experts + 1, dtype=jnp.int32) * sub
        below = keys[:, None, :] < bounds[None, :, None]
        return keys % sub, keys // sub, jnp.sum(below.astype(jnp.int32), axis=2)

    tokens_of, experts_of, offsets = places(keys)

    delta_group = gather_columns(cotangent)
    gathered = tokens <= 2 * SUB
    planes = ("dp", "col")
    all_delta, all_keys = delta_group, keys
    if gathered:
        all_delta = lax.all_gather(cotangent, planes, axis=0, tiled=True)
        all_keys = lax.all_gather(keys, "dp", axis=0, tiled=True)
    delta_rows = dispatch(tokens_of, delta_group.reshape(groups, sub, width_part))
    hidden_part = hidden_back(offsets, delta_rows, down_weight)

    residual = gather_columns(residual_in).astype(F32)
    first_scale = attention_gain.astype(F32)
    first_inverse = lax.rsqrt(
        total_rows(jnp.sum(residual * residual, axis=1)) / model_width + EPSILON
    )
    normed = (residual * first_inverse[:, None] * first_scale).astype(BF)
    joint = lax.psum_scatter(
        project(normed, query_weight, key_weight, value_weight, spans, slots),
        "row",
        scatter_dimension=0,
        tiled=False,
    )
    joint, hidden_part, all_keys = in_order(joint, hidden_part, all_keys)
    query_raw = joint[:, :own_part].astype(F32)
    key_raw = joint[:, own_part : 2 * own_part].astype(F32)
    value_round = joint[:, 2 * own_part :]
    span = tokens // spans
    span_start = row_index // slots * span

    def total_heads(first, second):
        sums = jnp.stack([jnp.sum(first, axis=1), jnp.sum(second, axis=1)])
        if spans > 1:
            sums = lax.dynamic_update_slice(
                jnp.zeros((2, tokens), F32), sums, (jnp.zeros((), jnp.int32), span_start)
            )
        sums = total_rows(exchange_columns(sums))
        return lax.dynamic_slice_in_dim(sums, span_start, span, 1) if spans > 1 else sums

    own_segments = lax.dynamic_slice_in_dim(segments, span_start, span, 0)
    square_sums = total_heads(query_raw * query_raw, key_raw * key_raw)
    query_inverse = lax.rsqrt(square_sums[0] / model_width + EPSILON)
    key_inverse = lax.rsqrt(square_sums[1] / model_width + EPSILON)
    own_start = (row_index % slots * own_part,)
    query_scale = lax.dynamic_slice(query_gain, own_start, (own_part,)).astype(F32)
    key_scale = lax.dynamic_slice(key_gain, own_start, (own_part,)).astype(F32)
    query_round = (query_raw * query_inverse[:, None] * query_scale).astype(BF)
    key_round = (key_raw * key_inverse[:, None] * key_scale).astype(BF)
    mixed, logs = attend(query_round, key_round, value_round, own_segments, length)
    mixed, all_delta = in_order(mixed, all_delta)
    mixed_group = lax.all_gather(mixed, "row", axis=0, tiled=False)
    hidden_delta = lax.psum_scatter(
        hidden_part.reshape(groups * rows, units),
        "row",
        scatter_dimension=0,
        tiled=True,
    )
    middle = residual + add_columns(output_project(mixed_group, output_weight, spans, slots))

    second_scale = expert_gain.astype(F32)
    second_inverse = lax.rsqrt(total_rows(jnp.sum(middle * middle, axis=1)) / model_width + EPSILON)
    second = (middle * second_inverse[:, None] * second_scale).astype(BF)
    logits = exchange(
        lax.dot_general(
            router_weight, second, (((0,), (1,)), ((), ())), preferred_element_type=F32
        ),
        "row",
    )
    turned_probs = jax.nn.softmax(logits, axis=0)
    router_probs = turned_probs.T
    second_rows = dispatch(tokens_of, second.reshape(groups, sub, width_part))
    scale = pick(
        tokens_of, experts_of, jnp.swapaxes(turned_probs.reshape(experts, groups, sub), 0, 1)
    )
    own_tokens = column_index * local_tokens
    shares, pairs = [], []
    for part in range(parts):
        made = gate_up(offsets, second_rows, gate_weight, up_weight, part, half)
        if part == 0:
            made, hidden_delta = in_order(made, hidden_delta)
        shares.append(
            lax.psum_scatter(
                made.reshape(groups * rows, 2 * half), "row", scatter_dimension=0, tiled=True
            )
        )
    def turned(value):
        return jnp.swapaxes(value.reshape(-1, sub, width_part), 1, 2)

    def back_of(part, pair, base, hidden_rows, hidden_base):
        return expert_back(
            offsets,
            jnp.stack([base, hidden_base]),
            pair,
            hidden_rows,
            gate_weight,
            up_weight,
            tokens_of,
            scale,
            part,
            half,
            sub,
        )

    zero = jnp.zeros((), jnp.int32)
    if gathered:
        every = ("dp", "row")
        all_scales = gather_planes(scale)
        all_second = gather_planes(second)
        all_hidden = lax.all_gather(hidden_delta, every, axis=0, tiled=True)
        all_tokens_of, _, all_offsets = places(all_keys)
        segment_count = all_offsets.shape[0]
        sources = [turned(all_second), turned(all_delta)]
        shares[-1], all_hidden, all_scales, *sources = in_order(
            shares[-1], all_hidden, all_scales, *sources
        )
        second_turned, delta_turned = dispatch_turned(all_tokens_of, all_scales, *sources)
        hidden_rows = all_hidden.reshape(segment_count, rows, units)
        base = lax.axis_index("dp") * groups
        last = lax.all_gather(shares[-1], "row", axis=0, tiled=True)
        shares[0], last = in_order(shares[0], last)
        last = last.reshape(groups, rows, 2 * half)
        back = back_of(parts - 1, [(last, 0), (last, 1)], zero, hidden_rows, base)
        pairs, bases, all_pairs = [], [], []
        for part in range(parts):
            taken = lax.all_gather(shares[part], every, axis=0, tiled=True)
            if part + 1 < parts:
                shares[part + 1], taken, back, second_turned, delta_turned = in_order(
                    shares[part + 1], taken, back, second_turned, delta_turned
                )
                whole = taken.reshape(segment_count, rows, 2 * half)
                pairs.append([(whole, 0), (whole, 1)])
                bases.append(base)
                back = back + back_of(part, pairs[part], base, hidden_rows, base)
            all_pairs.append([taken.reshape(segment_count, 1, rows, 2 * half)])
        pairs.append([(last, 0), (last, 1)])
        bases.append(zero)
    else:
        all_tokens_of, all_offsets, all_scales = tokens_of, offsets, scale
        segment_count = groups
        all_second = second
        hidden_rows = lax.all_gather(hidden_delta, "row", axis=0, tiled=True).reshape(
            groups, rows, units
        )
        wholes = [
            lax.all_gather(share, "row", axis=0, tiled=True).reshape(groups, rows, 2 * half)
            for share in shares
        ]
        pairs = [[(value, 0), (value, 1)] for value in wholes]
        all_pairs = [[value[:, None]] for value in wholes]
        second_turned, delta_turned = dispatch_turned(
            all_tokens_of, all_scales, turned(all_second), turned(all_delta)
        )
        bases = [zero] * parts
        back = sum(back_of(part, pairs[part], zero, hidden_rows, zero) for part in range(parts))
    bases = jnp.stack(bases)
    back = back.reshape(tokens, width_part + TILE)

    def gradients_of(part, start, count, before):
        return expert_gradients(
            all_offsets,
            all_pairs[part],
            hidden_rows,
            second_turned,
            delta_turned,
            part,
            start,
            count,
            before,
        )

    picked_delta = (
        back[:, width_part : width_part + experts]
        + back[:, width_part + experts : width_part + 2 * experts]
    )
    logits_delta = (
        picked_delta - router_probs * jnp.sum(picked_delta, axis=1, keepdims=True)
    ).astype(BF)
    second_delta = add_columns(
        (back[:, :width_part] + dot_nt(logits_delta, router_weight)).astype(BF)
    )
    router_part = exchange_columns(dot_tn(logits_delta, second))

    out_delta = delta_group.astype(F32)
    second_inner = total_rows(jnp.sum(second_delta * second_scale * middle, axis=1))
    middle_delta = (
        out_delta
        + second_inverse[:, None] * second_scale * second_delta
        - middle * (second_inverse**3 * second_inner / model_width)[:, None]
    )
    second_gain_part = jnp.sum(second_delta * middle * second_inverse[:, None], axis=0)
    attention_round = middle_delta.astype(BF)
    expert_out = expert_down(offsets, bases, pairs, half, down_weight, tokens_of, scale, sub)
    some = experts // 2 if parts > 1 else 0
    gradients = gradients_of(0, 0, some, ()) if some else ()
    attention_round, expert_out, all_pairs[-1][0], gradients = in_order(
        attention_round, expert_out, all_pairs[-1][0], gradients
    )
    output_gradient = jnp.einsum(
        "srth,std->rhd",
        mixed_group.reshape(spans, slots, span, own_part),
        attention_round.reshape(spans, span, width_part),
        preferred_element_type=F32,
    ).reshape(head_part, width_part)
    early_gradient = jnp.concatenate([output_gradient, router_part], axis=0).astype(BF)


    mixed_delta = scatter_rows(output_back(attention_round, output_weight, spans, slots))
    query_delta, key_delta, value_delta = attend_back(
        query_round, key_round, value_round, mixed_delta, logs, own_segments, length
    )
    inner_sums = total_heads(
        query_delta * query_scale * query_raw, key_delta * key_scale * key_raw
    )
    query_raw_delta = (
        query_inverse[:, None] * query_scale * query_delta
        - query_raw * (query_inverse**3 * inner_sums[0] / model_width)[:, None]
    )
    key_raw_delta = (
        key_inverse[:, None] * key_scale * key_delta
        - key_raw * (key_inverse**3 * inner_sums[1] / model_width)[:, None]
    )
    query_gain_part = jnp.sum(query_delta * query_raw * query_inverse[:, None], axis=0)
    key_gain_part = jnp.sum(key_delta * key_raw * key_inverse[:, None], axis=0)
    joint_delta = jnp.concatenate([query_raw_delta, key_raw_delta, value_delta], axis=1).astype(BF)
    joint_group = lax.all_gather(joint_delta, "row", axis=0, tiled=False)
    first_delta = share_columns(
        project_back(joint_group, query_weight, key_weight, value_weight, spans, slots)
    )
    if some:
        gradients = gradients_of(0, some, experts - some, gradients)
        joint_group, gradients = in_order(joint_group, gradients)
    joint_gradients = project_gradient(normed.T, joint_group, spans, slots)

    own_residual = residual_in.astype(F32)
    own_inverse = lax.dynamic_slice_in_dim(first_inverse, own_tokens, local_tokens, 0)
    first_inner = total_rows(jnp.sum(first_delta * first_scale * own_residual, axis=1))
    input_gradient = (
        lax.dynamic_slice_in_dim(middle_delta, own_tokens, local_tokens, 0)
        + own_inverse[:, None] * first_scale * first_delta
        - own_residual * (own_inverse**3 * first_inner / model_width)[:, None]
    )
    first_gain_part = jnp.sum(first_delta * own_residual * own_inverse[:, None], axis=0)

    expert_out = share_columns(expert_out.reshape(tokens, width_part).astype(BF))
    residual_out = (
        lax.dynamic_slice_in_dim(middle, own_tokens, local_tokens, 0) + expert_out
    ).astype(BF)

    *joint_gradients, early_gradient, gradients = in_order(
        *joint_gradients, early_gradient, gradients
    )
    *head_gradients, early_gradient = [
        lax.psum(value, "dp") for value in (*joint_gradients, early_gradient)
    ]
    early_gradient = early_gradient.astype(F32)
    query_gradient, key_gradient, value_gradient = [value.astype(F32) for value in head_gradients]
    output_gradient = early_gradient[:head_part]
    router_gradient = early_gradient[head_part:].T
    gains = jnp.concatenate(
        [exchange_columns(first_gain_part), second_gain_part, query_gain_part, key_gain_part]
    )
    gains = exchange(gains, "dp")
    head_gains = lax.all_gather(
        gains[2 * width_part :].reshape(2, own_part), "row", axis=1, tiled=True
    )
    head_gains = jnp.sum(head_gains.reshape(2, spans, head_part), axis=1)
    if not some:
        gradients = ()
    gradients, input_gradient, residual_out, gains, head_gains = in_order(
        gradients, input_gradient, residual_out, gains, head_gains
    )
    gradients = gradients_of(parts - 1, 0, experts, gradients)
    if not gathered:
        gradients = [lax.psum(value.astype(BF), "dp").astype(F32) for value in gradients]
    gate_gradient, up_gradient, down_gradient = gradients

    return (
        residual_out,
        input_gradient,
        gains[:width_part],
        query_gradient,
        key_gradient,
        value_gradient,
        head_gains[0],
        head_gains[1],
        output_gradient,
        gains[width_part : 2 * width_part],
        router_gradient,
        gate_gradient,
        up_gradient,
        down_gradient,
    )


def solution(mesh):
    tokens, routed = P(("dp", "col"), "row"), P(None, "row", "col")
    heads, gain = P("row", "col"), P("row")
    down, back = P(None, "col", "row"), P("col", "row")
    return jax.shard_map(
        on_device,
        mesh=mesh,
        in_specs=(
            tokens,
            gain,
            heads,
            heads,
            heads,
            P("col"),
            P("col"),
            back,
            gain,
            P("row", None),
            routed,
            routed,
            down,
            P("dp"),
            P("dp", None),
            tokens,
        ),
        out_specs=(
            tokens,
            tokens,
            gain,
            heads,
            heads,
            heads,
            P("col"),
            P("col"),
            back,
            gain,
            P("row", None),
            routed,
            routed,
            down,
        ),
        check_vma=False,
    )
```

```python
import functools

import jax
import jax.numpy as jnp
from jax import lax
from jax.experimental import pallas as pl
from jax.experimental.pallas import tpu as pltpu
from jax.sharding import PartitionSpec as P

HEAD_DIM = 128
MAX_LEN = 2048
EPSILON = 1e-05
NEGATIVE = -1e30

TILE = 128
WIDE = 512
SUB = 1024
PACK = 4
BAND = 4
RING = 8
MEGA = 1 << 20
BF = jnp.bfloat16
F32 = jnp.float32


def dot(left, right):
    return jnp.dot(left, right, preferred_element_type=F32)


def dot_nt(left, right):
    return lax.dot_general(left, right, (((1,), (1,)), ((), ())), preferred_element_type=F32)


def dot_tn(left, right):
    return lax.dot_general(left, right, (((0,), (0,)), ((), ())), preferred_element_type=F32)


def iota(shape, axis):
    return lax.broadcasted_iota(jnp.int32, shape, axis)


def params(mebibytes):
    return pltpu.CompilerParams(vmem_limit_bytes=mebibytes * MEGA)


def cost(flops, nbytes):
    return pl.CostEstimate(
        flops=int(flops) // 64, bytes_accessed=int(nbytes) // 64, transcendentals=0
    )


def once(shape, index):
    return pl.BlockSpec(shape, index, pipeline_mode=pl.Buffered(buffer_count=1))


def project_kernel(x_ref, q_ref, k_ref, v_ref, o_ref):
    width = q_ref.shape[1]
    x = x_ref[...]
    o_ref[0, :, :width] = dot(x, q_ref[...]).astype(BF)
    o_ref[0, :, width : 2 * width] = dot(x, k_ref[...]).astype(BF)
    o_ref[0, :, 2 * width :] = dot(x, v_ref[...]).astype(BF)


def project(x, query, key, value, spans, slots):
    tokens, depth = x.shape
    width, span = query.shape[1] // slots, tokens // spans
    weight = pl.BlockSpec((depth, width), lambda s, h: (0, h))
    return pl.pallas_call(
        project_kernel,
        grid=(spans, slots),
        in_specs=[pl.BlockSpec((span, depth), lambda s, h: (s, 0)), weight, weight, weight],
        out_specs=pl.BlockSpec((1, span, 3 * width), lambda s, h: (s * slots + h, 0, 0)),
        out_shape=jax.ShapeDtypeStruct((spans * slots, span, 3 * width), BF),
        compiler_params=params(48),
        cost_estimate=cost(6 * tokens * depth * width * slots, 6 * tokens * width * slots),
        name="project",
    )(x, query, key, value)


def project_back_kernel(d_ref, q_ref, k_ref, v_ref, o_ref, acc):
    slot = pl.program_id(1)
    width = q_ref.shape[1]

    @pl.when(slot == 0)
    def _():
        acc[...] = jnp.zeros_like(acc)

    acc[...] += (
        dot_nt(d_ref[0, :, :width], q_ref[...])
        + dot_nt(d_ref[0, :, width : 2 * width], k_ref[...])
        + dot_nt(d_ref[0, :, 2 * width :], v_ref[...])
    )

    @pl.when(slot == pl.num_programs(1) - 1)
    def _():
        o_ref[...] = acc[...].astype(BF)


def project_back(delta, query, key, value, spans, slots):
    _, span, joint = delta.shape
    depth, width = query.shape[0], joint // 3
    weight = pl.BlockSpec((depth, width), lambda s, h: (0, h))
    return pl.pallas_call(
        project_back_kernel,
        grid=(spans, slots),
        in_specs=[
            pl.BlockSpec((1, span, joint), lambda s, h: (s * slots + h, 0, 0)),
            weight,
            weight,
            weight,
        ],
        out_specs=pl.BlockSpec((span, depth), lambda s, h: (s, 0)),
        out_shape=jax.ShapeDtypeStruct((spans * span, depth), BF),
        scratch_shapes=[pltpu.VMEM((span, depth), F32)],
        compiler_params=params(48),
        cost_estimate=cost(2 * spans * span * depth * joint * slots, 2 * spans * span * joint * slots),
        name="project_back",
    )(delta, query, key, value)


def project_gradient_kernel(x_ref, d_ref, q_ref, k_ref, v_ref, acc):
    span = pl.program_id(1)
    made = dot(x_ref[...], d_ref[0])

    @pl.when(span == 0)
    def _():
        acc[...] = made

    @pl.when(span > 0)
    def _():
        acc[...] += made

    @pl.when(span == pl.num_programs(1) - 1)
    def _():
        width = q_ref.shape[1]
        q_ref[...] = acc[:, :width].astype(BF)
        k_ref[...] = acc[:, width : 2 * width].astype(BF)
        v_ref[...] = acc[:, 2 * width :].astype(BF)


def project_gradient(turned, delta, spans, slots):
    depth, tokens = turned.shape
    _, span, joint = delta.shape
    width = joint // 3
    out = pl.BlockSpec((depth, width), lambda h, s: (0, h))
    return pl.pallas_call(
        project_gradient_kernel,
        grid=(slots, spans),
        in_specs=[
            pl.BlockSpec((depth, span), lambda h, s: (0, s)),
            pl.BlockSpec((1, span, joint), lambda h, s: (s * slots + h, 0, 0)),
        ],
        out_specs=[out, out, out],
        out_shape=[jax.ShapeDtypeStruct((depth, width * slots), BF)] * 3,
        scratch_shapes=[pltpu.VMEM((depth, joint), F32)],
        compiler_params=params(48),
        cost_estimate=cost(2 * tokens * depth * joint * slots, 2 * tokens * joint * slots),
        name="project_gradient",
    )(turned, delta)


def output_kernel(m_ref, w_ref, o_ref, acc):
    slot = pl.program_id(1)

    @pl.when(slot == 0)
    def _():
        acc[...] = jnp.zeros_like(acc)

    acc[...] += dot(m_ref[0], w_ref[...])

    @pl.when(slot == pl.num_programs(1) - 1)
    def _():
        o_ref[...] = acc[...].astype(BF)


def output_project(mixed, weight, spans, slots):
    _, span, width = mixed.shape
    depth = weight.shape[1]
    return pl.pallas_call(
        output_kernel,
        grid=(spans, slots),
        in_specs=[
            pl.BlockSpec((1, span, width), lambda s, h: (s * slots + h, 0, 0)),
            pl.BlockSpec((width, depth), lambda s, h: (h, 0)),
        ],
        out_specs=pl.BlockSpec((span, depth), lambda s, h: (s, 0)),
        out_shape=jax.ShapeDtypeStruct((spans * span, depth), BF),
        scratch_shapes=[pltpu.VMEM((span, depth), F32)],
        compiler_params=params(48),
        cost_estimate=cost(2 * spans * span * depth * width * slots, 2 * spans * span * width * slots),
        name="output_project",
    )(mixed, weight)


def output_back_kernel(d_ref, w_ref, o_ref):
    o_ref[0] = dot_nt(d_ref[...], w_ref[...]).astype(BF)


def output_back(delta, weight, spans, slots):
    tokens, depth = delta.shape
    width, span = weight.shape[0] // slots, tokens // spans
    return pl.pallas_call(
        output_back_kernel,
        grid=(spans, slots),
        in_specs=[
            pl.BlockSpec((span, depth), lambda s, h: (s, 0)),
            pl.BlockSpec((width, depth), lambda s, h: (h, 0)),
        ],
        out_specs=pl.BlockSpec((1, span, width), lambda s, h: (s * slots + h, 0, 0)),
        out_shape=jax.ShapeDtypeStruct((spans * slots, span, width), BF),
        compiler_params=params(48),
        cost_estimate=cost(2 * tokens * depth * width * slots, 2 * tokens * width * slots),
        name="output_back",
    )(delta, weight)


def allowed_pairs(column_ref, row_ref, start, block, reach):
    marks = column_ref[start : start + block, :] == row_ref[0, :, :reach]
    places = iota((block, reach), 1) <= iota((block, reach), 0) + start
    return marks & places


def attend_kernel(q_ref, k_ref, v_ref, column_ref, row_ref, o_ref, log_ref):
    length = q_ref.shape[0]
    block = min(256, length)
    for start in range(0, length, block):
        reach = start + block
        scores = dot_nt(q_ref[start:reach, :], k_ref[:reach, :]) * HEAD_DIM**-0.5
        scores = jnp.where(
            allowed_pairs(column_ref, row_ref, start, block, reach), scores, NEGATIVE
        )
        largest = jnp.max(scores, axis=1, keepdims=True)
        raised = jnp.exp(scores - largest)
        summed = jnp.sum(raised, axis=1, keepdims=True)
        weights = (raised * (1.0 / summed)).astype(BF)
        o_ref[start:reach, :] = dot(weights, v_ref[:reach, :]).astype(BF)
        log_ref[0, start:reach, :] = largest + jnp.log(summed)


def attend(query, key, value, marks, length):
    tokens, width = query.shape
    heads, count = width // HEAD_DIM, tokens // length
    rows = pl.BlockSpec((length, HEAD_DIM), lambda b, h: (b, h))
    return pl.pallas_call(
        attend_kernel,
        grid=(count, heads),
        in_specs=[
            rows,
            rows,
            rows,
            pl.BlockSpec((length, 1), lambda b, h: (b, 0)),
            pl.BlockSpec((1, 1, length), lambda b, h: (b, 0, 0)),
        ],
        out_specs=[rows, pl.BlockSpec((1, length, 1), lambda b, h: (h, b, 0))],
        out_shape=[
            jax.ShapeDtypeStruct((tokens, width), BF),
            jax.ShapeDtypeStruct((heads, tokens, 1), F32),
        ],
        compiler_params=params(48),
        cost_estimate=cost(4 * tokens * length * width, 8 * tokens * width),
        name="attend",
    )(query, key, value, marks.reshape(tokens, 1), marks.reshape(count, 1, length))


def attend_back_kernel(
    q_ref, k_ref, v_ref, d_ref, log_ref, column_ref, row_ref, dq_ref, dk_ref, dv_ref
):
    length = q_ref.shape[0]
    block = min(256, length)
    scale = HEAD_DIM**-0.5
    for start in reversed(range(0, length, block)):
        reach = start + block
        query, delta = q_ref[start:reach, :], d_ref[start:reach, :]
        key, value = k_ref[:reach, :], v_ref[:reach, :]
        scores = dot_nt(query, key) * scale
        allowed = allowed_pairs(column_ref, row_ref, start, block, reach)
        probs = jnp.where(allowed, jnp.exp(scores - log_ref[0, start:reach, :]), 0.0)
        weights_delta = dot_nt(delta, value)
        centre = jnp.sum(probs * weights_delta, axis=1, keepdims=True)
        score_delta = (probs * (weights_delta - centre)).astype(BF)
        dq_ref[start:reach, :] = dot(score_delta, key) * scale
        key_delta = dot_tn(score_delta, query) * scale
        value_delta = dot_tn(probs.astype(BF), delta)
        if reach == length:
            dk_ref[...] = key_delta
            dv_ref[...] = value_delta
        else:
            dk_ref[:reach, :] += key_delta
            dv_ref[:reach, :] += value_delta


def attend_back(query, key, value, delta, logs, marks, length):
    tokens, width = query.shape
    heads, count = width // HEAD_DIM, tokens // length
    rows = pl.BlockSpec((length, HEAD_DIM), lambda b, h: (b, h))
    return pl.pallas_call(
        attend_back_kernel,
        grid=(count, heads),
        in_specs=[
            rows,
            rows,
            rows,
            rows,
            pl.BlockSpec((1, length, 1), lambda b, h: (h, b, 0)),
            pl.BlockSpec((length, 1), lambda b, h: (b, 0)),
            pl.BlockSpec((1, 1, length), lambda b, h: (b, 0, 0)),
        ],
        out_specs=[rows, rows, rows],
        out_shape=[jax.ShapeDtypeStruct((tokens, width), F32)] * 3,
        compiler_params=params(48),
        cost_estimate=cost(10 * tokens * length * width, 20 * tokens * width),
        name="attend_back",
    )(query, key, value, delta, logs, marks.reshape(tokens, 1), marks.reshape(count, 1, length))


def dispatch_kernel(token_ref, source_ref, o_ref):
    tokens = source_ref.shape[1]
    bands = []
    for i in range(WIDE // TILE):
        ids = jnp.broadcast_to(token_ref[0, 0, i : i + 1, :], (TILE, TILE)).T
        bands.append(
            jnp.concatenate(
                [
                    jnp.where(ids == iota((TILE, TILE), 1) + j, 1.0, 0.0).astype(BF)
                    for j in range(0, tokens, TILE)
                ],
                axis=1,
            )
        )
    o_ref[0] = dot(jnp.concatenate(bands, axis=0), source_ref[0]).astype(BF)


def dispatch(tokens_of, source):
    groups, rows = tokens_of.shape
    _, tokens, depth = source.shape
    return pl.pallas_call(
        dispatch_kernel,
        grid=(groups, rows // WIDE),
        in_specs=[
            pl.BlockSpec((1, 1, WIDE // TILE, TILE), lambda g, i: (g, i, 0, 0)),
            pl.BlockSpec((1, tokens, depth), lambda g, i: (g, 0, 0)),
        ],
        out_specs=pl.BlockSpec((1, WIDE, depth), lambda g, i: (g, i, 0)),
        out_shape=jax.ShapeDtypeStruct((groups, rows, depth), BF),
        compiler_params=params(48),
        cost_estimate=cost(2 * groups * rows * tokens * depth, 2 * groups * rows * depth),
        name="dispatch",
    )(tokens_of.reshape(groups, rows // WIDE, WIDE // TILE, TILE), source)


def dispatch_turned_kernel(token_ref, scale_ref, first_ref, second_ref, a_ref, b_ref):
    tokens = first_ref.shape[2]
    chosen = jnp.where(iota((tokens, WIDE), 0) == token_ref[0, 0], 1.0, 0.0).astype(BF)
    scale = scale_ref[0, 0]
    for source, out in ((first_ref, a_ref), (second_ref, b_ref)):
        rows = (dot(source[0], chosen) * scale).astype(BF)
        for i in range(WIDE // TILE):
            out[0, i] = rows[:, i * TILE : (i + 1) * TILE]


def dispatch_turned(tokens_of, scale, first, second):
    groups, rows = tokens_of.shape
    _, depth, tokens = first.shape
    line = pl.BlockSpec((1, 1, 1, WIDE), lambda g, i: (g, i, 0, 0))
    source = pl.BlockSpec((1, depth, tokens), lambda g, i: (g, 0, 0))
    out = pl.BlockSpec((1, WIDE // TILE, depth, TILE), lambda g, i: (g, i, 0, 0))
    return pl.pallas_call(
        dispatch_turned_kernel,
        grid=(groups, rows // WIDE),
        in_specs=[line, line, source, source],
        out_specs=[out, out],
        out_shape=[jax.ShapeDtypeStruct((groups, rows // TILE, depth, TILE), BF)] * 2,
        compiler_params=params(48),
        cost_estimate=cost(4 * groups * rows * tokens * depth, 4 * groups * rows * depth),
        name="dispatch_turned",
    )(
        tokens_of.reshape(groups, rows // WIDE, 1, WIDE),
        scale.reshape(groups, rows // WIDE, 1, WIDE),
        first,
        second,
    )


def pick_kernel(token_ref, expert_ref, probs_ref, o_ref):
    experts, tokens = probs_ref.shape[1], probs_ref.shape[2]
    left, parts = probs_ref[0], []
    for _ in range(3):
        part = left.astype(BF)
        parts.append(part)
        left = left - part.astype(F32)
    chosen = jnp.where(iota((tokens, WIDE), 0) == token_ref[0, 0], 1.0, 0.0).astype(BF)
    found = dot(parts[0], chosen) + dot(parts[1], chosen) + dot(parts[2], chosen)
    match = iota((experts, WIDE), 0) == expert_ref[0, 0]
    o_ref[0, 0] = jnp.sum(jnp.where(match, found, 0.0), axis=0, keepdims=True)


def pick(tokens_of, experts_of, probs):
    groups, rows = tokens_of.shape
    _, experts, tokens = probs.shape
    line = pl.BlockSpec((1, 1, 1, WIDE), lambda g, i: (g, i, 0, 0))
    shape = (groups, rows // WIDE, 1, WIDE)
    return pl.pallas_call(
        pick_kernel,
        grid=(groups, rows // WIDE),
        in_specs=[line, line, pl.BlockSpec((1, experts, tokens), lambda g, i: (g, 0, 0))],
        out_specs=line,
        out_shape=jax.ShapeDtypeStruct(shape, F32),
        compiler_params=params(48),
        cost_estimate=cost(6 * groups * rows * tokens * experts, 8 * groups * rows),
        name="pick",
    )(tokens_of.reshape(shape), experts_of.reshape(shape), probs).reshape(groups, rows)


def each_expert(offset_ref, total, run):
    group, step = pl.program_id(0), pl.program_id(1)
    spans = []
    for i in range(PACK):
        expert = step * PACK + i
        low, high = offset_ref[group, expert], offset_ref[group, expert + 1]
        spans.append((expert, low, high, low // TILE * TILE))
    rounds = 0
    for _, low, high, first in spans:
        rounds = jnp.maximum(rounds, jnp.where(high > low, (high - first + WIDE - 1) // WIDE, 0))

    def turn(j, carry):
        for i, (expert, low, high, first) in enumerate(spans):
            base = pl.multiple_of(jnp.minimum(first + j * WIDE, total - WIDE), TILE)
            run(i, expert, base, low, high)
        return carry

    lax.fori_loop(0, rounds, turn, 0)


def kept(base, rows, low, high):
    places = base + iota((rows, 1), 0)
    return (places >= low) & (places < high)


def gate_up_kernel(offset_ref, x_ref, gate_ref, up_ref, o_ref):
    half = gate_ref.shape[2]

    def run(i, expert, base, low, high):
        rows = pl.ds(base, WIDE)
        keep = kept(base, WIDE, low, high)
        x = x_ref[0, rows, :]
        for start, weight in ((0, gate_ref), (half, up_ref)):
            columns = slice(start, start + half)
            made = dot(x, weight[i]).astype(BF)
            o_ref[0, rows, columns] = jnp.where(keep, made, o_ref[0, rows, columns])

    each_expert(offset_ref, x_ref.shape[1], run)


def gate_up(offsets, x, gate, up, part, half):
    groups, rows, depth = x.shape
    experts = gate.shape[0]
    weight = pl.BlockSpec((PACK, depth, half), lambda g, e, o: (e, 0, part))
    return pl.pallas_call(
        gate_up_kernel,
        grid_spec=pltpu.PrefetchScalarGridSpec(
            num_scalar_prefetch=1,
            grid=(groups, experts // PACK),
            in_specs=[once((1, rows, depth), lambda g, e, o: (g, 0, 0)), weight, weight],
            out_specs=once((1, rows, 2 * half), lambda g, e, o: (g, 0, 0)),
        ),
        out_shape=jax.ShapeDtypeStruct((groups, rows, 2 * half), BF),
        compiler_params=params(56),
        cost_estimate=cost(6 * groups * rows * depth * half, 2 * groups * rows * depth),
        name="gate_up",
    )(offsets, x, gate, up)


def hidden_back_kernel(offset_ref, x_ref, down_ref, o_ref):
    def run(i, expert, base, low, high):
        rows = pl.ds(base, WIDE)
        made = dot_nt(x_ref[0, rows, :], down_ref[i]).astype(BF)
        keep = kept(base, WIDE, low, high)
        o_ref[0, rows, :] = jnp.where(keep, made, o_ref[0, rows, :])

    each_expert(offset_ref, x_ref.shape[1], run)


def hidden_back(offsets, x, down):
    groups, rows, depth = x.shape
    experts, units, _ = down.shape
    return pl.pallas_call(
        hidden_back_kernel,
        grid_spec=pltpu.PrefetchScalarGridSpec(
            num_scalar_prefetch=1,
            grid=(groups, experts // PACK),
            in_specs=[
                once((1, rows, depth), lambda g, e, o: (g, 0, 0)),
                pl.BlockSpec((PACK, units, depth), lambda g, e, o: (e, 0, 0)),
            ],
            out_specs=once((1, rows, units), lambda g, e, o: (g, 0, 0)),
        ),
        out_shape=jax.ShapeDtypeStruct((groups, rows, units), BF),
        compiler_params=params(56),
        cost_estimate=cost(3 * groups * rows * depth * units, 2 * groups * rows * depth),
        name="hidden_back",
    )(offsets, x, down)


def slopes(gate):
    gate = 0.5 * gate.astype(F32)
    turned = jnp.tanh(gate)
    product = gate * turned
    return gate + product, (0.5 + 0.5 * turned) * ((1.0 + gate) - product)


def combine(token_ref, scale_ref, rows_ref, o_ref, before_ref=None):
    tokens = o_ref.shape[1]
    o_ref[0] = jnp.zeros(o_ref.shape[1:], F32) if before_ref is None else before_ref[0]

    def step(i, carry):
        chosen = iota((tokens, WIDE), 0) == token_ref[0, i]
        chosen = jnp.where(chosen, scale_ref[0, i], 0.0).astype(BF)
        o_ref[0] += dot(chosen, rows_ref[pl.ds(pl.multiple_of(i * WIDE, WIDE), WIDE), :])
        return carry

    lax.fori_loop(0, rows_ref.shape[0] // WIDE, step, 0)


def expert_back_kernel(
    part, offset_ref, _, g_ref, u_ref, hd_ref, gate_ref, up_ref, token_ref, scale_ref, *rest
):
    *before_ref, o_ref, made_ref = rest
    experts = PACK * pl.num_programs(1)
    depth, half = gate_ref.shape[1], gate_ref.shape[2]

    def run(i, expert, base, low, high):
        rows = pl.ds(base, WIDE)
        keep = kept(base, WIDE, low, high)
        silu, slope = slopes(g_ref[0, rows, :])
        delta = hd_ref[0, rows, part * half : (part + 1) * half]
        through = delta * u_ref[0, rows, :]
        picked = through.astype(F32) * silu
        made = dot_nt(through * slope.astype(BF), gate_ref[i])
        made += dot_nt(delta * silu.astype(BF), up_ref[i])
        made_ref[rows, :depth] = jnp.where(keep, made.astype(BF), made_ref[rows, :depth])
        picked = jnp.sum(picked, axis=1, keepdims=True)
        upper = picked.astype(BF).astype(F32)
        lane = iota((WIDE, TILE), 1)
        spread = jnp.where(
            lane == expert, upper, jnp.where(lane == expert + experts, picked - upper, 0.0)
        )
        made_ref[rows, depth:] = jnp.where(keep, spread.astype(BF), made_ref[rows, depth:])

    each_expert(offset_ref, made_ref.shape[0], run)

    @pl.when(pl.program_id(1) == pl.num_programs(1) - 1)
    def _():
        combine(token_ref, scale_ref, made_ref, o_ref, *before_ref)


def expert_back(offsets, base, pair, hd, gate, up, tokens_of, scale, part, half, tokens, before):
    groups, rows = tokens_of.shape
    units = hd.shape[2]
    experts, depth = gate.shape[:2]
    weight = pl.BlockSpec((PACK, depth, half), lambda g, e, o, b: (e, 0, part))
    line = once((1, rows // WIDE, 1, WIDE), lambda g, e, o, b: (g, 0, 0, 0))
    shape = (groups, rows // WIDE, 1, WIDE)
    total = once((1, tokens, depth + TILE), lambda g, e, o, b: (g, 0, 0))
    return pl.pallas_call(
        functools.partial(expert_back_kernel, part),
        grid_spec=pltpu.PrefetchScalarGridSpec(
            num_scalar_prefetch=2,
            grid=(groups, experts // PACK),
            in_specs=[
                *[
                    once((1, rows, half), lambda g, e, o, b, c=column: (b[0] + g, 0, c))
                    for _, column in pair
                ],
                once((1, rows, units), lambda g, e, o, b: (b[1] + g, 0, 0)),
                weight,
                weight,
                line,
                line,
                *[total] * len(before),
            ],
            out_specs=total,
            scratch_shapes=[pltpu.VMEM((rows, depth + TILE), BF)],
        ),
        out_shape=jax.ShapeDtypeStruct((groups, tokens, depth + TILE), F32),
        compiler_params=params(56),
        cost_estimate=cost(
            groups * rows * depth * (6 * half + 2 * tokens), 2 * groups * rows * (2 * half + units)
        ),
        name="expert_back",
    )(offsets, base, pair[0][0], pair[1][0], hd, gate, up, tokens_of.reshape(shape), scale.reshape(shape), *before)


def down_kernel(offset_ref, base_ref, down_ref, token_ref, scale_ref, *rest):
    sources, (o_ref, made_ref) = rest[:-2], rest[-2:]
    half = sources[0].shape[2]

    def run(i, expert, base, low, high):
        rows = pl.ds(base, WIDE)
        keep = kept(base, WIDE, low, high)
        hidden = []
        for gate_ref, up_ref in zip(sources[::2], sources[1::2]):
            gate = 0.5 * gate_ref[0, rows, :].astype(F32)
            silu = gate + gate * jnp.tanh(gate)
            hidden.append((silu * up_ref[0, rows, :].astype(F32)).astype(BF))
        made = dot(jnp.concatenate(hidden, axis=1), down_ref[i])
        made_ref[rows, :] = jnp.where(keep, made.astype(BF), made_ref[rows, :])

    each_expert(offset_ref, made_ref.shape[0], run)

    @pl.when(pl.program_id(1) == pl.num_programs(1) - 1)
    def _():
        combine(token_ref, scale_ref, made_ref, o_ref)


def expert_down(offsets, bases, pairs, half, down, tokens_of, scale, tokens):
    groups, rows = tokens_of.shape
    experts, units, depth = down.shape
    line = once((1, rows // WIDE, 1, WIDE), lambda g, e, o, b: (g, 0, 0, 0))
    shape = (groups, rows // WIDE, 1, WIDE)

    def source(i, column):
        return once((1, rows, half), lambda g, e, o, b: (b[i] + g, 0, column))

    specs = [source(i, column) for i, pair in enumerate(pairs) for _, column in pair]
    sources = [value for pair in pairs for value, _ in pair]
    return pl.pallas_call(
        down_kernel,
        grid_spec=pltpu.PrefetchScalarGridSpec(
            num_scalar_prefetch=2,
            grid=(groups, experts // PACK),
            in_specs=[
                pl.BlockSpec((PACK, units, depth), lambda g, e, o, b: (e, 0, 0)),
                line,
                line,
                *specs,
            ],
            out_specs=once((1, tokens, depth), lambda g, e, o, b: (g, 0, 0)),
            scratch_shapes=[pltpu.VMEM((rows, depth), BF)],
        ),
        out_shape=jax.ShapeDtypeStruct((groups, tokens, depth), F32),
        compiler_params=params(56),
        cost_estimate=cost(
            groups * rows * depth * (3 * units + 2 * tokens), 4 * groups * rows * units
        ),
        name="expert_down",
    )(offsets, bases, down, tokens_of.reshape(shape), scale.reshape(shape), *sources)


def gradient_kernel(part, start, pieces, aliased, offset_ref, *rest):
    piece_refs, rest = rest[:pieces], rest[pieces:]
    hd_ref, xs_ref, xc_ref = rest[:3]
    rest = rest[3 + 3 * aliased :]
    gate_out, up_out, down_out = rest[:3]
    gu_ring, hd_ring, xs_ring, xc_ring, narrow, issued, waited, sems = rest[3:]
    segments, tiles = xs_ref.shape[:2]
    shares, run_tiles = piece_refs[0].shape[1:3]
    share_tiles = pieces * run_tiles
    half = gate_out.shape[2]
    expert = start + pl.program_id(0)
    stop = start + pl.num_programs(0)

    def copies(segment, tile):
        slot = lax.rem(tile, RING)
        units = pl.ds(part * half, half)
        return [
            pltpu.make_async_copy(
                hd_ref.at[segment, tile, :, units],
                hd_ring.at[segment, slot],
                sems.at[1, segment, slot],
            ),
            pltpu.make_async_copy(
                xs_ref.at[segment, tile], xs_ring.at[segment, slot], sems.at[2, segment, slot]
            ),
            pltpu.make_async_copy(
                xc_ref.at[segment, tile], xc_ring.at[segment, slot], sems.at[3, segment, slot]
            ),
        ]

    def piece_copy(piece, segment, tile):
        slot = lax.rem(tile, RING)
        share, place = tile // share_tiles, lax.rem(tile, run_tiles)
        return pltpu.make_async_copy(
            piece_refs[piece].at[segment, share, place],
            gu_ring.at[segment, slot],
            sems.at[0, segment, slot],
        )

    def start_until(segment, limit):
        def step(tile, carry):
            for copy in copies(segment, tile):
                copy.start()
            if pieces == 1:
                piece_copy(0, segment, tile).start()
            else:
                held = lax.rem(tile, share_tiles) // run_tiles
                for piece in range(pieces):
                    pl.when(held == piece)(
                        lambda piece=piece: piece_copy(piece, segment, tile).start()
                    )
            return carry

        lax.fori_loop(issued[segment], limit, step, 0)
        issued[segment] = jnp.maximum(issued[segment], limit)

    def wait_until(segment, limit):
        def step(tile, carry):
            for copy in copies(segment, tile):
                copy.wait()
            piece_copy(0, segment, tile).wait()
            return carry

        lax.fori_loop(waited[segment], limit, step, 0)
        waited[segment] = jnp.maximum(waited[segment], limit)

    bounds = [
        (offset_ref[i, start] // TILE, (offset_ref[i, stop] + TILE - 1) // TILE)
        for i in range(segments)
    ]

    @pl.when(expert == start)
    def _():
        for segment, (head, tail) in enumerate(bounds):
            issued[segment] = head
            waited[segment] = head
            start_until(segment, jnp.minimum(head + RING - 1, tail))
            wait_until(segment, jnp.minimum(head + 1, tail))

            @pl.when(tail <= head)
            def _():
                slot = lax.rem(head, RING)
                for ring in (gu_ring, hd_ring, xs_ring, xc_ring):
                    ring[segment, slot] = jnp.zeros(ring.shape[2:], BF)

    spans, rounds = [], 0
    for segment in range(segments):
        low, high = offset_ref[segment, expert], offset_ref[segment, expert + 1]
        first = low // TILE
        last = jnp.where(high > low, (high + TILE - 1) // TILE, first)
        spans.append((low, high, first, last))
        rounds = jnp.maximum(rounds, (last - first + BAND - 1) // BAND)

    def turn(i, carry, fresh=False):
        for segment, (low, high, first, last) in enumerate(spans):
            tile = jnp.minimum(first + BAND * i, last)
            start_until(segment, jnp.minimum(bounds[segment][1], tile + RING - 1))
            wait_until(segment, jnp.minimum(last, tile + BAND))
        for segment, (low, high, first, last) in enumerate(spans):
            if segment % 2 == 0:
                gates, ups, hidden, xs, xc = [], [], [], [], []
            for j in range(BAND):
                tile = first + BAND * i + j
                slot = lax.rem(jnp.maximum(jnp.minimum(tile, last - 1), bounds[segment][0]), RING)
                keep = kept(tile * TILE, TILE, low, high)
                silu, slope = slopes(gu_ring[segment, slot, :, :half])
                silu = jnp.where(keep, silu, 0.0).astype(BF)
                slope = jnp.where(keep, slope, 0.0).astype(BF)
                up, delta = gu_ring[segment, slot, :, half:], hd_ring[segment, slot]
                gates.append(delta * up * slope)
                ups.append(delta * silu)
                hidden.append(silu * up)
                xs.append(xs_ring[segment, slot])
                xc.append(xc_ring[segment, slot])
            if segment % 2 == 0 and segment + 1 < segments:
                continue
            left, right = jnp.concatenate(xs, axis=1), jnp.concatenate(xc, axis=1)
            made = [
                (gate_out, (0,), dot(left, jnp.concatenate(gates, axis=0))),
                (up_out, (0,), dot(left, jnp.concatenate(ups, axis=0))),
                (narrow, (), dot(right, jnp.concatenate(hidden, axis=0))),
            ]
            for out, place, value in made:
                if fresh and segment < 2:
                    out[(*place, ...)] = value
                else:
                    out[(*place, ...)] += value
        return carry

    turn(0, 0, fresh=True)
    lax.fori_loop(1, rounds, turn, 0)

    @pl.when(expert == stop - 1)
    def _():
        for segment in range(segments):
            wait_until(segment, issued[segment])

    down_out[0] = narrow[...].T


def expert_gradients(offsets, pieces, hd, xs, xc, part, start, count, before):
    segments, shares, run, pair = pieces[0].shape
    half, rows = pair // 2, hd.shape[1]
    tiles = rows // TILE
    units = hd.shape[2]
    depth = xs.shape[2]
    experts = offsets.shape[1] - 1
    anywhere = pl.BlockSpec(memory_space=pl.ANY)
    columns = pl.BlockSpec((1, depth, half), lambda e, o: (start + e, 0, part))
    before = list(before)
    return pl.pallas_call(
        functools.partial(gradient_kernel, part, start, len(pieces), int(bool(before))),
        grid_spec=pltpu.PrefetchScalarGridSpec(
            num_scalar_prefetch=1,
            grid=(count,),
            in_specs=[anywhere] * (len(pieces) + 3 + len(before)),
            out_specs=[
                columns,
                columns,
                pl.BlockSpec((1, half, depth), lambda e, o: (start + e, part, 0)),
            ],
            scratch_shapes=[
                pltpu.VMEM((segments, RING, TILE, pair), BF),
                pltpu.VMEM((segments, RING, TILE, half), BF),
                pltpu.VMEM((segments, RING, depth, TILE), BF),
                pltpu.VMEM((segments, RING, depth, TILE), BF),
                pltpu.VMEM((depth, half), F32),
                pltpu.SMEM((segments,), jnp.int32),
                pltpu.SMEM((segments,), jnp.int32),
                pltpu.SemaphoreType.DMA((4, segments, RING)),
            ],
        ),
        out_shape=[
            jax.ShapeDtypeStruct((experts, depth, units), F32),
            jax.ShapeDtypeStruct((experts, depth, units), F32),
            jax.ShapeDtypeStruct((experts, units, depth), F32),
        ],
        input_output_aliases={len(pieces) + 4 + i: i for i in range(len(before))},
        compiler_params=params(56),
        cost_estimate=cost(
            9 * segments * rows * depth * half, 2 * segments * rows * (3 * half + 2 * depth)
        ),
        name="expert_gradients",
    )(
        offsets,
        *[piece.reshape(segments, shares, run // TILE, TILE, pair) for piece in pieces],
        hd.reshape(segments, tiles, TILE, units),
        xs,
        xc,
        *before,
    )


def in_order(*values):
    return lax.optimization_barrier(values)


def total_rows(value):
    return lax.psum(value, "row")


def neighbour_sum(value, axis, apart):
    count = lax.axis_size(axis)
    return value + lax.ppermute(value, axis, [(i, i ^ apart) for i in range(count)])


def exchange(value, axis):
    count, apart = lax.axis_size(axis), 1
    while apart < count:
        value = value + lax.ppermute(value, axis, [(i, i ^ apart) for i in range(count)])
        apart *= 2
    return value


def scatter_rows(value):
    count = lax.axis_size("row")
    if count != 4:
        return lax.psum_scatter(value, "row", scatter_dimension=0, tiled=False)
    index = lax.axis_index("row")

    def halve(value, axis, mine, apart):
        sent = lax.dynamic_index_in_dim(value, 1 - mine, axis, False)
        kept = lax.dynamic_index_in_dim(value, mine, axis, False)
        other = lax.ppermute(sent, "row", [(i, i ^ apart) for i in range(count)])
        return (kept.astype(F32) + other.astype(F32)).astype(BF)

    value = halve(value.reshape(2, 2, *value.shape[1:]), 1, index % 2, 1)
    return halve(value, 0, index // 2, 2)


def gather_planes(value):
    count = lax.axis_size("dp")
    pieces = [value] + [
        lax.ppermute(value, "dp", [(i, (i - apart) % count) for i in range(count)])
        for apart in range(1, count)
    ]
    first = (count - lax.axis_index("dp")) % count * value.shape[0]
    return lax.dynamic_slice_in_dim(
        jnp.concatenate(pieces + pieces[:-1], axis=0), first, count * value.shape[0], 0
    )


def exchange_columns(value):
    if lax.axis_size("col") != 2:
        return lax.psum(value, "col")
    return value + lax.ppermute(value, "col", [(0, 1), (1, 0)])


def gather_columns(value):
    if lax.axis_size("col") != 2:
        return lax.all_gather(value, "col", axis=0, tiled=True)
    other = lax.ppermute(value, "col", [(0, 1), (1, 0)])
    first = lax.axis_index("col") == 0
    return jnp.concatenate(
        [jnp.where(first, value, other), jnp.where(first, other, value)], axis=0
    )


def add_columns(value):
    if lax.axis_size("col") != 2:
        return lax.psum(value, "col").astype(F32)
    other = lax.ppermute(value, "col", [(0, 1), (1, 0)])
    return value.astype(F32) + other.astype(F32)


def share_columns(value):
    count = lax.axis_size("col")
    if count != 2:
        return lax.psum_scatter(value, "col", scatter_dimension=0, tiled=True).astype(F32)
    index = lax.axis_index("col")
    halves = value.reshape(2, value.shape[0] // 2, value.shape[1])
    other = lax.ppermute(
        lax.dynamic_index_in_dim(halves, 1 - index, 0, False), "col", [(0, 1), (1, 0)]
    )
    return lax.dynamic_index_in_dim(halves, index, 0, False).astype(F32) + other.astype(F32)


def on_device(
    residual_in,
    attention_gain,
    query_weight,
    key_weight,
    value_weight,
    query_gain,
    key_gain,
    output_weight,
    expert_gain,
    router_weight,
    gate_weight,
    up_weight,
    down_weight,
    segments,
    routes,
    cotangent,
):
    row_count = lax.axis_size("row")
    row_index = lax.axis_index("row")
    column_count = lax.axis_size("col")
    column_index = lax.axis_index("col")
    local_tokens, width_part = residual_in.shape
    model_width = width_part * row_count
    tokens = local_tokens * column_count
    head_part = query_weight.shape[1]
    heads_here = head_part // HEAD_DIM
    slots = min(row_count, heads_here)
    spans = row_count // slots
    own_part = head_part // slots
    experts, _, units = gate_weight.shape
    parts = 2 if units % 256 == 0 else 1
    half = units // parts
    top_count = routes.shape[1]
    length = min(MAX_LEN, tokens)
    sub = min(SUB, tokens)
    groups = tokens // sub
    rows = sub * top_count

    keys = routes * sub + (jnp.arange(tokens, dtype=jnp.int32) % sub)[:, None]
    keys = lax.sort(keys.reshape(groups, rows), dimension=1)

    def places(keys):
        bounds = jnp.arange(experts + 1, dtype=jnp.int32) * sub
        below = keys[:, None, :] < bounds[None, :, None]
        return keys % sub, keys // sub, jnp.sum(below.astype(jnp.int32), axis=2)

    tokens_of, experts_of, offsets = places(keys)

    delta_group = gather_columns(cotangent)
    gathered = tokens <= 2 * SUB
    planes = ("dp", "col")
    all_delta, all_keys = delta_group, keys
    if gathered:
        all_delta = lax.all_gather(cotangent, planes, axis=0, tiled=True)
        all_keys = lax.all_gather(keys, "dp", axis=0, tiled=True)
    delta_rows = dispatch(tokens_of, delta_group.reshape(groups, sub, width_part))
    hidden_part = hidden_back(offsets, delta_rows, down_weight)

    residual = gather_columns(residual_in).astype(F32)
    first_scale = attention_gain.astype(F32)
    first_inverse = lax.rsqrt(
        total_rows(jnp.sum(residual * residual, axis=1)) / model_width + EPSILON
    )
    normed = (residual * first_inverse[:, None] * first_scale).astype(BF)
    joint = lax.psum_scatter(
        project(normed, query_weight, key_weight, value_weight, spans, slots),
        "row",
        scatter_dimension=0,
        tiled=False,
    )
    joint, hidden_part, all_keys = in_order(joint, hidden_part, all_keys)
    query_raw = joint[:, :own_part].astype(F32)
    key_raw = joint[:, own_part : 2 * own_part].astype(F32)
    value_round = joint[:, 2 * own_part :]
    span = tokens // spans
    span_start = row_index // slots * span

    def total_heads(first, second):
        sums = jnp.stack([jnp.sum(first, axis=1), jnp.sum(second, axis=1)])
        if spans > 1:
            sums = lax.dynamic_update_slice(
                jnp.zeros((2, tokens), F32), sums, (jnp.zeros((), jnp.int32), span_start)
            )
        sums = total_rows(exchange_columns(sums))
        return lax.dynamic_slice_in_dim(sums, span_start, span, 1) if spans > 1 else sums

    own_segments = lax.dynamic_slice_in_dim(segments, span_start, span, 0)
    square_sums = total_heads(query_raw * query_raw, key_raw * key_raw)
    query_inverse = lax.rsqrt(square_sums[0] / model_width + EPSILON)
    key_inverse = lax.rsqrt(square_sums[1] / model_width + EPSILON)
    own_start = (row_index % slots * own_part,)
    query_scale = lax.dynamic_slice(query_gain, own_start, (own_part,)).astype(F32)
    key_scale = lax.dynamic_slice(key_gain, own_start, (own_part,)).astype(F32)
    query_round = (query_raw * query_inverse[:, None] * query_scale).astype(BF)
    key_round = (key_raw * key_inverse[:, None] * key_scale).astype(BF)
    mixed, logs = attend(query_round, key_round, value_round, own_segments, length)
    mixed, all_delta = in_order(mixed, all_delta)
    mixed_group = lax.all_gather(mixed, "row", axis=0, tiled=False)
    hidden_delta = lax.psum_scatter(
        hidden_part.reshape(groups * rows, units),
        "row",
        scatter_dimension=0,
        tiled=True,
    )
    middle = residual + add_columns(output_project(mixed_group, output_weight, spans, slots))

    second_scale = expert_gain.astype(F32)
    second_inverse = lax.rsqrt(total_rows(jnp.sum(middle * middle, axis=1)) / model_width + EPSILON)
    second = (middle * second_inverse[:, None] * second_scale).astype(BF)
    logits = exchange(
        lax.dot_general(
            router_weight, second, (((0,), (1,)), ((), ())), preferred_element_type=F32
        ),
        "row",
    )
    turned_probs = jax.nn.softmax(logits, axis=0)
    router_probs = turned_probs.T
    second_rows = dispatch(tokens_of, second.reshape(groups, sub, width_part))
    scale = pick(
        tokens_of, experts_of, jnp.swapaxes(turned_probs.reshape(experts, groups, sub), 0, 1)
    )
    own_tokens = column_index * local_tokens
    shares, pairs = [], []
    for part in range(parts):
        made = gate_up(offsets, second_rows, gate_weight, up_weight, part, half)
        if part == 0:
            made, hidden_delta = in_order(made, hidden_delta)
        shares.append(
            lax.psum_scatter(
                made.reshape(groups * rows, 2 * half), "row", scatter_dimension=0, tiled=True
            )
        )
    def turned(value):
        return jnp.swapaxes(value.reshape(-1, sub, width_part), 1, 2)

    def back_of(part, pair, base, hidden_rows, hidden_base, before=()):
        return expert_back(
            offsets,
            jnp.stack([base, hidden_base]),
            pair,
            hidden_rows,
            gate_weight,
            up_weight,
            tokens_of,
            scale,
            part,
            half,
            sub,
            before,
        )

    zero = jnp.zeros((), jnp.int32)
    if gathered:
        every = ("dp", "row")
        all_scales = gather_planes(scale)
        all_second = gather_planes(second)
        all_hidden = lax.all_gather(hidden_delta, every, axis=0, tiled=True)
        all_tokens_of, _, all_offsets = places(all_keys)
        segment_count = all_offsets.shape[0]
        sources = [turned(all_second), turned(all_delta)]
        shares[-1], all_hidden, all_scales, *sources = in_order(
            shares[-1], all_hidden, all_scales, *sources
        )
        second_turned, delta_turned = dispatch_turned(all_tokens_of, all_scales, *sources)
        hidden_rows = all_hidden.reshape(segment_count, rows, units)
        base = lax.axis_index("dp") * groups
        last = lax.all_gather(shares[-1], "row", axis=0, tiled=True)
        shares[0], last = in_order(shares[0], last)
        last = last.reshape(groups, rows, 2 * half)
        back = back_of(parts - 1, [(last, 0), (last, 1)], zero, hidden_rows, base)
        pairs, bases, all_pairs = [], [], []
        for part in range(parts):
            taken = lax.all_gather(shares[part], every, axis=0, tiled=True)
            if part + 1 < parts:
                shares[part + 1], taken, back, second_turned, delta_turned = in_order(
                    shares[part + 1], taken, back, second_turned, delta_turned
                )
                whole = taken.reshape(segment_count, rows, 2 * half)
                pairs.append([(whole, 0), (whole, 1)])
                bases.append(base)
                back = back_of(part, pairs[part], base, hidden_rows, base, (back,))
            all_pairs.append([taken.reshape(segment_count, 1, rows, 2 * half)])
        pairs.append([(last, 0), (last, 1)])
        bases.append(zero)
    else:
        all_tokens_of, all_offsets, all_scales = tokens_of, offsets, scale
        segment_count = groups
        all_second = second
        hidden_rows = lax.all_gather(hidden_delta, "row", axis=0, tiled=True).reshape(
            groups, rows, units
        )
        wholes = [
            lax.all_gather(share, "row", axis=0, tiled=True).reshape(groups, rows, 2 * half)
            for share in shares
        ]
        pairs = [[(value, 0), (value, 1)] for value in wholes]
        all_pairs = [[value[:, None]] for value in wholes]
        second_turned, delta_turned = dispatch_turned(
            all_tokens_of, all_scales, turned(all_second), turned(all_delta)
        )
        bases = [zero] * parts
        back = sum(back_of(part, pairs[part], zero, hidden_rows, zero) for part in range(parts))
    bases = jnp.stack(bases)
    back = back.reshape(tokens, width_part + TILE)

    def gradients_of(part, start, count, before):
        return expert_gradients(
            all_offsets,
            all_pairs[part],
            hidden_rows,
            second_turned,
            delta_turned,
            part,
            start,
            count,
            before,
        )

    picked_delta = (
        back[:, width_part : width_part + experts]
        + back[:, width_part + experts : width_part + 2 * experts]
    )
    logits_delta = (
        picked_delta - router_probs * jnp.sum(picked_delta, axis=1, keepdims=True)
    ).astype(BF)
    second_delta = add_columns(
        (back[:, :width_part] + dot_nt(logits_delta, router_weight)).astype(BF)
    )
    router_part = exchange_columns(dot_tn(logits_delta, second))

    out_delta = delta_group.astype(F32)
    second_inner = total_rows(jnp.sum(second_delta * second_scale * middle, axis=1))
    middle_delta = (
        out_delta
        + second_inverse[:, None] * second_scale * second_delta
        - middle * (second_inverse**3 * second_inner / model_width)[:, None]
    )
    second_gain_part = jnp.sum(second_delta * middle * second_inverse[:, None], axis=0)
    attention_round = middle_delta.astype(BF)
    early = parts > 1
    gradients = gradients_of(0, 0, experts, ()) if early else ()
    attention_round, all_pairs[-1][0], gradients = in_order(
        attention_round, all_pairs[-1][0], gradients
    )
    output_gradient = jnp.einsum(
        "srth,std->rhd",
        mixed_group.reshape(spans, slots, span, own_part),
        attention_round.reshape(spans, span, width_part),
        preferred_element_type=F32,
    ).reshape(head_part, width_part)
    early_gradient = jnp.concatenate([output_gradient, router_part], axis=0).astype(BF)
    plane_count = lax.axis_size("dp")
    pairwise = early and plane_count == 4
    if pairwise:
        early_gradient = neighbour_sum(early_gradient, "dp", 1)


    mixed_delta = scatter_rows(output_back(attention_round, output_weight, spans, slots))
    query_delta, key_delta, value_delta = attend_back(
        query_round, key_round, value_round, mixed_delta, logs, own_segments, length
    )
    inner_sums = total_heads(
        query_delta * query_scale * query_raw, key_delta * key_scale * key_raw
    )
    query_raw_delta = (
        query_inverse[:, None] * query_scale * query_delta
        - query_raw * (query_inverse**3 * inner_sums[0] / model_width)[:, None]
    )
    key_raw_delta = (
        key_inverse[:, None] * key_scale * key_delta
        - key_raw * (key_inverse**3 * inner_sums[1] / model_width)[:, None]
    )
    query_gain_part = jnp.sum(query_delta * query_raw * query_inverse[:, None], axis=0)
    key_gain_part = jnp.sum(key_delta * key_raw * key_inverse[:, None], axis=0)
    joint_delta = jnp.concatenate([query_raw_delta, key_raw_delta, value_delta], axis=1).astype(BF)
    joint_delta, early_gradient = in_order(joint_delta, early_gradient)
    if pairwise:
        early_gradient = neighbour_sum(early_gradient, "dp", 2)
    else:
        early_gradient = lax.psum(early_gradient, "dp")
    joint_group = lax.all_gather(joint_delta, "row", axis=0, tiled=False)
    run = experts * 3 // 8
    gradients = gradients_of(parts - 1, 0, run, gradients)
    joint_group, gradients, early_gradient = in_order(joint_group, gradients, early_gradient)
    joint_gradients = project_gradient(normed.T, joint_group, spans, slots)
    *joint_gradients, joint_group = in_order(*joint_gradients, joint_group)
    head_gradients = [lax.psum(value, "dp") for value in joint_gradients]
    first_delta = share_columns(
        project_back(joint_group, query_weight, key_weight, value_weight, spans, slots)
    )
    expert_out = expert_down(offsets, bases, pairs, half, down_weight, tokens_of, scale, sub)
    first_delta, expert_out = in_order(first_delta, expert_out)

    own_residual = residual_in.astype(F32)
    own_inverse = lax.dynamic_slice_in_dim(first_inverse, own_tokens, local_tokens, 0)
    first_inner = total_rows(jnp.sum(first_delta * first_scale * own_residual, axis=1))
    input_gradient = (
        lax.dynamic_slice_in_dim(middle_delta, own_tokens, local_tokens, 0)
        + own_inverse[:, None] * first_scale * first_delta
        - own_residual * (own_inverse**3 * first_inner / model_width)[:, None]
    )
    first_gain_part = jnp.sum(first_delta * own_residual * own_inverse[:, None], axis=0)

    expert_out = share_columns(expert_out.reshape(tokens, width_part).astype(BF))
    residual_out = (
        lax.dynamic_slice_in_dim(middle, own_tokens, local_tokens, 0) + expert_out
    ).astype(BF)

    early_gradient = early_gradient.astype(F32)
    query_gradient, key_gradient, value_gradient = [value.astype(F32) for value in head_gradients]
    output_gradient = early_gradient[:head_part]
    router_gradient = early_gradient[head_part:].T
    gains = jnp.concatenate(
        [exchange_columns(first_gain_part), second_gain_part, query_gain_part, key_gain_part]
    )
    gains = exchange(gains, "dp")
    head_gains = lax.all_gather(
        gains[2 * width_part :].reshape(2, own_part), "row", axis=1, tiled=True
    )
    head_gains = jnp.sum(head_gains.reshape(2, spans, head_part), axis=1)
    gradients, input_gradient, gains, head_gains = in_order(
        gradients, input_gradient, gains, head_gains
    )
    gradients = gradients_of(parts - 1, run, experts - run, gradients)
    if not gathered:
        gradients = [lax.psum(value.astype(BF), "dp").astype(F32) for value in gradients]
    gate_gradient, up_gradient, down_gradient = gradients

    return (
        residual_out,
        input_gradient,
        gains[:width_part],
        query_gradient,
        key_gradient,
        value_gradient,
        head_gains[0],
        head_gains[1],
        output_gradient,
        gains[width_part : 2 * width_part],
        router_gradient,
        gate_gradient,
        up_gradient,
        down_gradient,
    )


def solution(mesh):
    tokens, routed = P(("dp", "col"), "row"), P(None, "row", "col")
    heads, gain = P("row", "col"), P("row")
    down, back = P(None, "col", "row"), P("col", "row")
    return jax.shard_map(
        on_device,
        mesh=mesh,
        in_specs=(
            tokens,
            gain,
            heads,
            heads,
            heads,
            P("col"),
            P("col"),
            back,
            gain,
            P("row", None),
            routed,
            routed,
            down,
            P("dp"),
            P("dp", None),
            tokens,
        ),
        out_specs=(
            tokens,
            tokens,
            gain,
            heads,
            heads,
            heads,
            P("col"),
            P("col"),
            back,
            gain,
            P("row", None),
            routed,
            routed,
            down,
        ),
        check_vma=False,
    )
```

```python
import functools

import jax
import jax.numpy as jnp
from jax import lax
from jax.experimental import pallas as pl
from jax.experimental.pallas import tpu as pltpu
from jax.sharding import PartitionSpec as P

HEAD_DIM = 128
MAX_LEN = 2048
EPSILON = 1e-05
NEGATIVE = -1e30

TILE = 128
WIDE = 512
SUB = 1024
PACK = 4
BAND = 4
RING = 8
MEGA = 1 << 20
BF = jnp.bfloat16
F32 = jnp.float32


def dot(left, right):
    return jnp.dot(left, right, preferred_element_type=F32)


def dot_nt(left, right):
    return lax.dot_general(left, right, (((1,), (1,)), ((), ())), preferred_element_type=F32)


def dot_tn(left, right):
    return lax.dot_general(left, right, (((0,), (0,)), ((), ())), preferred_element_type=F32)


def iota(shape, axis):
    return lax.broadcasted_iota(jnp.int32, shape, axis)


def params(mebibytes):
    return pltpu.CompilerParams(vmem_limit_bytes=mebibytes * MEGA)


def cost(flops, nbytes):
    return pl.CostEstimate(
        flops=int(flops) // 64, bytes_accessed=int(nbytes) // 64, transcendentals=0
    )


def once(shape, index):
    return pl.BlockSpec(shape, index, pipeline_mode=pl.Buffered(buffer_count=1))


def project_kernel(x_ref, q_ref, k_ref, v_ref, o_ref):
    width = q_ref.shape[1]
    x = x_ref[...]
    o_ref[0, :, :width] = dot(x, q_ref[...]).astype(BF)
    o_ref[0, :, width : 2 * width] = dot(x, k_ref[...]).astype(BF)
    o_ref[0, :, 2 * width :] = dot(x, v_ref[...]).astype(BF)


def project(x, query, key, value, spans, slots):
    tokens, depth = x.shape
    width, span = query.shape[1] // slots, tokens // spans
    weight = pl.BlockSpec((depth, width), lambda s, h: (0, h))
    return pl.pallas_call(
        project_kernel,
        grid=(spans, slots),
        in_specs=[pl.BlockSpec((span, depth), lambda s, h: (s, 0)), weight, weight, weight],
        out_specs=pl.BlockSpec((1, span, 3 * width), lambda s, h: (s * slots + h, 0, 0)),
        out_shape=jax.ShapeDtypeStruct((spans * slots, span, 3 * width), BF),
        compiler_params=params(48),
        cost_estimate=cost(6 * tokens * depth * width * slots, 6 * tokens * width * slots),
        name="project",
    )(x, query, key, value)


def project_back_kernel(d_ref, q_ref, k_ref, v_ref, o_ref, acc):
    slot = pl.program_id(1)
    width = q_ref.shape[1]

    @pl.when(slot == 0)
    def _():
        acc[...] = jnp.zeros_like(acc)

    acc[...] += (
        dot_nt(d_ref[0, :, :width], q_ref[...])
        + dot_nt(d_ref[0, :, width : 2 * width], k_ref[...])
        + dot_nt(d_ref[0, :, 2 * width :], v_ref[...])
    )

    @pl.when(slot == pl.num_programs(1) - 1)
    def _():
        o_ref[...] = acc[...].astype(BF)


def project_back(delta, query, key, value, spans, slots):
    _, span, joint = delta.shape
    depth, width = query.shape[0], joint // 3
    weight = pl.BlockSpec((depth, width), lambda s, h: (0, h))
    return pl.pallas_call(
        project_back_kernel,
        grid=(spans, slots),
        in_specs=[
            pl.BlockSpec((1, span, joint), lambda s, h: (s * slots + h, 0, 0)),
            weight,
            weight,
            weight,
        ],
        out_specs=pl.BlockSpec((span, depth), lambda s, h: (s, 0)),
        out_shape=jax.ShapeDtypeStruct((spans * span, depth), BF),
        scratch_shapes=[pltpu.VMEM((span, depth), F32)],
        compiler_params=params(48),
        cost_estimate=cost(2 * spans * span * depth * joint * slots, 2 * spans * span * joint * slots),
        name="project_back",
    )(delta, query, key, value)


def project_gradient_kernel(x_ref, d_ref, q_ref, k_ref, v_ref, acc):
    span = pl.program_id(1)
    made = dot(x_ref[...], d_ref[0])

    @pl.when(span == 0)
    def _():
        acc[...] = made

    @pl.when(span > 0)
    def _():
        acc[...] += made

    @pl.when(span == pl.num_programs(1) - 1)
    def _():
        width = q_ref.shape[1]
        q_ref[...] = acc[:, :width].astype(BF)
        k_ref[...] = acc[:, width : 2 * width].astype(BF)
        v_ref[...] = acc[:, 2 * width :].astype(BF)


def project_gradient(turned, delta, spans, slots):
    depth, tokens = turned.shape
    _, span, joint = delta.shape
    width = joint // 3
    out = pl.BlockSpec((depth, width), lambda h, s: (0, h))
    return pl.pallas_call(
        project_gradient_kernel,
        grid=(slots, spans),
        in_specs=[
            pl.BlockSpec((depth, span), lambda h, s: (0, s)),
            pl.BlockSpec((1, span, joint), lambda h, s: (s * slots + h, 0, 0)),
        ],
        out_specs=[out, out, out],
        out_shape=[jax.ShapeDtypeStruct((depth, width * slots), BF)] * 3,
        scratch_shapes=[pltpu.VMEM((depth, joint), F32)],
        compiler_params=params(48),
        cost_estimate=cost(2 * tokens * depth * joint * slots, 2 * tokens * joint * slots),
        name="project_gradient",
    )(turned, delta)


def output_kernel(m_ref, w_ref, o_ref, acc):
    slot = pl.program_id(1)

    @pl.when(slot == 0)
    def _():
        acc[...] = jnp.zeros_like(acc)

    acc[...] += dot(m_ref[0], w_ref[...])

    @pl.when(slot == pl.num_programs(1) - 1)
    def _():
        o_ref[...] = acc[...].astype(BF)


def output_project(mixed, weight, spans, slots):
    _, span, width = mixed.shape
    depth = weight.shape[1]
    return pl.pallas_call(
        output_kernel,
        grid=(spans, slots),
        in_specs=[
            pl.BlockSpec((1, span, width), lambda s, h: (s * slots + h, 0, 0)),
            pl.BlockSpec((width, depth), lambda s, h: (h, 0)),
        ],
        out_specs=pl.BlockSpec((span, depth), lambda s, h: (s, 0)),
        out_shape=jax.ShapeDtypeStruct((spans * span, depth), BF),
        scratch_shapes=[pltpu.VMEM((span, depth), F32)],
        compiler_params=params(48),
        cost_estimate=cost(2 * spans * span * depth * width * slots, 2 * spans * span * width * slots),
        name="output_project",
    )(mixed, weight)


def output_back_kernel(d_ref, w_ref, o_ref):
    o_ref[0] = dot_nt(d_ref[...], w_ref[...]).astype(BF)


def output_back(delta, weight, spans, slots):
    tokens, depth = delta.shape
    width, span = weight.shape[0] // slots, tokens // spans
    return pl.pallas_call(
        output_back_kernel,
        grid=(spans, slots),
        in_specs=[
            pl.BlockSpec((span, depth), lambda s, h: (s, 0)),
            pl.BlockSpec((width, depth), lambda s, h: (h, 0)),
        ],
        out_specs=pl.BlockSpec((1, span, width), lambda s, h: (s * slots + h, 0, 0)),
        out_shape=jax.ShapeDtypeStruct((spans * slots, span, width), BF),
        compiler_params=params(48),
        cost_estimate=cost(2 * tokens * depth * width * slots, 2 * tokens * width * slots),
        name="output_back",
    )(delta, weight)


def allowed_pairs(column_ref, row_ref, start, block, reach):
    marks = column_ref[start : start + block, :] == row_ref[0, :, :reach]
    places = iota((block, reach), 1) <= iota((block, reach), 0) + start
    return marks & places


def attend_kernel(q_ref, k_ref, v_ref, column_ref, row_ref, o_ref, log_ref):
    length = q_ref.shape[0]
    block = min(256, length)
    for start in range(0, length, block):
        reach = start + block
        scores = dot_nt(q_ref[start:reach, :], k_ref[:reach, :]) * HEAD_DIM**-0.5
        scores = jnp.where(
            allowed_pairs(column_ref, row_ref, start, block, reach), scores, NEGATIVE
        )
        largest = jnp.max(scores, axis=1, keepdims=True)
        raised = jnp.exp(scores - largest)
        summed = jnp.sum(raised, axis=1, keepdims=True)
        weights = (raised * (1.0 / summed)).astype(BF)
        o_ref[start:reach, :] = dot(weights, v_ref[:reach, :]).astype(BF)
        log_ref[0, start:reach, :] = largest + jnp.log(summed)


def attend(query, key, value, marks, length):
    tokens, width = query.shape
    heads, count = width // HEAD_DIM, tokens // length
    rows = pl.BlockSpec((length, HEAD_DIM), lambda b, h: (b, h))
    return pl.pallas_call(
        attend_kernel,
        grid=(count, heads),
        in_specs=[
            rows,
            rows,
            rows,
            pl.BlockSpec((length, 1), lambda b, h: (b, 0)),
            pl.BlockSpec((1, 1, length), lambda b, h: (b, 0, 0)),
        ],
        out_specs=[rows, pl.BlockSpec((1, length, 1), lambda b, h: (h, b, 0))],
        out_shape=[
            jax.ShapeDtypeStruct((tokens, width), BF),
            jax.ShapeDtypeStruct((heads, tokens, 1), F32),
        ],
        compiler_params=params(48),
        cost_estimate=cost(4 * tokens * length * width, 8 * tokens * width),
        name="attend",
    )(query, key, value, marks.reshape(tokens, 1), marks.reshape(count, 1, length))


def attend_back_kernel(
    q_ref, k_ref, v_ref, d_ref, log_ref, column_ref, row_ref, dq_ref, dk_ref, dv_ref
):
    length = q_ref.shape[0]
    block = min(256, length)
    scale = HEAD_DIM**-0.5
    for start in reversed(range(0, length, block)):
        reach = start + block
        query, delta = q_ref[start:reach, :], d_ref[start:reach, :]
        key, value = k_ref[:reach, :], v_ref[:reach, :]
        scores = dot_nt(query, key) * scale
        allowed = allowed_pairs(column_ref, row_ref, start, block, reach)
        probs = jnp.where(allowed, jnp.exp(scores - log_ref[0, start:reach, :]), 0.0)
        weights_delta = dot_nt(delta, value)
        centre = jnp.sum(probs * weights_delta, axis=1, keepdims=True)
        score_delta = (probs * (weights_delta - centre)).astype(BF)
        dq_ref[start:reach, :] = dot(score_delta, key) * scale
        key_delta = dot_tn(score_delta, query) * scale
        value_delta = dot_tn(probs.astype(BF), delta)
        if reach == length:
            dk_ref[...] = key_delta
            dv_ref[...] = value_delta
        else:
            dk_ref[:reach, :] += key_delta
            dv_ref[:reach, :] += value_delta


def attend_back(query, key, value, delta, logs, marks, length):
    tokens, width = query.shape
    heads, count = width // HEAD_DIM, tokens // length
    rows = pl.BlockSpec((length, HEAD_DIM), lambda b, h: (b, h))
    return pl.pallas_call(
        attend_back_kernel,
        grid=(count, heads),
        in_specs=[
            rows,
            rows,
            rows,
            rows,
            pl.BlockSpec((1, length, 1), lambda b, h: (h, b, 0)),
            pl.BlockSpec((length, 1), lambda b, h: (b, 0)),
            pl.BlockSpec((1, 1, length), lambda b, h: (b, 0, 0)),
        ],
        out_specs=[rows, rows, rows],
        out_shape=[jax.ShapeDtypeStruct((tokens, width), F32)] * 3,
        compiler_params=params(48),
        cost_estimate=cost(10 * tokens * length * width, 20 * tokens * width),
        name="attend_back",
    )(query, key, value, delta, logs, marks.reshape(tokens, 1), marks.reshape(count, 1, length))


def dispatch_kernel(token_ref, source_ref, o_ref):
    tokens = source_ref.shape[1]
    bands = []
    for i in range(WIDE // TILE):
        ids = jnp.broadcast_to(token_ref[0, 0, i : i + 1, :], (TILE, TILE)).T
        bands.append(
            jnp.concatenate(
                [
                    jnp.where(ids == iota((TILE, TILE), 1) + j, 1.0, 0.0).astype(BF)
                    for j in range(0, tokens, TILE)
                ],
                axis=1,
            )
        )
    o_ref[0] = dot(jnp.concatenate(bands, axis=0), source_ref[0]).astype(BF)


def dispatch(tokens_of, source):
    groups, rows = tokens_of.shape
    _, tokens, depth = source.shape
    return pl.pallas_call(
        dispatch_kernel,
        grid=(groups, rows // WIDE),
        in_specs=[
            pl.BlockSpec((1, 1, WIDE // TILE, TILE), lambda g, i: (g, i, 0, 0)),
            pl.BlockSpec((1, tokens, depth), lambda g, i: (g, 0, 0)),
        ],
        out_specs=pl.BlockSpec((1, WIDE, depth), lambda g, i: (g, i, 0)),
        out_shape=jax.ShapeDtypeStruct((groups, rows, depth), BF),
        compiler_params=params(48),
        cost_estimate=cost(2 * groups * rows * tokens * depth, 2 * groups * rows * depth),
        name="dispatch",
    )(tokens_of.reshape(groups, rows // WIDE, WIDE // TILE, TILE), source)


def dispatch_turned_kernel(token_ref, scale_ref, first_ref, second_ref, a_ref, b_ref):
    tokens = first_ref.shape[2]
    chosen = jnp.where(iota((tokens, WIDE), 0) == token_ref[0, 0], 1.0, 0.0).astype(BF)
    scale = scale_ref[0, 0]
    for source, out in ((first_ref, a_ref), (second_ref, b_ref)):
        rows = (dot(source[0], chosen) * scale).astype(BF)
        for i in range(WIDE // TILE):
            out[0, i] = rows[:, i * TILE : (i + 1) * TILE]


def dispatch_turned(tokens_of, scale, first, second):
    groups, rows = tokens_of.shape
    _, depth, tokens = first.shape
    line = pl.BlockSpec((1, 1, 1, WIDE), lambda g, i: (g, i, 0, 0))
    source = pl.BlockSpec((1, depth, tokens), lambda g, i: (g, 0, 0))
    out = pl.BlockSpec((1, WIDE // TILE, depth, TILE), lambda g, i: (g, i, 0, 0))
    return pl.pallas_call(
        dispatch_turned_kernel,
        grid=(groups, rows // WIDE),
        in_specs=[line, line, source, source],
        out_specs=[out, out],
        out_shape=[jax.ShapeDtypeStruct((groups, rows // TILE, depth, TILE), BF)] * 2,
        compiler_params=params(48),
        cost_estimate=cost(4 * groups * rows * tokens * depth, 4 * groups * rows * depth),
        name="dispatch_turned",
    )(
        tokens_of.reshape(groups, rows // WIDE, 1, WIDE),
        scale.reshape(groups, rows // WIDE, 1, WIDE),
        first,
        second,
    )


def pick_kernel(token_ref, expert_ref, probs_ref, o_ref):
    experts, tokens = probs_ref.shape[1], probs_ref.shape[2]
    left, parts = probs_ref[0], []
    for _ in range(3):
        part = left.astype(BF)
        parts.append(part)
        left = left - part.astype(F32)
    chosen = jnp.where(iota((tokens, WIDE), 0) == token_ref[0, 0], 1.0, 0.0).astype(BF)
    found = dot(parts[0], chosen) + dot(parts[1], chosen) + dot(parts[2], chosen)
    match = iota((experts, WIDE), 0) == expert_ref[0, 0]
    o_ref[0, 0] = jnp.sum(jnp.where(match, found, 0.0), axis=0, keepdims=True)


def pick(tokens_of, experts_of, probs):
    groups, rows = tokens_of.shape
    _, experts, tokens = probs.shape
    line = pl.BlockSpec((1, 1, 1, WIDE), lambda g, i: (g, i, 0, 0))
    shape = (groups, rows // WIDE, 1, WIDE)
    return pl.pallas_call(
        pick_kernel,
        grid=(groups, rows // WIDE),
        in_specs=[line, line, pl.BlockSpec((1, experts, tokens), lambda g, i: (g, 0, 0))],
        out_specs=line,
        out_shape=jax.ShapeDtypeStruct(shape, F32),
        compiler_params=params(48),
        cost_estimate=cost(6 * groups * rows * tokens * experts, 8 * groups * rows),
        name="pick",
    )(tokens_of.reshape(shape), experts_of.reshape(shape), probs).reshape(groups, rows)


def each_expert(offset_ref, total, run):
    group, step = pl.program_id(0), pl.program_id(1)
    spans = []
    for i in range(PACK):
        expert = step * PACK + i
        low, high = offset_ref[group, expert], offset_ref[group, expert + 1]
        spans.append((expert, low, high, low // TILE * TILE))
    rounds = 0
    for _, low, high, first in spans:
        rounds = jnp.maximum(rounds, jnp.where(high > low, (high - first + WIDE - 1) // WIDE, 0))

    def turn(j, carry):
        for i, (expert, low, high, first) in enumerate(spans):
            base = pl.multiple_of(jnp.minimum(first + j * WIDE, total - WIDE), TILE)
            run(i, expert, base, low, high)
        return carry

    lax.fori_loop(0, rounds, turn, 0)


def kept(base, rows, low, high):
    places = base + iota((rows, 1), 0)
    return (places >= low) & (places < high)


def gate_up_kernel(offset_ref, x_ref, gate_ref, up_ref, o_ref):
    half = gate_ref.shape[2]

    def run(i, expert, base, low, high):
        rows = pl.ds(base, WIDE)
        keep = kept(base, WIDE, low, high)
        x = x_ref[0, rows, :]
        for start, weight in ((0, gate_ref), (half, up_ref)):
            columns = slice(start, start + half)
            made = dot(x, weight[i]).astype(BF)
            o_ref[0, rows, columns] = jnp.where(keep, made, o_ref[0, rows, columns])

    each_expert(offset_ref, x_ref.shape[1], run)


def gate_up(offsets, x, gate, up, part, half):
    groups, rows, depth = x.shape
    experts = gate.shape[0]
    weight = pl.BlockSpec((PACK, depth, half), lambda g, e, o: (e, 0, part))
    return pl.pallas_call(
        gate_up_kernel,
        grid_spec=pltpu.PrefetchScalarGridSpec(
            num_scalar_prefetch=1,
            grid=(groups, experts // PACK),
            in_specs=[once((1, rows, depth), lambda g, e, o: (g, 0, 0)), weight, weight],
            out_specs=once((1, rows, 2 * half), lambda g, e, o: (g, 0, 0)),
        ),
        out_shape=jax.ShapeDtypeStruct((groups, rows, 2 * half), BF),
        compiler_params=params(56),
        cost_estimate=cost(6 * groups * rows * depth * half, 2 * groups * rows * depth),
        name="gate_up",
    )(offsets, x, gate, up)


def hidden_back_kernel(offset_ref, x_ref, down_ref, o_ref):
    def run(i, expert, base, low, high):
        rows = pl.ds(base, WIDE)
        made = dot_nt(x_ref[0, rows, :], down_ref[i]).astype(BF)
        keep = kept(base, WIDE, low, high)
        o_ref[0, rows, :] = jnp.where(keep, made, o_ref[0, rows, :])

    each_expert(offset_ref, x_ref.shape[1], run)


def hidden_back(offsets, x, down):
    groups, rows, depth = x.shape
    experts, units, _ = down.shape
    return pl.pallas_call(
        hidden_back_kernel,
        grid_spec=pltpu.PrefetchScalarGridSpec(
            num_scalar_prefetch=1,
            grid=(groups, experts // PACK),
            in_specs=[
                once((1, rows, depth), lambda g, e, o: (g, 0, 0)),
                pl.BlockSpec((PACK, units, depth), lambda g, e, o: (e, 0, 0)),
            ],
            out_specs=once((1, rows, units), lambda g, e, o: (g, 0, 0)),
        ),
        out_shape=jax.ShapeDtypeStruct((groups, rows, units), BF),
        compiler_params=params(56),
        cost_estimate=cost(3 * groups * rows * depth * units, 2 * groups * rows * depth),
        name="hidden_back",
    )(offsets, x, down)


def slopes(gate):
    gate = 0.5 * gate.astype(F32)
    turned = jnp.tanh(gate)
    product = gate * turned
    return gate + product, (0.5 + 0.5 * turned) * ((1.0 + gate) - product)


def combine(token_ref, scale_ref, rows_ref, o_ref, before_ref=None):
    tokens = o_ref.shape[1]
    o_ref[0] = jnp.zeros(o_ref.shape[1:], F32) if before_ref is None else before_ref[0]

    def step(i, carry):
        chosen = iota((tokens, WIDE), 0) == token_ref[0, i]
        chosen = jnp.where(chosen, scale_ref[0, i], 0.0).astype(BF)
        o_ref[0] += dot(chosen, rows_ref[pl.ds(pl.multiple_of(i * WIDE, WIDE), WIDE), :])
        return carry

    lax.fori_loop(0, rows_ref.shape[0] // WIDE, step, 0)


def expert_back_kernel(
    part, offset_ref, _, g_ref, u_ref, hd_ref, gate_ref, up_ref, token_ref, scale_ref, *rest
):
    *before_ref, o_ref, made_ref = rest
    experts = PACK * pl.num_programs(1)
    depth, half = gate_ref.shape[1], gate_ref.shape[2]

    def run(i, expert, base, low, high):
        rows = pl.ds(base, WIDE)
        keep = kept(base, WIDE, low, high)
        silu, slope = slopes(g_ref[0, rows, :])
        delta = hd_ref[0, rows, part * half : (part + 1) * half]
        through = delta * u_ref[0, rows, :]
        picked = through.astype(F32) * silu
        made = dot_nt(through * slope.astype(BF), gate_ref[i])
        made += dot_nt(delta * silu.astype(BF), up_ref[i])
        made_ref[rows, :depth] = jnp.where(keep, made.astype(BF), made_ref[rows, :depth])
        picked = jnp.sum(picked, axis=1, keepdims=True)
        upper = picked.astype(BF).astype(F32)
        lane = iota((WIDE, TILE), 1)
        spread = jnp.where(
            lane == expert, upper, jnp.where(lane == expert + experts, picked - upper, 0.0)
        )
        made_ref[rows, depth:] = jnp.where(keep, spread.astype(BF), made_ref[rows, depth:])

    each_expert(offset_ref, made_ref.shape[0], run)

    @pl.when(pl.program_id(1) == pl.num_programs(1) - 1)
    def _():
        combine(token_ref, scale_ref, made_ref, o_ref, *before_ref)


def expert_back(offsets, base, pair, hd, gate, up, tokens_of, scale, part, half, tokens, before):
    groups, rows = tokens_of.shape
    units = hd.shape[2]
    experts, depth = gate.shape[:2]
    weight = pl.BlockSpec((PACK, depth, half), lambda g, e, o, b: (e, 0, part))
    line = once((1, rows // WIDE, 1, WIDE), lambda g, e, o, b: (g, 0, 0, 0))
    shape = (groups, rows // WIDE, 1, WIDE)
    total = once((1, tokens, depth + TILE), lambda g, e, o, b: (g, 0, 0))
    return pl.pallas_call(
        functools.partial(expert_back_kernel, part),
        grid_spec=pltpu.PrefetchScalarGridSpec(
            num_scalar_prefetch=2,
            grid=(groups, experts // PACK),
            in_specs=[
                *[
                    once((1, rows, half), lambda g, e, o, b, c=column: (b[0] + g, 0, c))
                    for _, column in pair
                ],
                once((1, rows, units), lambda g, e, o, b: (b[1] + g, 0, 0)),
                weight,
                weight,
                line,
                line,
                *[total] * len(before),
            ],
            out_specs=total,
            scratch_shapes=[pltpu.VMEM((rows, depth + TILE), BF)],
        ),
        out_shape=jax.ShapeDtypeStruct((groups, tokens, depth + TILE), F32),
        compiler_params=params(56),
        cost_estimate=cost(
            groups * rows * depth * (6 * half + 2 * tokens), 2 * groups * rows * (2 * half + units)
        ),
        name="expert_back",
    )(offsets, base, pair[0][0], pair[1][0], hd, gate, up, tokens_of.reshape(shape), scale.reshape(shape), *before)


def down_kernel(start, count, offset_ref, base_ref, down_ref, token_ref, scale_ref, *rest):
    sources, (*before_ref, o_ref, made_ref) = rest[: 2 * count], rest[2 * count :]
    half = sources[0].shape[2]

    def run(i, expert, base, low, high):
        rows = pl.ds(base, WIDE)
        keep = kept(base, WIDE, low, high)
        hidden = []
        for gate_ref, up_ref in zip(sources[::2], sources[1::2]):
            gate = 0.5 * gate_ref[0, rows, :].astype(F32)
            silu = gate + gate * jnp.tanh(gate)
            hidden.append((silu * up_ref[0, rows, :].astype(F32)).astype(BF))
        units = slice(start * half, (start + count) * half)
        made = dot(jnp.concatenate(hidden, axis=1), down_ref[i, units, :])
        made_ref[rows, :] = jnp.where(keep, made.astype(BF), made_ref[rows, :])

    each_expert(offset_ref, made_ref.shape[0], run)

    @pl.when(pl.program_id(1) == pl.num_programs(1) - 1)
    def _():
        combine(token_ref, scale_ref, made_ref, o_ref, *before_ref)


def expert_down(offsets, bases, pairs, half, down, tokens_of, scale, tokens, start, before):
    groups, rows = tokens_of.shape
    experts, units, depth = down.shape
    line = once((1, rows // WIDE, 1, WIDE), lambda g, e, o, b: (g, 0, 0, 0))
    shape = (groups, rows // WIDE, 1, WIDE)

    def source(i, column):
        return once((1, rows, half), lambda g, e, o, b: (b[i] + g, 0, column))

    total = once((1, tokens, depth), lambda g, e, o, b: (g, 0, 0))
    specs = [source(i, column) for i, pair in enumerate(pairs) for _, column in pair]
    sources = [value for pair in pairs for value, _ in pair]
    return pl.pallas_call(
        functools.partial(down_kernel, start, len(pairs)),
        grid_spec=pltpu.PrefetchScalarGridSpec(
            num_scalar_prefetch=2,
            grid=(groups, experts // PACK),
            in_specs=[
                pl.BlockSpec((PACK, units, depth), lambda g, e, o, b: (e, 0, 0)),
                line,
                line,
                *specs,
                *[total] * len(before),
            ],
            out_specs=total,
            scratch_shapes=[pltpu.VMEM((rows, depth), BF)],
        ),
        out_shape=jax.ShapeDtypeStruct((groups, tokens, depth), F32),
        compiler_params=params(56),
        cost_estimate=cost(
            groups * rows * depth * (3 * units + 2 * tokens), 4 * groups * rows * units
        ),
        name="expert_down",
    )(offsets, bases, down, tokens_of.reshape(shape), scale.reshape(shape), *sources, *before)


def gradient_kernel(part, start, pieces, aliased, offset_ref, *rest):
    piece_refs, rest = rest[:pieces], rest[pieces:]
    hd_ref, xs_ref, xc_ref = rest[:3]
    rest = rest[3 + 3 * aliased :]
    gate_out, up_out, down_out = rest[:3]
    gu_ring, hd_ring, xs_ring, xc_ring, narrow, issued, waited, sems = rest[3:]
    segments, tiles = xs_ref.shape[:2]
    shares, run_tiles = piece_refs[0].shape[1:3]
    share_tiles = pieces * run_tiles
    half = gate_out.shape[2]
    expert = start + pl.program_id(0)
    stop = start + pl.num_programs(0)

    def copies(segment, tile):
        slot = lax.rem(tile, RING)
        units = pl.ds(part * half, half)
        return [
            pltpu.make_async_copy(
                hd_ref.at[segment, tile, :, units],
                hd_ring.at[segment, slot],
                sems.at[1, segment, slot],
            ),
            pltpu.make_async_copy(
                xs_ref.at[segment, tile], xs_ring.at[segment, slot], sems.at[2, segment, slot]
            ),
            pltpu.make_async_copy(
                xc_ref.at[segment, tile], xc_ring.at[segment, slot], sems.at[3, segment, slot]
            ),
        ]

    def piece_copy(piece, segment, tile):
        slot = lax.rem(tile, RING)
        share, place = tile // share_tiles, lax.rem(tile, run_tiles)
        return pltpu.make_async_copy(
            piece_refs[piece].at[segment, share, place],
            gu_ring.at[segment, slot],
            sems.at[0, segment, slot],
        )

    def start_until(segment, limit):
        def step(tile, carry):
            for copy in copies(segment, tile):
                copy.start()
            if pieces == 1:
                piece_copy(0, segment, tile).start()
            else:
                held = lax.rem(tile, share_tiles) // run_tiles
                for piece in range(pieces):
                    pl.when(held == piece)(
                        lambda piece=piece: piece_copy(piece, segment, tile).start()
                    )
            return carry

        lax.fori_loop(issued[segment], limit, step, 0)
        issued[segment] = jnp.maximum(issued[segment], limit)

    def wait_until(segment, limit):
        def step(tile, carry):
            for copy in copies(segment, tile):
                copy.wait()
            piece_copy(0, segment, tile).wait()
            return carry

        lax.fori_loop(waited[segment], limit, step, 0)
        waited[segment] = jnp.maximum(waited[segment], limit)

    bounds = [
        (offset_ref[i, start] // TILE, (offset_ref[i, stop] + TILE - 1) // TILE)
        for i in range(segments)
    ]

    @pl.when(expert == start)
    def _():
        for segment, (head, tail) in enumerate(bounds):
            issued[segment] = head
            waited[segment] = head
            start_until(segment, jnp.minimum(head + RING - 1, tail))
            wait_until(segment, jnp.minimum(head + 1, tail))

            @pl.when(tail <= head)
            def _():
                slot = lax.rem(head, RING)
                for ring in (gu_ring, hd_ring, xs_ring, xc_ring):
                    ring[segment, slot] = jnp.zeros(ring.shape[2:], BF)

    spans, rounds = [], 0
    for segment in range(segments):
        low, high = offset_ref[segment, expert], offset_ref[segment, expert + 1]
        first = low // TILE
        last = jnp.where(high > low, (high + TILE - 1) // TILE, first)
        spans.append((low, high, first, last))
        rounds = jnp.maximum(rounds, (last - first + BAND - 1) // BAND)

    def turn(i, carry, fresh=False):
        for segment, (low, high, first, last) in enumerate(spans):
            tile = jnp.minimum(first + BAND * i, last)
            start_until(segment, jnp.minimum(bounds[segment][1], tile + RING - 1))
            wait_until(segment, jnp.minimum(last, tile + BAND))
        for segment, (low, high, first, last) in enumerate(spans):
            if segment % 2 == 0:
                gates, ups, hidden, xs, xc = [], [], [], [], []
            for j in range(BAND):
                tile = first + BAND * i + j
                slot = lax.rem(jnp.maximum(jnp.minimum(tile, last - 1), bounds[segment][0]), RING)
                keep = kept(tile * TILE, TILE, low, high)
                silu, slope = slopes(gu_ring[segment, slot, :, :half])
                silu = jnp.where(keep, silu, 0.0).astype(BF)
                slope = jnp.where(keep, slope, 0.0).astype(BF)
                up, delta = gu_ring[segment, slot, :, half:], hd_ring[segment, slot]
                gates.append(delta * up * slope)
                ups.append(delta * silu)
                hidden.append(silu * up)
                xs.append(xs_ring[segment, slot])
                xc.append(xc_ring[segment, slot])
            if segment % 2 == 0 and segment + 1 < segments:
                continue
            left, right = jnp.concatenate(xs, axis=1), jnp.concatenate(xc, axis=1)
            made = [
                (gate_out, (0,), dot(left, jnp.concatenate(gates, axis=0))),
                (up_out, (0,), dot(left, jnp.concatenate(ups, axis=0))),
                (narrow, (), dot(right, jnp.concatenate(hidden, axis=0))),
            ]
            for out, place, value in made:
                if fresh and segment < 2:
                    out[(*place, ...)] = value
                else:
                    out[(*place, ...)] += value
        return carry

    turn(0, 0, fresh=True)
    lax.fori_loop(1, rounds, turn, 0)

    @pl.when(expert == stop - 1)
    def _():
        for segment in range(segments):
            wait_until(segment, issued[segment])

    down_out[0] = narrow[...].T


def expert_gradients(offsets, pieces, hd, xs, xc, part, start, count, before):
    segments, shares, run, pair = pieces[0].shape
    half, rows = pair // 2, hd.shape[1]
    tiles = rows // TILE
    units = hd.shape[2]
    depth = xs.shape[2]
    experts = offsets.shape[1] - 1
    anywhere = pl.BlockSpec(memory_space=pl.ANY)
    columns = pl.BlockSpec((1, depth, half), lambda e, o: (start + e, 0, part))
    before = list(before)
    return pl.pallas_call(
        functools.partial(gradient_kernel, part, start, len(pieces), int(bool(before))),
        grid_spec=pltpu.PrefetchScalarGridSpec(
            num_scalar_prefetch=1,
            grid=(count,),
            in_specs=[anywhere] * (len(pieces) + 3 + len(before)),
            out_specs=[
                columns,
                columns,
                pl.BlockSpec((1, half, depth), lambda e, o: (start + e, part, 0)),
            ],
            scratch_shapes=[
                pltpu.VMEM((segments, RING, TILE, pair), BF),
                pltpu.VMEM((segments, RING, TILE, half), BF),
                pltpu.VMEM((segments, RING, depth, TILE), BF),
                pltpu.VMEM((segments, RING, depth, TILE), BF),
                pltpu.VMEM((depth, half), F32),
                pltpu.SMEM((segments,), jnp.int32),
                pltpu.SMEM((segments,), jnp.int32),
                pltpu.SemaphoreType.DMA((4, segments, RING)),
            ],
        ),
        out_shape=[
            jax.ShapeDtypeStruct((experts, depth, units), F32),
            jax.ShapeDtypeStruct((experts, depth, units), F32),
            jax.ShapeDtypeStruct((experts, units, depth), F32),
        ],
        input_output_aliases={len(pieces) + 4 + i: i for i in range(len(before))},
        compiler_params=params(56),
        cost_estimate=cost(
            9 * segments * rows * depth * half, 2 * segments * rows * (3 * half + 2 * depth)
        ),
        name="expert_gradients",
    )(
        offsets,
        *[piece.reshape(segments, shares, run // TILE, TILE, pair) for piece in pieces],
        hd.reshape(segments, tiles, TILE, units),
        xs,
        xc,
        *before,
    )


def in_order(*values):
    return lax.optimization_barrier(values)


def total_rows(value):
    return lax.psum(value, "row")


def neighbour_sum(value, axis, apart):
    count = lax.axis_size(axis)
    return value + lax.ppermute(value, axis, [(i, i ^ apart) for i in range(count)])


def exchange(value, axis):
    count, apart = lax.axis_size(axis), 1
    while apart < count:
        value = value + lax.ppermute(value, axis, [(i, i ^ apart) for i in range(count)])
        apart *= 2
    return value


def scatter_rows(value):
    count = lax.axis_size("row")
    if count != 4:
        return lax.psum_scatter(value, "row", scatter_dimension=0, tiled=False)
    index = lax.axis_index("row")

    def halve(value, axis, mine, apart):
        sent = lax.dynamic_index_in_dim(value, 1 - mine, axis, False)
        kept = lax.dynamic_index_in_dim(value, mine, axis, False)
        other = lax.ppermute(sent, "row", [(i, i ^ apart) for i in range(count)])
        return (kept.astype(F32) + other.astype(F32)).astype(BF)

    value = halve(value.reshape(2, 2, *value.shape[1:]), 1, index % 2, 1)
    return halve(value, 0, index // 2, 2)


def gather_planes(value):
    count = lax.axis_size("dp")
    pieces = [value] + [
        lax.ppermute(value, "dp", [(i, (i - apart) % count) for i in range(count)])
        for apart in range(1, count)
    ]
    first = (count - lax.axis_index("dp")) % count * value.shape[0]
    return lax.dynamic_slice_in_dim(
        jnp.concatenate(pieces + pieces[:-1], axis=0), first, count * value.shape[0], 0
    )


def exchange_columns(value):
    if lax.axis_size("col") != 2:
        return lax.psum(value, "col")
    return value + lax.ppermute(value, "col", [(0, 1), (1, 0)])


def gather_columns(value):
    if lax.axis_size("col") != 2:
        return lax.all_gather(value, "col", axis=0, tiled=True)
    other = lax.ppermute(value, "col", [(0, 1), (1, 0)])
    first = lax.axis_index("col") == 0
    return jnp.concatenate(
        [jnp.where(first, value, other), jnp.where(first, other, value)], axis=0
    )


def add_columns(value):
    if lax.axis_size("col") != 2:
        return lax.psum(value, "col").astype(F32)
    other = lax.ppermute(value, "col", [(0, 1), (1, 0)])
    return value.astype(F32) + other.astype(F32)


def share_columns(value):
    count = lax.axis_size("col")
    if count != 2:
        return lax.psum_scatter(value, "col", scatter_dimension=0, tiled=True).astype(F32)
    index = lax.axis_index("col")
    halves = value.reshape(2, value.shape[0] // 2, value.shape[1])
    other = lax.ppermute(
        lax.dynamic_index_in_dim(halves, 1 - index, 0, False), "col", [(0, 1), (1, 0)]
    )
    return lax.dynamic_index_in_dim(halves, index, 0, False).astype(F32) + other.astype(F32)


def on_device(
    residual_in,
    attention_gain,
    query_weight,
    key_weight,
    value_weight,
    query_gain,
    key_gain,
    output_weight,
    expert_gain,
    router_weight,
    gate_weight,
    up_weight,
    down_weight,
    segments,
    routes,
    cotangent,
):
    row_count = lax.axis_size("row")
    row_index = lax.axis_index("row")
    column_count = lax.axis_size("col")
    column_index = lax.axis_index("col")
    local_tokens, width_part = residual_in.shape
    model_width = width_part * row_count
    tokens = local_tokens * column_count
    head_part = query_weight.shape[1]
    heads_here = head_part // HEAD_DIM
    slots = min(row_count, heads_here)
    spans = row_count // slots
    own_part = head_part // slots
    experts, _, units = gate_weight.shape
    parts = 2 if units % 256 == 0 else 1
    half = units // parts
    top_count = routes.shape[1]
    length = min(MAX_LEN, tokens)
    sub = min(SUB, tokens)
    groups = tokens // sub
    rows = sub * top_count

    keys = routes * sub + (jnp.arange(tokens, dtype=jnp.int32) % sub)[:, None]
    keys = lax.sort(keys.reshape(groups, rows), dimension=1)

    def places(keys):
        bounds = jnp.arange(experts + 1, dtype=jnp.int32) * sub
        below = keys[:, None, :] < bounds[None, :, None]
        return keys % sub, keys // sub, jnp.sum(below.astype(jnp.int32), axis=2)

    tokens_of, experts_of, offsets = places(keys)

    delta_group = gather_columns(cotangent)
    gathered = tokens <= 2 * SUB
    planes = ("dp", "col")
    all_delta, all_keys = delta_group, keys
    if gathered:
        all_delta = lax.all_gather(cotangent, planes, axis=0, tiled=True)
        all_keys = lax.all_gather(keys, "dp", axis=0, tiled=True)
    delta_rows = dispatch(tokens_of, delta_group.reshape(groups, sub, width_part))
    hidden_part = hidden_back(offsets, delta_rows, down_weight)

    residual = gather_columns(residual_in).astype(F32)
    first_scale = attention_gain.astype(F32)
    first_inverse = lax.rsqrt(
        total_rows(jnp.sum(residual * residual, axis=1)) / model_width + EPSILON
    )
    normed = (residual * first_inverse[:, None] * first_scale).astype(BF)
    joint = lax.psum_scatter(
        project(normed, query_weight, key_weight, value_weight, spans, slots),
        "row",
        scatter_dimension=0,
        tiled=False,
    )
    joint, hidden_part, all_keys = in_order(joint, hidden_part, all_keys)
    query_raw = joint[:, :own_part].astype(F32)
    key_raw = joint[:, own_part : 2 * own_part].astype(F32)
    value_round = joint[:, 2 * own_part :]
    span = tokens // spans
    span_start = row_index // slots * span

    def total_heads(first, second):
        sums = jnp.stack([jnp.sum(first, axis=1), jnp.sum(second, axis=1)])
        if spans > 1:
            sums = lax.dynamic_update_slice(
                jnp.zeros((2, tokens), F32), sums, (jnp.zeros((), jnp.int32), span_start)
            )
        sums = total_rows(exchange_columns(sums))
        return lax.dynamic_slice_in_dim(sums, span_start, span, 1) if spans > 1 else sums

    own_segments = lax.dynamic_slice_in_dim(segments, span_start, span, 0)
    square_sums = total_heads(query_raw * query_raw, key_raw * key_raw)
    query_inverse = lax.rsqrt(square_sums[0] / model_width + EPSILON)
    key_inverse = lax.rsqrt(square_sums[1] / model_width + EPSILON)
    own_start = (row_index % slots * own_part,)
    query_scale = lax.dynamic_slice(query_gain, own_start, (own_part,)).astype(F32)
    key_scale = lax.dynamic_slice(key_gain, own_start, (own_part,)).astype(F32)
    query_round = (query_raw * query_inverse[:, None] * query_scale).astype(BF)
    key_round = (key_raw * key_inverse[:, None] * key_scale).astype(BF)
    mixed, logs = attend(query_round, key_round, value_round, own_segments, length)
    mixed, all_delta = in_order(mixed, all_delta)
    mixed_group = lax.all_gather(mixed, "row", axis=0, tiled=False)
    hidden_delta = lax.psum_scatter(
        hidden_part.reshape(groups * rows, units),
        "row",
        scatter_dimension=0,
        tiled=True,
    )
    middle = residual + add_columns(output_project(mixed_group, output_weight, spans, slots))

    second_scale = expert_gain.astype(F32)
    second_inverse = lax.rsqrt(total_rows(jnp.sum(middle * middle, axis=1)) / model_width + EPSILON)
    second = (middle * second_inverse[:, None] * second_scale).astype(BF)
    logits = exchange(
        lax.dot_general(
            router_weight, second, (((0,), (1,)), ((), ())), preferred_element_type=F32
        ),
        "row",
    )
    turned_probs = jax.nn.softmax(logits, axis=0)
    router_probs = turned_probs.T
    second_rows = dispatch(tokens_of, second.reshape(groups, sub, width_part))
    scale = pick(
        tokens_of, experts_of, jnp.swapaxes(turned_probs.reshape(experts, groups, sub), 0, 1)
    )
    own_tokens = column_index * local_tokens
    shares, pairs = [], []
    for part in range(parts):
        made = gate_up(offsets, second_rows, gate_weight, up_weight, part, half)
        if part == 0:
            made, hidden_delta = in_order(made, hidden_delta)
        shares.append(
            lax.psum_scatter(
                made.reshape(groups * rows, 2 * half), "row", scatter_dimension=0, tiled=True
            )
        )
    def turned(value):
        return jnp.swapaxes(value.reshape(-1, sub, width_part), 1, 2)

    def back_of(part, pair, base, hidden_rows, hidden_base, before=()):
        return expert_back(
            offsets,
            jnp.stack([base, hidden_base]),
            pair,
            hidden_rows,
            gate_weight,
            up_weight,
            tokens_of,
            scale,
            part,
            half,
            sub,
            before,
        )

    zero, down_part = jnp.zeros((), jnp.int32), []
    if gathered:
        every = ("dp", "row")
        all_scales = gather_planes(scale)
        all_second = gather_planes(second)
        all_hidden = lax.all_gather(hidden_delta, every, axis=0, tiled=True)
        all_tokens_of, _, all_offsets = places(all_keys)
        segment_count = all_offsets.shape[0]
        sources = [turned(all_second), turned(all_delta)]
        shares[-1], all_hidden, all_scales, *sources = in_order(
            shares[-1], all_hidden, all_scales, *sources
        )
        second_turned, delta_turned = dispatch_turned(all_tokens_of, all_scales, *sources)
        hidden_rows = all_hidden.reshape(segment_count, rows, units)
        base = lax.axis_index("dp") * groups
        last = lax.all_gather(shares[-1], "row", axis=0, tiled=True)
        shares[0], last = in_order(shares[0], last)
        last = last.reshape(groups, rows, 2 * half)
        back = back_of(parts - 1, [(last, 0), (last, 1)], zero, hidden_rows, base)
        if parts > 1:
            down_part = [
                expert_down(
                    offsets,
                    zero[None],
                    [[(last, 0), (last, 1)]],
                    half,
                    down_weight,
                    tokens_of,
                    scale,
                    sub,
                    parts - 1,
                    (),
                )
            ]
        pairs, bases, all_pairs = [], [], []
        for part in range(parts):
            taken = lax.all_gather(shares[part], every, axis=0, tiled=True)
            if part + 1 < parts:
                shares[part + 1], taken, back, second_turned, delta_turned, *down_part = in_order(
                    shares[part + 1], taken, back, second_turned, delta_turned, *down_part
                )
                whole = taken.reshape(segment_count, rows, 2 * half)
                pairs.append([(whole, 0), (whole, 1)])
                bases.append(base)
                back = back_of(part, pairs[part], base, hidden_rows, base, (back,))
            all_pairs.append([taken.reshape(segment_count, 1, rows, 2 * half)])
        pairs.append([(last, 0), (last, 1)])
        bases.append(zero)
    else:
        all_tokens_of, all_offsets, all_scales = tokens_of, offsets, scale
        segment_count = groups
        all_second = second
        hidden_rows = lax.all_gather(hidden_delta, "row", axis=0, tiled=True).reshape(
            groups, rows, units
        )
        wholes = [
            lax.all_gather(share, "row", axis=0, tiled=True).reshape(groups, rows, 2 * half)
            for share in shares
        ]
        pairs = [[(value, 0), (value, 1)] for value in wholes]
        all_pairs = [[value[:, None]] for value in wholes]
        second_turned, delta_turned = dispatch_turned(
            all_tokens_of, all_scales, turned(all_second), turned(all_delta)
        )
        bases = [zero] * parts
        back = sum(back_of(part, pairs[part], zero, hidden_rows, zero) for part in range(parts))
    bases = jnp.stack(bases)
    back = back.reshape(tokens, width_part + TILE)

    def gradients_of(part, start, count, before):
        return expert_gradients(
            all_offsets,
            all_pairs[part],
            hidden_rows,
            second_turned,
            delta_turned,
            part,
            start,
            count,
            before,
        )

    picked_delta = (
        back[:, width_part : width_part + experts]
        + back[:, width_part + experts : width_part + 2 * experts]
    )
    logits_delta = (
        picked_delta - router_probs * jnp.sum(picked_delta, axis=1, keepdims=True)
    ).astype(BF)
    second_delta = add_columns(
        (back[:, :width_part] + dot_nt(logits_delta, router_weight)).astype(BF)
    )
    router_part = exchange_columns(dot_tn(logits_delta, second))

    out_delta = delta_group.astype(F32)
    second_inner = total_rows(jnp.sum(second_delta * second_scale * middle, axis=1))
    middle_delta = (
        out_delta
        + second_inverse[:, None] * second_scale * second_delta
        - middle * (second_inverse**3 * second_inner / model_width)[:, None]
    )
    second_gain_part = jnp.sum(second_delta * middle * second_inverse[:, None], axis=0)
    attention_round = middle_delta.astype(BF)
    early = parts > 1
    gradients = gradients_of(0, 0, experts, ()) if early else ()
    attention_round, all_pairs[-1][0], gradients = in_order(
        attention_round, all_pairs[-1][0], gradients
    )
    output_gradient = jnp.einsum(
        "srth,std->rhd",
        mixed_group.reshape(spans, slots, span, own_part),
        attention_round.reshape(spans, span, width_part),
        preferred_element_type=F32,
    ).reshape(head_part, width_part)
    early_gradient = jnp.concatenate([output_gradient, router_part], axis=0).astype(BF)
    plane_count = lax.axis_size("dp")
    pairwise = early and plane_count == 4
    if pairwise:
        early_gradient = neighbour_sum(early_gradient, "dp", 1)


    mixed_delta = scatter_rows(output_back(attention_round, output_weight, spans, slots))
    query_delta, key_delta, value_delta = attend_back(
        query_round, key_round, value_round, mixed_delta, logs, own_segments, length
    )
    inner_sums = total_heads(
        query_delta * query_scale * query_raw, key_delta * key_scale * key_raw
    )
    query_raw_delta = (
        query_inverse[:, None] * query_scale * query_delta
        - query_raw * (query_inverse**3 * inner_sums[0] / model_width)[:, None]
    )
    key_raw_delta = (
        key_inverse[:, None] * key_scale * key_delta
        - key_raw * (key_inverse**3 * inner_sums[1] / model_width)[:, None]
    )
    query_gain_part = jnp.sum(query_delta * query_raw * query_inverse[:, None], axis=0)
    key_gain_part = jnp.sum(key_delta * key_raw * key_inverse[:, None], axis=0)
    joint_delta = jnp.concatenate([query_raw_delta, key_raw_delta, value_delta], axis=1).astype(BF)
    joint_delta, early_gradient = in_order(joint_delta, early_gradient)
    if pairwise:
        early_gradient = neighbour_sum(early_gradient, "dp", 2)
    else:
        early_gradient = lax.psum(early_gradient, "dp")
    joint_group = lax.all_gather(joint_delta, "row", axis=0, tiled=False)
    run = experts * 3 // 8
    gradients = gradients_of(parts - 1, 0, run, gradients)
    joint_group, gradients, early_gradient = in_order(joint_group, gradients, early_gradient)
    joint_gradients = project_gradient(normed.T, joint_group, spans, slots)
    *joint_gradients, joint_group = in_order(*joint_gradients, joint_group)
    head_gradients = [lax.psum(value, "dp") for value in joint_gradients]
    first_delta = share_columns(
        project_back(joint_group, query_weight, key_weight, value_weight, spans, slots)
    )
    left = parts - len(down_part)
    expert_out = expert_down(
        offsets, bases, pairs[:left], half, down_weight, tokens_of, scale, sub, 0, down_part
    )
    first_delta, expert_out = in_order(first_delta, expert_out)

    own_residual = residual_in.astype(F32)
    own_inverse = lax.dynamic_slice_in_dim(first_inverse, own_tokens, local_tokens, 0)
    first_inner = total_rows(jnp.sum(first_delta * first_scale * own_residual, axis=1))
    input_gradient = (
        lax.dynamic_slice_in_dim(middle_delta, own_tokens, local_tokens, 0)
        + own_inverse[:, None] * first_scale * first_delta
        - own_residual * (own_inverse**3 * first_inner / model_width)[:, None]
    )
    first_gain_part = jnp.sum(first_delta * own_residual * own_inverse[:, None], axis=0)

    expert_out = share_columns(expert_out.reshape(tokens, width_part).astype(BF))
    residual_out = (
        lax.dynamic_slice_in_dim(middle, own_tokens, local_tokens, 0) + expert_out
    ).astype(BF)

    early_gradient = early_gradient.astype(F32)
    query_gradient, key_gradient, value_gradient = [value.astype(F32) for value in head_gradients]
    output_gradient = early_gradient[:head_part]
    router_gradient = early_gradient[head_part:].T
    gains = jnp.concatenate(
        [exchange_columns(first_gain_part), second_gain_part, query_gain_part, key_gain_part]
    )
    gains = exchange(gains, "dp")
    head_gains = lax.all_gather(
        gains[2 * width_part :].reshape(2, own_part), "row", axis=1, tiled=True
    )
    head_gains = jnp.sum(head_gains.reshape(2, spans, head_part), axis=1)
    gradients, input_gradient, gains, head_gains = in_order(
        gradients, input_gradient, gains, head_gains
    )
    gradients = gradients_of(parts - 1, run, experts - run, gradients)
    if not gathered:
        gradients = [lax.psum(value.astype(BF), "dp").astype(F32) for value in gradients]
    gate_gradient, up_gradient, down_gradient = gradients

    return (
        residual_out,
        input_gradient,
        gains[:width_part],
        query_gradient,
        key_gradient,
        value_gradient,
        head_gains[0],
        head_gains[1],
        output_gradient,
        gains[width_part : 2 * width_part],
        router_gradient,
        gate_gradient,
        up_gradient,
        down_gradient,
    )


def solution(mesh):
    tokens, routed = P(("dp", "col"), "row"), P(None, "row", "col")
    heads, gain = P("row", "col"), P("row")
    down, back = P(None, "col", "row"), P("col", "row")
    return jax.shard_map(
        on_device,
        mesh=mesh,
        in_specs=(
            tokens,
            gain,
            heads,
            heads,
            heads,
            P("col"),
            P("col"),
            back,
            gain,
            P("row", None),
            routed,
            routed,
            down,
            P("dp"),
            P("dp", None),
            tokens,
        ),
        out_specs=(
            tokens,
            tokens,
            gain,
            heads,
            heads,
            heads,
            P("col"),
            P("col"),
            back,
            gain,
            P("row", None),
            routed,
            routed,
            down,
        ),
        check_vma=False,
    )
```
